32 devices in a mesh: segment: 4 (over y, x), dp: 8 (over z, core).
Axes of the slice: x: 2, y: 2, z: 4, core: 2. Of those that a mesh axis runs over, the one named last changes fastest.
Arguments:
- block_input: bfloat16 [16, 1024, 768], P('dp')
- cotangent: bfloat16 [16, 1024, 768], P('dp'), may hold values from -6 to 6
- lengths: int32 [16], P('dp'), may hold values from 128 to 1024, as said below
- steps: int32 [16], P('dp'), may hold values from 0 to 1023
- mod_weight: bfloat16 [4, 768, 2304], P('segment'), may hold values from -0.21875 to 0.21875
- mod_bias: bfloat16 [4, 2304], P('segment'), may hold values from -3 to 3
- first_weight: bfloat16 [4, 768, 3072], P('segment')
- down_rows: bfloat16 [4, 1536, 768], P('segment'), may hold values from -0.109375 to 0.109375
Outputs:
- block_output: bfloat16 [16, 1024, 768], P('dp', 'segment')
- input_grad: float32 [16, 1024, 768], P('dp', 'segment')
- mod_weight_grad: float32 [4, 768, 2304], P('segment', 'dp')
- mod_bias_grad: float32 [4, 2304], P('segment', 'dp')
- first_weight_grad: float32 [4, 768, 3072], P('segment', 'dp')
- down_rows_grad: float32 [4, 1536, 768], P('segment', 'dp')
The draws below stay inside these ranges and needn't reach their ends.
Inputs may be any that keep to these rules, and one draw needn't show every extreme that they name: In each aligned group of 2 sequences (those of one index of dp) one, drawn from the seed, has exactly 1024 tokens; the others lean to short lengths.
All inputs are finite; a program needn't handle non-finite values.
Results may differ from the reference program's by a relative error of at most 0.028.
Values may be sent and summed in bfloat16 or wider, within the bound.
A program may use at most 320 MiB of HBM per device.

```python
import math
import jax
import jax.numpy as jnp
from jax import lax

D = 768
HEADS = 12
HEAD_DIM = 64
FF = 3072
SEQ_LEN = 1024
MIN_LEN = 128
MICRO = 2
HALVES = 4
TSTEPS = 1024
SEQS = 16


def draw_lengths(key, part):
    key = jax.random.fold_in(key, 1)
    draw_key, pick_key = jax.random.split(key)
    raw_draws = jax.random.randint(draw_key, (3, SEQS), 0, SEQ_LEN - MIN_LEN + 1)
    shortest = MIN_LEN + jnp.min(raw_draws, axis=0)
    chosen = jax.random.randint(pick_key, (SEQS // MICRO, 1), 0, MICRO)
    marks = jnp.arange(MICRO)[None, :] == chosen
    grouped = jnp.where(marks, SEQ_LEN, shortest.reshape(SEQS // MICRO, MICRO))
    return grouped.reshape(SEQS).astype(jnp.int32)


def draw_block_input(key, part):
    key = jax.random.fold_in(key, 2)
    base_key, row_key, column_key = jax.random.split(key, 3)
    full_shape = (SEQS, SEQ_LEN, D)
    row_scale = jnp.exp(jax.random.uniform(row_key, (SEQS, SEQ_LEN, 1), minval=math.log(0.3), maxval=math.log(3.0)))
    column_scale = jnp.exp(jax.random.uniform(column_key, (D,), minval=math.log(0.5), maxval=math.log(2.0)))
    base_values = jax.random.normal(base_key, full_shape)
    return (jnp.clip(base_values, -4.0, 4.0) * row_scale * column_scale).astype(jnp.bfloat16)


def draw_first_weight(key, part):
    key = jax.random.fold_in(key, 3)
    full_shape = (HALVES, D, FF)
    base_values = jnp.clip(jax.random.normal(key, full_shape), -4.0, 4.0)
    boost = math.sqrt((MIN_LEN + SEQ_LEN) / 8.0)
    attention_rows = (jnp.arange(HALVES) % 2 == 0)[:, None, None]
    output_columns = (jnp.arange(FF) >= 3 * D)[None, None, :]
    factor = jnp.where(attention_rows & output_columns, boost, 1.0)
    return (base_values * factor / math.sqrt(D)).astype(jnp.bfloat16)


def with_ends(values, rng, least, largest):
    extent = values.shape
    spot = [jax.random.randint(jax.random.fold_in(rng, axis), (), 0, extent[axis]) for axis in range(len(extent))]
    values = values.at[tuple(spot)].set(least)
    longest = extent.index(max(extent))
    spot[longest] = (spot[longest] + 1) % extent[longest]
    return values.at[tuple(spot)].set(largest)


def block_levels(key, dims, shards, least, high):
    def one(axis_at, blocks):
        heights = jax.random.uniform(jax.random.fold_in(jax.random.fold_in(key, 6), axis_at), (blocks,), jnp.float32, least / len(shards), high / len(shards))
        return jnp.repeat(jnp.exp(heights), dims[axis_at] // blocks).reshape((-1,) + (1,) * (len(dims) - axis_at - 1))

    gain = one(*shards[0])
    for cut in shards[1:]:
        gain = gain * one(*cut)
    return gain


def centred(key, shape, deviation, limit, cuts=(), held_as=jnp.bfloat16):
    values = jax.random.normal(key, shape, jnp.float32) * deviation
    if len(cuts) > 0:
        values = block_levels(key, shape, cuts, -0.22, 0.18) * values
    return jnp.clip(values, min=-limit, max=limit).astype(held_as)


def setup_inputs(seed: int = 0) -> dict:
    keys = jax.random.split(jax.random.key(seed), 9)
    return {
        "block_input": draw_block_input(jax.random.fold_in(keys[8], 71), 0),
        "cotangent": centred(keys[1], (SEQS, SEQ_LEN, D), 1.0, 6.0, ((0, 8),)),
        "lengths": draw_lengths(jax.random.fold_in(keys[8], 71), 0),
        "steps": with_ends(jax.random.randint(keys[3], (SEQS,), 0, TSTEPS), jax.random.fold_in(keys[3], 1), 0, TSTEPS - 1).astype(jnp.int32),
        "mod_weight": centred(keys[4], (HALVES, D, 3 * D), D ** -0.5, 0.21875, ((0, 4),)),
        "mod_bias": centred(keys[5], (HALVES, 3 * D), 0.5, 3.0, ((0, 4),)),
        "first_weight": draw_first_weight(jax.random.fold_in(keys[8], 71), 0),
        "down_rows": centred(keys[7], (HALVES, FF // 2, D), FF ** -0.5, 0.109375, ((0, 4),)),
    }


@jax.custom_vjp
def low(v):
    return lax.optimization_barrier(v.astype(jnp.bfloat16)).astype(jnp.float32)

@jax.custom_vjp
def low_back(v):
    return v

def low_keep(v):
    return (low(v), None)

def low_pass(kept, grad):
    return (grad,)

def back_keep(v):
    return (v, None)

def back_low(kept, grad):
    return (low(grad),)
low.defvjp(low_keep, low_pass)
low_back.defvjp(back_keep, back_low)

def matmul(left, right):
    return jnp.dot(left, right, precision=lax.Precision.HIGHEST, preferred_element_type=jnp.float32)

def time_cond(steps):
    half_width = D // 2
    frequency = jnp.exp(jnp.arange(half_width, dtype=jnp.float32) * (-math.log(10000.0) / half_width))
    angles = steps.astype(jnp.float32)[:, None] * frequency[None, :]
    return jax.nn.silu(jnp.concatenate([jnp.cos(angles), jnp.sin(angles)], axis=1))

def rope_tables():
    pair_count = HEAD_DIM // 2
    inverse = jnp.exp(jnp.arange(pair_count, dtype=jnp.float32) * (-math.log(10000.0) / pair_count))
    angles = jnp.arange(SEQ_LEN, dtype=jnp.float32)[:, None] * inverse[None, :]
    return (jnp.cos(angles)[:, None, :], jnp.sin(angles)[:, None, :])

def rotate(values, cosine, sine_table):
    first_half = values[..., :HEAD_DIM // 2]
    second_half = values[..., HEAD_DIM // 2:]
    return jnp.concatenate([first_half * cosine - second_half * sine_table, second_half * cosine + first_half * sine_table], axis=-1)

def layer_norm(stream):
    center = stream - lax.optimization_barrier(jnp.mean(stream, axis=-1, keepdims=True))
    return center * lax.rsqrt(lax.optimization_barrier(jnp.mean(center * center, axis=-1, keepdims=True)) + 1e-06)

def attention_half(stream, live_rows, length, modrow, weights):
    offset, scaling, gating = (modrow[:D], modrow[D:2 * D], modrow[2 * D:])
    normed = low(layer_norm(stream) * (1.0 + scaling) + offset)
    project = low_back(matmul(normed, weights[:, :3 * D]))
    cosine, sine_table = rope_tables()
    queries = project[:, :D].reshape(SEQ_LEN, HEADS, HEAD_DIM)
    keys_rot = project[:, D:2 * D].reshape(SEQ_LEN, HEADS, HEAD_DIM)
    values = project[:, 2 * D:].reshape(SEQ_LEN, HEADS, HEAD_DIM)
    queries = low(low_back(rotate(queries, cosine, sine_table) * 0.125))
    keys_rot = low(low_back(rotate(keys_rot, cosine, sine_table)))
    values = low(low_back(values))
    usable = jnp.arange(SEQ_LEN) < length
    block_rows = min(512, SEQ_LEN)

    def attend_block(query_block):
        scores = low_back(jnp.einsum('qhd,khd->hqk', query_block, keys_rot, precision=lax.Precision.HIGHEST))
        scores = jnp.where(usable[None, None, :], scores, -jnp.inf)
        weights_soft = low(jax.nn.softmax(scores, axis=-1))
        return jnp.einsum('hqk,khd->qhd', weights_soft, values, precision=lax.Precision.HIGHEST)
    mixture = lax.map(jax.checkpoint(attend_block), queries.reshape(SEQ_LEN // block_rows, block_rows, HEADS, HEAD_DIM))
    mixture = low(low_back(mixture.reshape(SEQ_LEN, D)))
    branch = low_back(matmul(mixture, weights[:, 3 * D:]))
    return stream + live_rows[:, None] * gating * branch

def feedforward_half(stream, live_rows, modrow, weights, down_full):
    offset, scaling, gating = (modrow[:D], modrow[D:2 * D], modrow[2 * D:])
    normed = low(layer_norm(stream) * (1.0 + scaling) + offset)
    hidden = low_back(matmul(normed, weights))
    activation = low(jax.nn.gelu(hidden, approximate=True))
    branch = low_back(matmul(activation, down_full))
    return stream + live_rows[:, None] * gating * branch

def run_sequence(stream, length, condrow, mod_weight, mod_bias, firsts, down_sets):
    live_rows = (jnp.arange(SEQ_LEN) < length).astype(jnp.float32)
    for section in range(HALVES):
        modrow = matmul(low(condrow)[None, :], mod_weight[section])[0] + mod_bias[section]
        if section % 2 == 0:
            output = attention_half(stream, live_rows, length, modrow, firsts[section])
        else:
            down_full = jnp.concatenate([down_sets[section - 1], down_sets[section]], axis=0)
            output = feedforward_half(stream, live_rows, modrow, firsts[section], down_full)
        if section + 1 < HALVES:
            stream = low(low_back(output))
        else:
            stream = output
    return stream

def reference(block_input, cotangent, lengths, steps, mod_weight, mod_bias, first_weight, down_rows):
    conditions = time_cond(steps)

    def forward(stream_all, mod_w_all, mod_b_all, firsts, down_sets):

        def one_sequence(pieces):
            return run_sequence(pieces[0], pieces[1], pieces[2], mod_w_all, mod_b_all, firsts, down_sets)
        return lax.map(jax.checkpoint(one_sequence), (stream_all, lengths, conditions))
    output, pullback = jax.vjp(forward, block_input.astype(jnp.float32), mod_weight.astype(jnp.float32), mod_bias.astype(jnp.float32), first_weight.astype(jnp.float32), down_rows.astype(jnp.float32))
    gradients = pullback(cotangent.astype(jnp.float32))
    return (output.astype(jnp.bfloat16), gradients[0], gradients[1], gradients[2], gradients[3], gradients[4])
```

```python
import functools
import math

import jax
import jax.numpy as jnp
import numpy as np
from jax import lax
from jax.experimental import pallas as pl
from jax.experimental.pallas import tpu as pltpu
from jax.sharding import PartitionSpec as P

D = 768
HEADS = 12
HEAD_DIM = 64
FF = 3072
SEQ_LEN = 1024
BLK = 256
HALF = SEQ_LEN // 2
MB = 4
XS, QS, AT, BR, NM, GB, DQ = range(7)
VLIM = 56 << 20
bf16, f32, i32 = jnp.bfloat16, jnp.float32, jnp.int32


def dot(a, b):
    return lax.dot_general(a, b, (((1,), (0,)), ((), ())), preferred_element_type=f32)


def dot_nt(a, b):
    return lax.dot_general(a, b, (((1,), (1,)), ((), ())), preferred_element_type=f32)


def dot_tn(a, b):
    return lax.dot_general(a, b, (((0,), (0,)), ((), ())), preferred_element_type=f32)


def block_rows(b):
    return pl.ds(pl.multiple_of(b * BLK, BLK), BLK)


def lanes(p):
    return pl.ds(pl.multiple_of(p * 128, 128), 128)


def norm_parts(x):
    center = x - jnp.mean(x, axis=-1, keepdims=True)
    rstd = lax.rsqrt(jnp.mean(center * center, axis=-1, keepdims=True) + 1e-06)
    return center * rstd, rstd


def norm_back(d_normed, n, rstd, scl):
    dn = d_normed * scl
    return (
        dn - jnp.mean(dn, axis=-1, keepdims=True) - n * jnp.mean(dn * n, axis=-1, keepdims=True)
    ) * rstd


def turn(v, cosine, sine):
    lane = lax.broadcasted_iota(i32, v.shape, 1)
    partner = jnp.where(lane % 64 < 32, pltpu.roll(v, 96, 1), pltpu.roll(v, 32, 1))
    return v * cosine + partner * sine


def live_column(rows, c, length, first=0):
    r = lax.broadcasted_iota(i32, (rows, 1), 0) + first
    position = r + BLK * c + jnp.where(r >= BLK, BLK, 0)
    return position < length


def counts(length, c):
    nk = lax.shift_right_logical(length + (BLK - 1), 8)
    return nk, lax.shift_right_logical(nk - c + 1, 1)


class Copies:
    def __init__(self, sems):
        self.sems, self.started = sems, []

    def add(self, src, dst):
        copy = pltpu.make_async_copy(src, dst, self.sems.at[len(self.started)])
        copy.start()
        self.started.append(copy)

    def wait(self):
        for copy in self.started:
            copy.wait()


def att_f_kernel(sc, tt, hop_own, hop_oth, own_x, rcv_x, w, cos, sin, mod, st_i, kv_i, lse_i,
                 out, st, kv, lse,
                 xv, nv, wv, kvv, vv, qv, av, bv, ov, lv, cv, sv, sem, osem):
    role = sc[0]
    mb = tt[role]

    @pl.when(mb >= 0)
    def _():
        c, length, idx = sc[1], sc[2 + mb], sc[6 + mb]
        nk, ns = counts(length, c)
        mine = lax.rem(mb, 2) == c

        @pl.when((role == 0) & mine)
        def _():
            pltpu.make_async_copy(own_x.at[idx], xv, sem.at[0]).start()

        @pl.when((role == 0) & jnp.logical_not(mine))
        def _():
            pltpu.make_async_copy(rcv_x.at[idx], xv, sem.at[0]).start()

        @pl.when(role != 0)
        def _():
            for j in range(2):
                rows = pl.ds(j * BLK, BLK)
                pltpu.make_async_copy(
                    hop_own.at[rows], xv.at[block_rows(c + 2 * j)], sem.at[0]
                ).start()
                pltpu.make_async_copy(
                    hop_oth.at[rows], xv.at[block_rows(1 - c + 2 * j)], sem.at[0]
                ).start()

        wcopies = []
        for part in (1, 2, 0, 3):
            cols = pl.ds(part * D, D)
            copy = pltpu.make_async_copy(w.at[:, cols], wv.at[:, cols], sem.at[1 + part])
            copy.start()
            wcopies.append(copy)
        tables = [
            pltpu.make_async_copy(cos, cv, sem.at[5]),
            pltpu.make_async_copy(sin, sv, sem.at[6]),
        ]
        for copy in tables:
            copy.start()
        off, scl, gat = mod[mb, 0:1, :], 1.0 + mod[mb, 1:2, :], mod[mb, 2:3, :]
        pltpu.make_async_copy(own_x.at[0], xv, sem.at[0]).wait()

        def norm_block(b, carry):
            rows = block_rows(b)
            n, _ = norm_parts(xv[rows, :].astype(f32))
            nv[rows, :] = (n * scl + off).astype(bf16)
            return carry

        lax.fori_loop(0, nk, norm_block, 0)
        for copy in tables:
            copy.wait()
        wcopies[0].wait()
        wcopies[1].wait()

        def kv_block(b, carry):
            rows = block_rows(b)
            n = nv[rows, :]
            cosine, sine = cv[rows, :], sv[rows, :]
            kk = dot(n, wv[:, D : 2 * D])
            for p in range(6):
                kvv[rows, p * 128 : (p + 1) * 128] = turn(
                    kk[:, p * 128 : (p + 1) * 128], cosine, sine
                ).astype(bf16)
            vv[rows, :] = dot(n, wv[:, 2 * D : 3 * D]).astype(bf16)
            return carry

        lax.fori_loop(0, nk, kv_block, 0)
        wcopies[2].wait()

        def q_block(j, carry):
            nat = block_rows(c + 2 * j)
            rows = block_rows(j)
            cosine, sine = cv[nat, :] * 0.125, sv[nat, :] * 0.125
            qq = dot(nv[nat, :], wv[:, 0:D])
            for p in range(6):
                qv[rows, p * 128 : (p + 1) * 128] = turn(
                    qq[:, p * 128 : (p + 1) * 128], cosine, sine
                ).astype(bf16)
            return carry

        lax.fori_loop(0, ns, q_block, 0)
        sends = Copies(osem)
        sends.add(qv, st.at[QS, mb])
        sends.add(kvv, kv.at[0, mb])
        sends.add(vv, kv.at[1, mb])
        for j in range(2):
            sends.add(xv.at[block_rows(c + 2 * j)], st.at[XS, mb, pl.ds(j * BLK, BLK)])

        lane = lax.broadcasted_iota(i32, (BLK, 128), 1)

        def attend(keys, masked):
            if masked:
                position = lax.broadcasted_iota(i32, (1, keys), 1)
                bias = jnp.where(position < length, 0.0, -1e30).astype(f32)

            def slot(j, carry):
                rows = block_rows(j)
                lv[rows, :] = jnp.zeros((BLK, 128), f32)

                def pair(hp, carry):
                    ls = lanes(hp)
                    k2, v2, q2 = kvv[0:keys, ls], vv[0:keys, ls], qv[rows, ls]
                    outs, stats = [], lv[rows, :]
                    for a in range(2):
                        s = dot_nt(jnp.where((lane < 64) == (a == 0), q2, jnp.zeros_like(q2)), k2)
                        if masked:
                            s = s + bias
                        m = jnp.max(s, axis=1, keepdims=True)
                        e = jnp.exp(s - m)
                        total = jnp.sum(e, axis=1, keepdims=True)
                        outs.append(dot(e.astype(bf16), v2) / total)
                        stats = jnp.where(lane == 2 * hp + a, m + jnp.log(total), stats)
                    av[rows, ls] = jnp.where(lane < 64, outs[0], outs[1]).astype(bf16)
                    lv[rows, :] = stats
                    return carry

                return lax.fori_loop(0, HEADS // 2, pair, carry)

            lax.fori_loop(0, ns, slot, 0)

        pl.when(length == SEQ_LEN)(lambda: attend(SEQ_LEN, False))
        for blocks in range(1, 5):
            pl.when((nk == blocks) & (length < SEQ_LEN))(
                functools.partial(attend, blocks * BLK, True)
            )
        wcopies[3].wait()

        def out_block(j, carry):
            rows = block_rows(j)
            branch = dot(av[rows, :], wv[:, 3 * D : 4 * D])
            live = live_column(BLK, c, length, j * BLK)
            x = xv[block_rows(c + 2 * j), :].astype(f32)
            ov[rows, :] = (x + jnp.where(live, gat * branch, 0.0)).astype(bf16)
            bv[rows, :] = branch.astype(bf16)
            return carry

        lax.fori_loop(0, ns, out_block, 0)
        sends.add(ov, out)
        sends.add(av, st.at[AT, mb])
        sends.add(bv, st.at[BR, mb])
        sends.add(lv, lse.at[mb])
        sends.wait()


def load_ff_weights(c, w1, prt_own, prt_oth, rows2, w1v, w2v, sem):
    half = FF // 4
    ups = []
    for part in range(4):
        cols = pl.ds(part * D, D)
        ups.append(pltpu.make_async_copy(w1.at[:, cols], w1v.at[:, cols], sem.at[part]))
        ups[-1].start()
        if part == 0:
            mine = pl.ds(pl.multiple_of(c * half, half), half)
            other = pl.ds(pl.multiple_of((1 - c) * half, half), half)
            pltpu.make_async_copy(prt_own, w2v.at[mine], sem.at[4]).start()
            pltpu.make_async_copy(prt_oth, w2v.at[other], sem.at[4]).start()
    tail = pl.ds(2 * half, 2 * half)
    second = pltpu.make_async_copy(rows2, w2v.at[tail], sem.at[5])
    second.start()

    def wait(part):
        ups[part].wait()
        if part == 0:
            pltpu.make_async_copy(rows2, w2v.at[tail], sem.at[4]).wait()
        if part == 2:
            second.wait()

    return wait


def gelu_parts(u):
    u2 = u * u
    t = jnp.tanh(0.7978845608028654 * (u * (1.0 + 0.044715 * u2)))
    return t, u2


def ff_f_kernel(sc, tt, hop, w1, prt_own, prt_oth, rows2, mod, st_i,
                out, st, xv, nv, w1v, w2v, ov, bv, sem, osem):
    role = sc[0]
    mb = tt[role]

    @pl.when(mb >= 0)
    def _():
        c, length = sc[1], sc[2 + mb]
        _, ns = counts(length, c)
        load = pltpu.make_async_copy(hop, xv, sem.at[6])
        load.start()
        wait = load_ff_weights(c, w1, prt_own, prt_oth, rows2, w1v, w2v, sem)
        off, scl, gat = mod[mb, 0:1, :], 1.0 + mod[mb, 1:2, :], mod[mb, 2:3, :]
        load.wait()
        sends = Copies(osem)
        sends.add(xv, st.at[XS, mb])

        def norm_block(j, carry):
            rows = block_rows(j)
            n, _ = norm_parts(xv[rows, :].astype(f32))
            nv[rows, :] = (n * scl + off).astype(bf16)
            return carry

        lax.fori_loop(0, ns, norm_block, 0)
        for part in range(4):
            wait(part)

        def body(rows):
            acc = jnp.zeros((rows, D), f32)
            for part in range(4):
                u = dot(nv[0:rows, :], w1v[:, part * D : (part + 1) * D])
                t, _ = gelu_parts(u)
                act = (0.5 * u * (1.0 + t)).astype(bf16)
                acc = acc + dot(act, w2v[part * D : (part + 1) * D, :])
            live = live_column(rows, c, length)
            x = xv[0:rows, :].astype(f32)
            ov[0:rows, :] = (x + jnp.where(live, gat * acc, 0.0)).astype(bf16)
            bv[0:rows, :] = acc.astype(bf16)

        pl.when(ns == 2)(lambda: body(HALF))
        pl.when(ns == 1)(lambda: body(BLK))
        sends.add(ov, out)
        sends.add(bv, st.at[BR, mb])
        sends.wait()


def ff_b_kernel(sc, tt, hop, own_c, rcv_c, w1, prt_own, prt_oth, rows2, mod, st_i, y_i, act_i, dm_i,
                out, st, y, act, dm,
                xv, gv, brv, nv, gbv, w1v, w2v, duv, actv, ov, dmv, sem, osem):
    role = sc[0]
    mb = tt[role]

    @pl.when(mb >= 0)
    def _():
        c, length, idx = sc[1], sc[2 + mb], sc[6 + mb]
        _, ns = counts(length, c)
        mine = lax.rem(mb, 2) == c

        @pl.when(role == 1)
        def _():
            pltpu.make_async_copy(hop, gv, sem.at[6]).start()

        for pick, source in ((mine, own_c), (jnp.logical_not(mine), rcv_c)):

            @pl.when((role == 3) & pick)
            def _():
                for j in range(2):
                    pltpu.make_async_copy(
                        source.at[idx, block_rows(c + 2 * j)], gv.at[pl.ds(j * BLK, BLK)], sem.at[6]
                    ).start()

        loads = [
            pltpu.make_async_copy(st.at[XS, mb], xv, sem.at[7]),
            pltpu.make_async_copy(st.at[BR, mb], brv, sem.at[8]),
        ]
        for copy in loads:
            copy.start()
        wait = load_ff_weights(c, w1, prt_own, prt_oth, rows2, w1v, w2v, sem)
        off, scl, gat = mod[mb, 0:1, :], 1.0 + mod[mb, 1:2, :], mod[mb, 2:3, :]
        dmv[...] = jnp.zeros((8, D), f32)
        pltpu.make_async_copy(hop, gv, sem.at[6]).wait()
        for copy in loads:
            copy.wait()

        def norm_block(j, carry):
            rows = block_rows(j)
            n, _ = norm_parts(xv[rows, :].astype(f32))
            nv[rows, :] = (n * scl + off).astype(bf16)
            live = live_column(BLK, c, length, j * BLK)
            gl = jnp.where(live, gv[rows, :].astype(f32), 0.0)
            gbv[rows, :] = (gl * gat).astype(bf16)
            dmv[2:3, :] += jnp.sum(gl * brv[rows, :].astype(f32), axis=0, keepdims=True)
            return carry

        lax.fori_loop(0, ns, norm_block, 0)
        sends = Copies(osem)
        sends.add(nv, st.at[NM, mb])
        sends.add(gbv, st.at[GB, mb])
        for part in range(4):
            wait(part)

        def body(rows):
            acc = jnp.zeros((rows, D), f32)
            for part in range(4):
                cols = slice(part * D, (part + 1) * D)
                u = dot(nv[0:rows, :], w1v[:, cols])
                t, u2 = gelu_parts(u)
                half = 0.5 * (1.0 + t)
                actv[0:rows, cols] = (u * half).astype(bf16)
                slope = half + 0.5 * u * (1.0 - t * t) * (
                    0.7978845608028654 * (1.0 + 3 * 0.044715 * u2)
                )
                du = (dot_nt(gbv[0:rows, :], w2v[cols, :]) * slope).astype(bf16)
                duv[0:rows, cols] = du
                acc = acc + dot_nt(du, w1v[:, cols])
            n, rstd = norm_parts(xv[0:rows, :].astype(f32))
            dmv[0:1, :] = jnp.sum(acc, axis=0, keepdims=True)
            dmv[1:2, :] = jnp.sum(acc * n, axis=0, keepdims=True)
            ov[0:rows, :] = (
                gv[0:rows, :].astype(f32) + norm_back(acc, n, rstd, scl)
            ).astype(bf16)

        pl.when(ns == 2)(lambda: body(HALF))
        pl.when(ns == 1)(lambda: body(BLK))
        sends.add(ov, out)
        sends.add(duv, y.at[mb])
        sends.add(actv, act.at[mb])
        sends.add(dmv, dm.at[mb])
        sends.wait()


def att_b1_kernel(sc, tt, hop0, hop2, w, mod, kv, lse, st_i, y_i,
                  own, snd, st, y,
                  gv, atv, qv, kvv, vv, wo, lv, gbv, dov, dqv, dkt, dvt, sem, osem):
    role = sc[0]
    mb = tt[role]

    @pl.when(mb >= 0)
    def _():
        c, length = sc[1], sc[2 + mb]
        nk, ns = counts(length, c)
        for who, hop in ((0, hop0), (2, hop2)):
            pl.when(role == who)(lambda: pltpu.make_async_copy(hop, gv, sem.at[0]).start())
        loads = [
            pltpu.make_async_copy(w.at[:, pl.ds(3 * D, D)], wo, sem.at[1]),
            pltpu.make_async_copy(st.at[QS, mb], qv, sem.at[2]),
            pltpu.make_async_copy(kv.at[0, mb], kvv, sem.at[3]),
            pltpu.make_async_copy(kv.at[1, mb], vv, sem.at[4]),
            pltpu.make_async_copy(st.at[AT, mb], atv, sem.at[5]),
            pltpu.make_async_copy(lse.at[mb], lv, sem.at[6]),
        ]
        for copy in loads:
            copy.start()
        gat = mod[mb, 2:3, :]
        pltpu.make_async_copy(hop0, gv, sem.at[0]).wait()
        loads[0].wait()

        def grad_block(j, carry):
            rows = block_rows(j)
            live = live_column(BLK, c, length, j * BLK)
            gb = jnp.where(live, gv[rows, :].astype(f32) * gat, 0.0).astype(bf16)
            gbv[rows, :] = gb
            dov[rows, :] = dot_nt(gb, wo[...]).astype(bf16)
            return carry

        lax.fori_loop(0, ns, grad_block, 0)
        sends = Copies(osem)
        sends.add(gbv, y.at[mb, :, pl.ds(3 * D, D)])
        for copy in loads[1:]:
            copy.wait()

        def attend(rows, keys, masked):
            lane = lax.broadcasted_iota(i32, (rows, 128), 1)
            if masked:
                position = lax.broadcasted_iota(i32, (1, keys), 1)
                bias = jnp.where(position < length, 0.0, -1e30).astype(f32)

            def pair(hp, carry):
                ls = lanes(hp)
                k2, v2 = kvv[0:keys, ls], vv[0:keys, ls]
                q2, do2 = qv[0:rows, ls], dov[0:rows, ls]
                q2t, do2t = q2.T, do2.T
                both = do2.astype(f32) * atv[0:rows, ls].astype(f32)
                stats = lv[0:rows, :]
                dqs = []
                for a in range(2):
                    head = (lane < 64) == (a == 0)
                    zero = jnp.zeros_like(q2)
                    s = dot_nt(jnp.where(head, q2, zero), k2)
                    if masked:
                        s = s + bias
                    base = jnp.sum(jnp.where(lane == 2 * hp + a, stats, 0.0), axis=1, keepdims=True)
                    p = jnp.exp(s - base)
                    dp = dot_nt(jnp.where(head, do2, zero), v2)
                    delta = jnp.sum(jnp.where(head, both, 0.0), axis=1, keepdims=True)
                    ds = (p * (dp - delta)).astype(bf16)
                    dqs.append(dot(ds, k2))
                    at = pl.ds(pl.multiple_of(hp * 128 + a * 64, 64), 64)
                    dkt[at, 0:keys] = dot(q2t[a * 64 : (a + 1) * 64, :], ds).astype(bf16)
                    dvt[at, 0:keys] = dot(do2t[a * 64 : (a + 1) * 64, :], p.astype(bf16)).astype(
                        bf16
                    )
                dqv[0:rows, ls] = jnp.where(lane < 64, dqs[0], dqs[1]).astype(bf16)
                return carry

            lax.fori_loop(0, HEADS // 2, pair, 0)

        pl.when(length == SEQ_LEN)(lambda: attend(HALF, SEQ_LEN, False))
        for slots, blocks in ((1, 1), (1, 2), (1, 3), (2, 3), (2, 4)):
            pl.when((ns == slots) & (nk == blocks) & (length < SEQ_LEN))(
                functools.partial(attend, slots * BLK, blocks * BLK, True)
            )

        @pl.when(ns == 0)
        def _():
            dkt[:, 0:BLK] = jnp.zeros((D, BLK), bf16)
            dvt[:, 0:BLK] = jnp.zeros((D, BLK), bf16)

        sends.add(dqv, st.at[DQ, mb])
        for part, grad in enumerate((dkt, dvt)):
            for j in range(2):
                cols = pl.ds(j * BLK, BLK)
                sends.add(grad.at[:, block_rows(c + 2 * j)], own.at[part, :, cols])
                sends.add(grad.at[:, block_rows(1 - c + 2 * j)], snd.at[part, :, cols])
        sends.wait()


def att_b2_kernel(sc, tt, hop0, hop2, own, rcv, w, cos, sin, mod, st_i, y_i, dm_i,
                  out, st, y, dm,
                  gv, xv, brv, dqv, ownv, rcvv, wv, cv, sv, nv, dpv, ov, dmv, sem, osem):
    role = sc[0]
    mb = tt[role]

    @pl.when(mb >= 0)
    def _():
        c, length = sc[1], sc[2 + mb]
        _, ns = counts(length, c)
        for who, hop in ((0, hop0), (2, hop2)):
            pl.when(role == who)(lambda: pltpu.make_async_copy(hop, gv, sem.at[0]).start())
        loads = [
            pltpu.make_async_copy(own, ownv, sem.at[1]),
            pltpu.make_async_copy(rcv, rcvv, sem.at[2]),
            pltpu.make_async_copy(st.at[DQ, mb], dqv, sem.at[3]),
            pltpu.make_async_copy(st.at[XS, mb], xv, sem.at[4]),
            pltpu.make_async_copy(st.at[BR, mb], brv, sem.at[5]),
            pltpu.make_async_copy(cos, cv, sem.at[6]),
            pltpu.make_async_copy(sin, sv, sem.at[7]),
            pltpu.make_async_copy(w.at[:, pl.ds(0, 3 * D)], wv, sem.at[8]),
        ]
        for copy in loads:
            copy.start()
        off, scl = mod[mb, 0:1, :], 1.0 + mod[mb, 1:2, :]
        dmv[...] = jnp.zeros((8, D), f32)
        pltpu.make_async_copy(hop0, gv, sem.at[0]).wait()
        for copy in loads[:-1]:
            copy.wait()

        def first(j, carry):
            rows, nat = block_rows(j), block_rows(c + 2 * j)
            cosine, sine = cv[nat, :], -sv[nat, :]
            for p in range(6):
                ls = slice(p * 128, (p + 1) * 128)
                dpv[rows, ls] = (turn(dqv[rows, ls].astype(f32), cosine, sine) * 0.125).astype(bf16)
                for part in range(2):
                    total = ownv[part, ls, rows].astype(f32) + rcvv[part, ls, rows].astype(f32)
                    grad = total.T
                    if part == 0:
                        grad = turn(grad.astype(bf16).astype(f32), cosine, sine)
                    dpv[rows, (part + 1) * D + p * 128 : (part + 1) * D + (p + 1) * 128] = (
                        grad.astype(bf16)
                    )
            return carry

        lax.fori_loop(0, ns, first, 0)
        sends = Copies(osem)
        sends.add(dpv, y.at[mb, :, pl.ds(0, 3 * D)])
        loads[-1].wait()

        def second(j, carry):
            rows = block_rows(j)
            acc = dot_nt(dpv[rows, :], wv[...])
            n, rstd = norm_parts(xv[rows, :].astype(f32))
            nv[rows, :] = (n * scl + off).astype(bf16)
            g = gv[rows, :].astype(f32)
            live = live_column(BLK, c, length, j * BLK)
            gl = jnp.where(live, g, 0.0)
            dmv[0:1, :] += jnp.sum(acc, axis=0, keepdims=True)
            dmv[1:2, :] += jnp.sum(acc * n, axis=0, keepdims=True)
            dmv[2:3, :] += jnp.sum(gl * brv[rows, :].astype(f32), axis=0, keepdims=True)
            ov[rows, :] = (g + norm_back(acc, n, rstd, scl)).astype(bf16)
            return carry

        lax.fori_loop(0, ns, second, 0)
        sends.add(ov, out)
        sends.add(nv, st.at[NM, mb])
        sends.add(dmv, dm.at[mb])
        sends.wait()


def first_grad_kernel(sc, x1, x2, y, out, acc):
    c = sc[1]
    acc[...] = jnp.zeros((D, D), f32)
    second = (lax.rem(sc[0], 2) == 0) & (pl.program_id(0) == 3)
    for mb in range(MB):
        _, ns = counts(sc[2 + mb], c)
        for slots in (1, 2):
            rows = slots * BLK

            @pl.when((ns == slots) & second)
            def _():
                acc[...] += dot_tn(x2[0, mb, 0:rows, :], y[mb, 0:rows, :])

            @pl.when((ns == slots) & jnp.logical_not(second))
            def _():
                acc[...] += dot_tn(x1[0, mb, 0:rows, :], y[mb, 0:rows, :])

    out[...] = acc[...].astype(bf16)


def down_grad_kernel(sc, act, gb, out, acc):
    c = sc[1]

    @pl.when(lax.rem(sc[0], 2) == 1)
    def _():
        acc[...] = jnp.zeros((D, D), f32)
        for mb in range(MB):
            _, ns = counts(sc[2 + mb], c)
            for slots in (1, 2):
                rows = slots * BLK

                @pl.when(ns == slots)
                def _():
                    acc[...] += dot_tn(act[mb, 0:rows, :], gb[0, mb, 0:rows, :])

        out[...] = acc[...].astype(bf16)


ANY = pl.BlockSpec(memory_space=pl.ANY)
VMEM = pl.BlockSpec(memory_space=pltpu.VMEM)


def shape(dims, dtype=bf16):
    return jax.ShapeDtypeStruct(dims, dtype)


ROWS = shape((HALF, D))
ST = shape((7, MB, HALF, D))
KV = shape((2, MB, SEQ_LEN, D))
LSE = shape((MB, HALF, 128), f32)
YS = shape((MB, HALF, FF))
DM = shape((MB, 8, D), f32)
DKV = shape((2, D, HALF))


def vm(dims, dtype=bf16):
    return pltpu.VMEM(dims, dtype)


HV, FV = vm((HALF, D)), vm((SEQ_LEN, D))


def call(kernel, scalars, operands, vmem_at, outs, aliases, scratch, sems, name):
    specs = [VMEM if i in vmem_at else ANY for i in range(len(operands))]
    return pl.pallas_call(
        kernel,
        grid_spec=pltpu.PrefetchScalarGridSpec(
            num_scalar_prefetch=2,
            grid=(1,),
            in_specs=specs,
            out_specs=[ANY] * len(outs),
            scratch_shapes=list(scratch)
            + [pltpu.SemaphoreType.DMA((9,)), pltpu.SemaphoreType.DMA((sems,))],
        ),
        out_shape=list(outs),
        input_output_aliases={i + 2: o for i, o in aliases.items()},
        compiler_params=pltpu.CompilerParams(vmem_limit_bytes=VLIM),
        name=name,
    )(*scalars, *operands)


def allocate(outs):
    return pl.pallas_call(
        lambda *refs: None,
        out_shape=list(outs),
        out_specs=[ANY] * len(outs),
        name="allocate",
    )()


def time_cond(steps):
    half_width = D // 2
    frequency = jnp.exp(
        jnp.arange(half_width, dtype=f32) * (-math.log(10000.0) / half_width)
    )
    angles = steps.astype(f32)[:, None] * frequency[None, :]
    return jax.nn.silu(jnp.concatenate([jnp.cos(angles), jnp.sin(angles)], axis=1))


def rope_tables():
    inverse = np.exp(np.arange(32, dtype=np.float32) * np.float32(-math.log(10000.0) / 32))
    angles = np.arange(SEQ_LEN, dtype=np.float32)[:, None] * inverse[None, :]
    cosine, sine = np.cos(angles), np.sin(angles)
    return (
        np.concatenate([cosine] * 4, axis=1).astype(np.float32),
        np.concatenate([-sine, sine, -sine, sine], axis=1).astype(np.float32),
    )


def local(block_input, cotangent, lengths, steps, mod_weight, mod_bias, first_weight, down_rows):
    ndp = lax.axis_size("dp")
    seg, dp = lax.axis_index("segment"), lax.axis_index("dp")
    core = dp % 2
    w, rows2 = first_weight[0], down_rows[0]

    def swap(value):
        return lax.ppermute(value, "dp", [(i, i ^ 1) for i in range(ndp)])

    def hop(value, pairs):
        return lax.ppermute(value, "segment", pairs)

    info = jnp.stack([lengths, steps])
    other_info = swap(info)
    other_x = swap(block_input)
    half_rows = lax.dynamic_slice_in_dim(rows2, core * (FF // 4), FF // 4, axis=0)
    prt_own = hop(half_rows, [(0, 1), (2, 3)])
    prt_oth = swap(prt_own)
    other_c = swap(cotangent)

    info0 = jnp.where(core == 0, info, other_info)
    info1 = jnp.where(core == 0, other_info, info)
    full0 = (info0[0, 1] > info0[0, 0]).astype(i32)
    full1 = (info1[0, 1] > info1[0, 0]).astype(i32)
    places = jnp.stack([full0, full1, 1 - full0, 1 - full1])
    chip = jnp.stack([info0[:, full0], info1[:, full1], info0[:, 1 - full0], info1[:, 1 - full1]])
    sc = jnp.concatenate([jnp.stack([seg, core]), chip[:, 0], places, jnp.zeros((6,), i32)]).astype(i32)
    conditions = time_cond(chip[:, 1]).astype(bf16)
    modulation = jnp.dot(conditions, mod_weight[0], preferred_element_type=f32)
    modulation = modulation + mod_bias[0].astype(f32)
    mod = jnp.pad(modulation.reshape(MB, 3, D), ((0, 0), (0, 5), (0, 0)))
    cos, sin = (jnp.asarray(t) for t in rope_tables())

    st, kv, lse, y, act, dm, blank = allocate([ST, KV, LSE, YS, YS, DM, ROWS])

    def table(turns):
        return np.array([t if 0 <= t < MB else -1 for t in turns], np.int32)

    def att_f(turns, own, oth, st, kv, lse):
        return call(
            att_f_kernel,
            (sc, table(turns)),
            (own, oth, block_input, other_x, w, cos, sin, mod, st, kv, lse),
            (7,),
            (ROWS, ST, KV, LSE),
            {8: 1, 9: 2, 10: 3},
            (FV, FV, vm((D, FF)), FV, FV, HV, HV, HV, HV, vm((HALF, 128), f32),
             vm((SEQ_LEN, 128), f32), vm((SEQ_LEN, 128), f32)),
            9,
            "attention_forward",
        )

    def ff_f(turns, x, st):
        return call(
            ff_f_kernel,
            (sc, table(turns)),
            (x, w, prt_own, prt_oth, rows2, mod, st),
            (5,),
            (ROWS, ST),
            {6: 1},
            (HV, HV, vm((D, FF)), vm((FF, D)), HV, HV),
            3,
            "feedforward_forward",
        )

    def ff_b(turns, g, st, y, act, dm):
        return call(
            ff_b_kernel,
            (sc, table(turns)),
            (g, cotangent, other_c, w, prt_own, prt_oth, rows2, mod, st, y, act, dm),
            (7,),
            (ROWS, ST, YS, YS, DM),
            {8: 1, 9: 2, 10: 3, 11: 4},
            (HV, HV, HV, HV, HV, vm((D, FF)), vm((FF, D)), vm((HALF, FF)), vm((HALF, FF)), HV,
             vm((8, D), f32)),
            6,
            "feedforward_backward",
        )

    def att_b1(turns, g0, g2, st, y):
        return call(
            att_b1_kernel,
            (sc, table(turns)),
            (g0, g2, w, mod, kv, lse, st, y),
            (3,),
            (DKV, DKV, ST, YS),
            {6: 2, 7: 3},
            (HV, HV, HV, FV, FV, vm((D, D)), vm((HALF, 128), f32), HV, HV, HV,
             vm((D, SEQ_LEN)), vm((D, SEQ_LEN))),
            10,
            "attention_backward",
        )

    def att_b2(turns, g0, g2, own, rcv, st, y, dm):
        return call(
            att_b2_kernel,
            (sc, table(turns)),
            (g0, g2, own, rcv, w, cos, sin, mod, st, y, dm),
            (7,),
            (ROWS, ST, YS, DM),
            {8: 1, 9: 2, 10: 3},
            (HV, HV, HV, HV, vm((2, D, HALF)), vm((2, D, HALF)), vm((D, 3 * D)),
             vm((SEQ_LEN, 128), f32), vm((SEQ_LEN, 128), f32), HV, vm((HALF, 3 * D)), HV,
             vm((8, D), f32)),
            4,
            "projection_backward",
        )

    into_ff, into_att = blank, blank
    finals, returned = [], []
    for t in range(7):
        ff_out = att_out = None
        if t >= 1:
            turns = (-1, t - 1, -1, t - 3)
            ff_out, st = ff_f(turns, into_ff, st)
        if t <= 5:
            other = swap(into_att) if 2 <= t else blank
            att_out, st, kv, lse = att_f((t, -1, t - 2, -1), into_att, other, st, kv, lse)
        if t >= 3:
            finals.append(ff_out)
        into_att_next = hop(ff_out, [(1, 2)]) if 1 <= t <= 4 else blank
        into_ff_next = blank
        if t <= 5:
            pairs = [(0, 1)] * (t <= 3) + [(2, 3)] * (t >= 2)
            into_ff_next = hop(att_out, pairs)
        if t >= 3:
            grad, st, y, act, dm = ff_b((-1, -1, -1, t - 3), blank, st, y, act, dm)
            returned.append(hop(grad, [(3, 2)]))
        into_ff, into_att = into_ff_next, into_att_next

    into_ff, into_att = blank, blank
    inputs = []
    for u in range(6):
        if 1 <= u <= 4:
            grad, st, y, act, dm = ff_b((-1, u - 1, -1, -1), into_ff, st, y, act, dm)
        g2 = returned[u] if u < MB else blank
        turns = (u - 2, -1, u, -1)
        own, snd, st, y = att_b1(turns, into_att, g2, st, y)
        rcv = swap(snd)
        gout, st, y, dm = att_b2(turns, into_att, g2, own, rcv, st, y, dm)
        if u >= 2:
            inputs.append(gout)
        into_att = hop(grad, [(1, 0)]) if 1 <= u <= 4 else blank
        into_ff = hop(gout, [(2, 1)]) if u <= 3 else blank

    def weight_call(kernel, operands, specs, out, out_spec, name):
        return pl.pallas_call(
            kernel,
            grid_spec=pltpu.PrefetchScalarGridSpec(
                num_scalar_prefetch=1,
                grid=(4,),
                in_specs=specs,
                out_specs=out_spec,
                scratch_shapes=[vm((D, D), f32)],
            ),
            out_shape=out,
            compiler_params=pltpu.CompilerParams(vmem_limit_bytes=VLIM),
            name=name,
        )(sc, *operands)

    def kept(kind):
        return pl.BlockSpec((1, MB, HALF, D), lambda j, s: (kind, 0, 0, 0))

    wide = pl.BlockSpec((MB, HALF, D), lambda j, s: (0, 0, j))
    down_grad = weight_call(
        down_grad_kernel, (act, st), [wide, kept(GB)], shape((FF, D)),
        pl.BlockSpec((D, D), lambda j, s: (j, 0)), "down_gradient",
    )
    first_grad = weight_call(
        first_grad_kernel, (st, st, y), [kept(NM), kept(AT), wide], shape((D, FF)),
        pl.BlockSpec((D, D), lambda j, s: (0, j)), "first_gradient",
    )
    half = FF // 2
    incoming = hop(down_grad[:half], [(1, 0), (3, 2)])
    rows_grad = jnp.where(seg % 2 == 1, down_grad[half:], incoming)
    first_sum = lax.psum_scatter(first_grad, "dp", scatter_dimension=0, tiled=True)
    rows_sum = lax.psum_scatter(rows_grad, "dp", scatter_dimension=0, tiled=True)

    mod_rows = dm[:, :3, :].reshape(MB, 3 * D)
    all_rows = lax.all_gather(mod_rows, "dp", axis=0, tiled=True)
    all_steps = lax.all_gather(chip[:, 1], "dp", axis=0, tiled=True)
    all_conditions = time_cond(all_steps).astype(bf16).astype(f32)
    depth = D // ndp
    mine = lax.dynamic_slice_in_dim(all_conditions, dp * depth, depth, axis=1)
    mod_w_sum = jnp.dot(mine.T, all_rows, precision=lax.Precision.HIGHEST, preferred_element_type=f32)
    width = 3 * D // ndp
    mod_b_sum = jnp.sum(lax.dynamic_slice_in_dim(all_rows, dp * width, width, axis=1), axis=0)

    def spread(halves, source):
        halves = jnp.stack(halves)
        got = jnp.where((seg == source) & (core == source % 2),
                        lax.slice_in_dim(halves, (source // 2) * BLK, (source // 2 + 1) * BLK, axis=1),
                        jnp.zeros((MB, BLK, D), bf16))
        for target in range(4):
            if target == source:
                continue
            piece = lax.slice_in_dim(halves, (target // 2) * BLK, (target // 2 + 1) * BLK, axis=1)
            pairs = [(source * ndp + d, target * ndp + d) for d in range(ndp) if d % 2 == target % 2]
            got = got + lax.ppermute(piece, ("segment", "dp"), pairs)
        pair = got.reshape(2, 2, BLK, D)
        keep = lax.dynamic_index_in_dim(pair, core, axis=1, keepdims=False)
        give = lax.dynamic_index_in_dim(pair, 1 - core, axis=1, keepdims=False)
        both = jnp.where(core == seg % 2, keep, swap(give))
        full = jnp.where(core == 0, full0, full1)
        return jnp.where(full == 0, both, both[::-1])

    live = (seg * BLK + jnp.arange(BLK))[None, :, None] < lengths[:, None, None]
    x_part = lax.dynamic_slice_in_dim(block_input, seg * BLK, BLK, axis=1)
    c_part = lax.dynamic_slice_in_dim(cotangent, seg * BLK, BLK, axis=1)
    block_output = jnp.where(live, spread(finals, 3), x_part)
    input_grad = jnp.where(live, spread(inputs, 0), c_part).astype(f32)
    return (
        block_output,
        input_grad,
        mod_w_sum[None],
        mod_b_sum[None],
        first_sum.astype(f32)[None],
        rows_sum.astype(f32)[None],
    )


def solution(mesh):
    in_specs = (
        P("dp", None, None),
        P("dp", None, None),
        P("dp"),
        P("dp"),
        P("segment", None, None),
        P("segment", None),
        P("segment", None, None),
        P("segment", None, None),
    )
    out_specs = (
        P("dp", "segment", None),
        P("dp", "segment", None),
        P("segment", "dp", None),
        P("segment", "dp"),
        P("segment", "dp", None),
        P("segment", "dp", None),
    )
    return jax.shard_map(local, mesh=mesh, in_specs=in_specs, out_specs=out_specs, check_vma=False)
```

```python
import functools
import math

import jax
import jax.numpy as jnp
import numpy as np
from jax import lax
from jax.experimental import pallas as pl
from jax.experimental.pallas import tpu as pltpu
from jax.sharding import PartitionSpec as P

D = 768
HEADS = 12
HEAD_DIM = 64
FF = 3072
SEQ_LEN = 1024
BLK = 256
HALF = SEQ_LEN // 2
MB = 4
XS, QS, AT, BR, NM, DQ, XF, BF, NF, GB = range(10)
VLIM = 56 << 20
bf16, f32, i32 = jnp.bfloat16, jnp.float32, jnp.int32


def dot(a, b):
    return lax.dot_general(a, b, (((1,), (0,)), ((), ())), preferred_element_type=f32)


def dot_nt(a, b):
    return lax.dot_general(a, b, (((1,), (1,)), ((), ())), preferred_element_type=f32)


def dot_tn(a, b):
    return lax.dot_general(a, b, (((0,), (0,)), ((), ())), preferred_element_type=f32)


def block_rows(b):
    return pl.ds(pl.multiple_of(b * BLK, BLK), BLK)


def lanes(p):
    return pl.ds(pl.multiple_of(p * 128, 128), 128)


def norm_parts(x):
    center = x - jnp.mean(x, axis=-1, keepdims=True)
    rstd = lax.rsqrt(jnp.mean(center * center, axis=-1, keepdims=True) + 1e-06)
    return center * rstd, rstd


def norm_back(d_normed, n, rstd, scl):
    dn = d_normed * scl
    return (
        dn - jnp.mean(dn, axis=-1, keepdims=True) - n * jnp.mean(dn * n, axis=-1, keepdims=True)
    ) * rstd


def turn(v, cosine, sine):
    lane = lax.broadcasted_iota(i32, v.shape, 1)
    partner = jnp.where(lane % 64 < 32, pltpu.roll(v, 96, 1), pltpu.roll(v, 32, 1))
    return v * cosine + partner * sine


def live_column(rows, c, length, first=0):
    r = lax.broadcasted_iota(i32, (rows, 1), 0) + first
    position = r + BLK * c + jnp.where(r >= BLK, BLK, 0)
    return position < length


def counts(length, c):
    nk = lax.shift_right_logical(length + (BLK - 1), 8)
    return nk, lax.shift_right_logical(nk - c + 1, 1)


class Copies:
    def __init__(self, sems):
        self.sems, self.started = sems, []

    def add(self, src, dst):
        copy = pltpu.make_async_copy(src, dst, self.sems.at[len(self.started)])
        copy.start()
        self.started.append(copy)

    def wait(self):
        for copy in self.started:
            copy.wait()


def load_shared(c, borrowed, w, wx_own, wx_oth, cols, wv, sem, into=None):
    into = cols if into is None else into
    whole = pltpu.make_async_copy(w.at[:, cols], wv.at[:, into], sem)
    pl.when(jnp.logical_not(borrowed))(lambda: whole.start())
    half = D // 2

    @pl.when(borrowed)
    def _():
        for source, at in ((wx_own, c), (wx_oth, 1 - c)):
            rows = pl.ds(pl.multiple_of(at * half, half), half)
            pltpu.make_async_copy(source.at[:, cols], wv.at[rows, into], sem).start()

    return whole


def att_f_kernel(sc, tt, own2, oth2, own3, oth3, own_x, rcv_full, rcv_short, w, wx_own, wx_oth,
                 cos, sin, mod,
                 st_i, kv_i, lse_i,
                 out, st, kv, lse,
                 xv, nv, wv, kvv, vv, qv, av, bv, ov, lv, cv, sv, sem, osem):
    role = sc[0]
    mb = tt[role]

    @pl.when(mb >= 0)
    def _():
        c, length, idx = sc[1], sc[2 + mb], sc[6 + mb]
        nk, ns = counts(length, c)
        mine = lax.rem(mb, 2) == c

        @pl.when((role == 0) & mine)
        def _():
            pltpu.make_async_copy(own_x.at[idx], xv, sem.at[0]).start()

        for pick, source in ((mb < 2, rcv_full), (mb >= 2, rcv_short)):

            @pl.when((role == 0) & jnp.logical_not(mine) & pick)
            def _():
                pltpu.make_async_copy(source, xv, sem.at[0]).start()

        for who, own, oth in ((2, own2, oth2), (3, own3, oth3)):

            @pl.when(role == who)
            def _():
                for j in range(2):
                    rows = pl.ds(j * BLK, BLK)
                    pltpu.make_async_copy(
                        own.at[rows], xv.at[block_rows(c + 2 * j)], sem.at[0]
                    ).start()
                    pltpu.make_async_copy(
                        oth.at[rows], xv.at[block_rows(1 - c + 2 * j)], sem.at[0]
                    ).start()

        wcopies = []
        for part in (1, 2, 0, 3):
            wcopies.append(
                load_shared(c, role == 3, w, wx_own, wx_oth, pl.ds(part * D, D), wv, sem.at[1 + part])
            )
        tables = [
            pltpu.make_async_copy(cos, cv, sem.at[5]),
            pltpu.make_async_copy(sin, sv, sem.at[6]),
        ]
        for copy in tables:
            copy.start()
        off, scl, gat = mod[mb, 0:1, :], 1.0 + mod[mb, 1:2, :], mod[mb, 2:3, :]
        pltpu.make_async_copy(own_x.at[0], xv, sem.at[0]).wait()

        def norm_block(b, carry):
            rows = block_rows(b)
            n, _ = norm_parts(xv[rows, :].astype(f32))
            nv[rows, :] = (n * scl + off).astype(bf16)
            return carry

        lax.fori_loop(0, nk, norm_block, 0)
        for copy in tables:
            copy.wait()
        wcopies[0].wait()
        wcopies[1].wait()

        def kv_block(b, carry):
            rows = block_rows(b)
            n = nv[rows, :]
            cosine, sine = cv[rows, :], sv[rows, :]
            kk = dot(n, wv[:, D : 2 * D])
            for p in range(6):
                ls = slice(p * 128, (p + 1) * 128)
                kvv[rows, ls] = turn(kk[:, ls], cosine, sine).astype(bf16)
            vv[rows, :] = dot(n, wv[:, 2 * D : 3 * D]).astype(bf16)
            return carry

        lax.fori_loop(0, nk, kv_block, 0)
        wcopies[2].wait()

        def q_block(j, carry):
            nat = block_rows(c + 2 * j)
            rows = block_rows(j)
            cosine, sine = cv[nat, :] * 0.125, sv[nat, :] * 0.125
            qq = dot(nv[nat, :], wv[:, 0:D])
            for p in range(6):
                ls = slice(p * 128, (p + 1) * 128)
                qv[rows, ls] = turn(qq[:, ls], cosine, sine).astype(bf16)
            return carry

        lax.fori_loop(0, ns, q_block, 0)

        lane = lax.broadcasted_iota(i32, (BLK, 128), 1)

        def clear_block(b):
            kvv[b * BLK : (b + 1) * BLK, :] = jnp.zeros((BLK, D), bf16)
            vv[b * BLK : (b + 1) * BLK, :] = jnp.zeros((BLK, D), bf16)

        def attend(keys):
            position = lax.broadcasted_iota(i32, (1, keys), 1)
            bias = jnp.where(position < length, 0.0, -1e30).astype(f32)

            def pair(i, carry):
                j, hp = lax.div(i, HEADS // 2), lax.rem(i, HEADS // 2)
                rows, ls = block_rows(j), lanes(hp)
                k2, v2, q2 = kvv[0:keys, ls], vv[0:keys, ls], qv[rows, ls]
                outs, stats = [], lv[rows, :]
                for a in range(2):
                    s = dot_nt(jnp.where((lane < 64) == (a == 0), q2, jnp.zeros_like(q2)), k2)
                    s = s + bias
                    m = jnp.max(s, axis=1, keepdims=True)
                    e = jnp.exp(s - m)
                    total = jnp.sum(e, axis=1, keepdims=True)
                    outs.append(dot(e.astype(bf16), v2) / total)
                    stats = jnp.where(lane == 2 * hp + a, m + jnp.log(total), stats)
                av[rows, ls] = jnp.where(lane < 64, outs[0], outs[1]).astype(bf16)
                lv[rows, :] = stats
                return carry

            lax.fori_loop(0, ns * (HEADS // 2), pair, 0)

        lv[...] = jnp.zeros((HALF, 128), f32)

        @pl.when(nk == 1)
        def _():
            clear_block(1)

        @pl.when(nk == 3)
        def _():
            clear_block(3)

        sends = Copies(osem)
        sends.add(qv, st.at[QS, mb])
        sends.add(kvv, kv.at[0, mb])
        sends.add(vv, kv.at[1, mb])
        for j in range(2):
            sends.add(xv.at[block_rows(c + 2 * j)], st.at[XS, mb, pl.ds(j * BLK, BLK)])
        pl.when(nk > 2)(lambda: attend(SEQ_LEN))
        pl.when(nk <= 2)(lambda: attend(HALF))
        wcopies[3].wait()

        def out_block(j, carry):
            rows = block_rows(j)
            branch = dot(av[rows, :], wv[:, 3 * D : 4 * D])
            live = live_column(BLK, c, length, j * BLK)
            x = xv[block_rows(c + 2 * j), :].astype(f32)
            ov[rows, :] = (x + jnp.where(live, gat * branch, 0.0)).astype(bf16)
            bv[rows, :] = branch.astype(bf16)
            return carry

        lax.fori_loop(0, ns, out_block, 0)
        sends.add(ov, out)
        sends.add(av, st.at[AT, mb])
        sends.add(bv, st.at[BR, mb])
        sends.add(lv, lse.at[mb])
        sends.wait()


def load_ff_weights(c, role, w1, wx_own, wx_oth, near, far, rows2, w1v, w2v, sem):
    quarter = FF // 4
    base = jnp.where(role == 2, 2, 0)

    def cols(part):
        return pl.ds(pl.multiple_of(part * quarter, quarter), quarter)

    def load_down(source, part):
        pltpu.make_async_copy(source, w2v.at[cols(part)], sem.at[4 + part]).start()

    ups = []
    for part in range(4):
        at = pl.ds(part * quarter, quarter)
        ups.append(load_shared(c, role == 2, w1, wx_own, wx_oth, at, w1v, sem.at[part]))
        if part < 2:
            load_down(rows2.at[cols(part)], 2 - base + part)
        if part == 0:
            for pick, halves in ((role == 1, near), (role != 1, far)):

                @pl.when(pick)
                def _():
                    load_down(halves[0], base + c)
                    load_down(halves[1], base + 1 - c)

    def wait(part):
        pltpu.make_async_copy(w1.at[:, cols(part)], w1v.at[:, cols(part)], sem.at[part]).wait()
        pltpu.make_async_copy(near[0], w2v.at[cols(part)], sem.at[4 + part]).wait()

    return wait


def gelu_parts(u):
    u2 = u * u
    t = jnp.tanh(0.7978845608028654 * (u * (1.0 + 0.044715 * u2)))
    return t, u2


def ff_f_kernel(sc, tt, hop, here, w1, wx_own, wx_oth, prt1_own, prt_own, prt1_oth, prt_oth, rows2,
                mod, st_i,
                out, st, xv, nv, w1v, w2v, ov, bv, accv, sem, osem):
    role = sc[0]
    mb = tt[role]

    @pl.when(mb >= 0)
    def _():
        c, length = sc[1], sc[2 + mb]
        _, ns = counts(length, c)
        load = pltpu.make_async_copy(hop, xv, sem.at[8])
        pl.when(role == 1)(lambda: load.start())
        pl.when(role != 1)(lambda: pltpu.make_async_copy(here, xv, sem.at[8]).start())
        wait = load_ff_weights(
            c, role, w1, wx_own, wx_oth, (prt1_own, prt1_oth), (prt_own, prt_oth), rows2, w1v, w2v, sem
        )
        off, scl, gat = mod[mb, 0:1, :], 1.0 + mod[mb, 1:2, :], mod[mb, 2:3, :]
        load.wait()
        sends = Copies(osem)
        sends.add(xv, st.at[XF, mb])

        def norm_block(j, carry):
            rows = block_rows(j)
            n, _ = norm_parts(xv[rows, :].astype(f32))
            nv[rows, :] = (n * scl + off).astype(bf16)
            return carry

        lax.fori_loop(0, ns, norm_block, 0)

        accv[...] = jnp.zeros((HALF, D), f32)

        def step(part, carry):
            wait(part)
            at = pl.ds(pl.multiple_of(part * D, D), D)

            def block(j, carry):
                rows = block_rows(j)
                u = dot(nv[rows, :], w1v[:, at])
                t, _ = gelu_parts(u)
                accv[rows, :] += dot((0.5 * u * (1.0 + t)).astype(bf16), w2v[at, :])
                return carry

            return lax.fori_loop(0, ns, block, carry)

        lax.fori_loop(0, 4, step, 0)

        def last(j, carry):
            rows = block_rows(j)
            acc = accv[rows, :]
            live = live_column(BLK, c, length, j * BLK)
            x = xv[rows, :].astype(f32)
            ov[rows, :] = (x + jnp.where(live, gat * acc, 0.0)).astype(bf16)
            bv[rows, :] = acc.astype(bf16)
            return carry

        lax.fori_loop(0, ns, last, 0)
        sends.add(ov, out)
        sends.add(bv, st.at[BF, mb])
        sends.wait()


def ff_b_kernel(sc, tt, hop, own_c, rcv_c, w1, wx_own, wx_oth, prt1_own, prt_own, prt1_oth, prt_oth,
                rows2, mod,
                 st_i, y_i, act_i, dm_i,
                out, st, y, act, dm,
                xv, gv, brv, nv, gbv, w1v, w2v, duv, actv, ov, dmv, accv, sem, osem):
    role = sc[0]
    mb = tt[role]

    @pl.when(mb >= 0)
    def _():
        c, length, idx = sc[1], sc[2 + mb], sc[6 + mb]
        _, ns = counts(length, c)
        mine = lax.rem(mb, 2) == c

        @pl.when(role == 1)
        def _():
            pltpu.make_async_copy(hop, gv, sem.at[8]).start()

        for pick, source in ((mine, own_c), (jnp.logical_not(mine), rcv_c)):

            @pl.when((role != 1) & pick)
            def _():
                for j in range(2):
                    pltpu.make_async_copy(
                        source.at[idx, block_rows(c + 2 * j)], gv.at[pl.ds(j * BLK, BLK)], sem.at[8]
                    ).start()

        loads = [
            pltpu.make_async_copy(st.at[XF, mb], xv, sem.at[9]),
            pltpu.make_async_copy(st.at[BF, mb], brv, sem.at[10]),
        ]
        for copy in loads:
            copy.start()
        wait = load_ff_weights(
            c, role, w1, wx_own, wx_oth, (prt1_own, prt1_oth), (prt_own, prt_oth), rows2, w1v, w2v, sem
        )
        off, scl, gat = mod[mb, 0:1, :], 1.0 + mod[mb, 1:2, :], mod[mb, 2:3, :]
        dmv[...] = jnp.zeros((8, D), f32)
        pltpu.make_async_copy(hop, gv, sem.at[8]).wait()
        for copy in loads:
            copy.wait()

        def norm_block(j, carry):
            rows = block_rows(j)
            n, _ = norm_parts(xv[rows, :].astype(f32))
            nv[rows, :] = (n * scl + off).astype(bf16)
            live = live_column(BLK, c, length, j * BLK)
            gl = jnp.where(live, gv[rows, :].astype(f32), 0.0)
            gbv[rows, :] = (gl * gat).astype(bf16)
            dmv[2:3, :] += jnp.sum(gl * brv[rows, :].astype(f32), axis=0, keepdims=True)
            return carry

        lax.fori_loop(0, ns, norm_block, 0)
        sends = Copies(osem)
        sends.add(nv, st.at[NF, mb])
        sends.add(gbv, st.at[GB, mb])

        accv[...] = jnp.zeros((HALF, D), f32)

        def step(part, carry):
            wait(part)
            cols = pl.ds(pl.multiple_of(part * D, D), D)

            def block(j, carry):
                rows = block_rows(j)
                u = dot(nv[rows, :], w1v[:, cols])
                t, u2 = gelu_parts(u)
                half = 0.5 * (1.0 + t)
                actv[rows, cols] = (u * half).astype(bf16)
                slope = half + 0.5 * u * (1.0 - t * t) * (
                    0.7978845608028654 * (1.0 + 3 * 0.044715 * u2)
                )
                du = (dot_nt(gbv[rows, :], w2v[cols, :]) * slope).astype(bf16)
                duv[rows, cols] = du
                accv[rows, :] += dot_nt(du, w1v[:, cols])
                return carry

            return lax.fori_loop(0, ns, block, carry)

        lax.fori_loop(0, 4, step, 0)

        def last(j, carry):
            rows = block_rows(j)
            acc = accv[rows, :]
            n, rstd = norm_parts(xv[rows, :].astype(f32))
            dmv[0:1, :] += jnp.sum(acc, axis=0, keepdims=True)
            dmv[1:2, :] += jnp.sum(acc * n, axis=0, keepdims=True)
            ov[rows, :] = (gv[rows, :].astype(f32) + norm_back(acc, n, rstd, scl)).astype(bf16)
            return carry

        lax.fori_loop(0, ns, last, 0)
        sends.add(ov, out)
        sends.add(duv, y.at[mb])
        sends.add(actv, act.at[mb])
        sends.add(dmv, dm.at[mb])
        sends.wait()


def att_b1_kernel(sc, tt, hop0, here2, here3, w, wx_own, wx_oth, mod, kv, lse, st_i, y_i,
                  own, snd, st, y,
                  gv, atv, qv, kvv, vv, wo, lv, gbv, dov, dqv, dkt, dvt, sem, osem):
    role = sc[0]
    mb = tt[role]

    @pl.when(mb >= 0)
    def _():
        c, length = sc[1], sc[2 + mb]
        nk, ns = counts(length, c)
        for who, hop in ((0, hop0), (2, here2), (3, here3)):
            pl.when(role == who)(lambda: pltpu.make_async_copy(hop, gv, sem.at[0]).start())
        out_weight = load_shared(
            c, role == 3, w, wx_own, wx_oth, pl.ds(3 * D, D), wo, sem.at[1], pl.ds(0, D)
        )
        loads = [
            pltpu.make_async_copy(st.at[QS, mb], qv, sem.at[2]),
            pltpu.make_async_copy(kv.at[0, mb], kvv, sem.at[3]),
            pltpu.make_async_copy(kv.at[1, mb], vv, sem.at[4]),
            pltpu.make_async_copy(st.at[AT, mb], atv, sem.at[5]),
            pltpu.make_async_copy(lse.at[mb], lv, sem.at[6]),
        ]
        for copy in loads:
            copy.start()
        gat = mod[mb, 2:3, :]
        pltpu.make_async_copy(hop0, gv, sem.at[0]).wait()
        out_weight.wait()

        def grad_block(j, carry):
            rows = block_rows(j)
            live = live_column(BLK, c, length, j * BLK)
            gb = jnp.where(live, gv[rows, :].astype(f32) * gat, 0.0).astype(bf16)
            gbv[rows, :] = gb
            dov[rows, :] = dot_nt(gb, wo[...]).astype(bf16)
            return carry

        lax.fori_loop(0, ns, grad_block, 0)
        sends = Copies(osem)
        sends.add(gbv, y.at[mb, :, pl.ds(3 * D, D)])
        for copy in loads:
            copy.wait()

        def attend(rows, keys):
            lane = lax.broadcasted_iota(i32, (rows, 128), 1)
            position = lax.broadcasted_iota(i32, (1, keys), 1)
            bias = jnp.where(position < length, 0.0, -1e30).astype(f32)

            def pair(hp, carry):
                ls = lanes(hp)
                k2, v2 = kvv[0:keys, ls], vv[0:keys, ls]
                q2, do2 = qv[0:rows, ls], dov[0:rows, ls]
                q2t, do2t = q2.T, do2.T
                both = do2.astype(f32) * atv[0:rows, ls].astype(f32)
                stats = lv[0:rows, :]
                dqs = []
                for a in range(2):
                    head = (lane < 64) == (a == 0)
                    zero = jnp.zeros_like(q2)
                    s = dot_nt(jnp.where(head, q2, zero), k2) + bias
                    base = jnp.sum(jnp.where(lane == 2 * hp + a, stats, 0.0), axis=1, keepdims=True)
                    p = jnp.exp(s - base)
                    dp = dot_nt(jnp.where(head, do2, zero), v2)
                    delta = jnp.sum(jnp.where(head, both, 0.0), axis=1, keepdims=True)
                    ds = (p * (dp - delta)).astype(bf16)
                    dqs.append(dot(ds, k2))
                    at = pl.ds(pl.multiple_of(hp * 128 + a * 64, 64), 64)
                    dkt[at, 0:keys] = dot(q2t[a * 64 : (a + 1) * 64, :], ds).astype(bf16)
                    dvt[at, 0:keys] = dot(do2t[a * 64 : (a + 1) * 64, :], p.astype(bf16)).astype(
                        bf16
                    )
                dqv[0:rows, ls] = jnp.where(lane < 64, dqs[0], dqs[1]).astype(bf16)
                return carry

            lax.fori_loop(0, HEADS // 2, pair, 0)

        @pl.when((ns == 1) & (nk > 2))
        def _():
            zero = jnp.zeros((BLK, D), bf16)
            qv[BLK:HALF, :], atv[BLK:HALF, :], dov[BLK:HALF, :] = zero, zero, zero
            lv[BLK:HALF, :] = jnp.zeros((BLK, 128), f32)

        pl.when(nk > 2)(lambda: attend(HALF, SEQ_LEN))
        pl.when((ns == 1) & (nk <= 2))(lambda: attend(BLK, HALF))

        @pl.when(ns == 0)
        def _():
            dkt[:, 0:BLK] = jnp.zeros((D, BLK), bf16)
            dvt[:, 0:BLK] = jnp.zeros((D, BLK), bf16)

        sends.add(dqv, st.at[DQ, mb])
        for part, grad in enumerate((dkt, dvt)):
            for j in range(2):
                cols = pl.ds(j * BLK, BLK)
                sends.add(grad.at[:, block_rows(c + 2 * j)], own.at[part, :, cols])
                sends.add(grad.at[:, block_rows(1 - c + 2 * j)], snd.at[part, :, cols])
        sends.wait()


def att_b2_kernel(sc, tt, hop0, here2, here3, own, rcv0, rcv2, rcv3, w, wx_own, wx_oth, cos, sin, mod, st_i, y_i, dm_i,
                  out, st, y, dm,
                  gv, xv, brv, dqv, ownv, rcvv, wv, cv, sv, nv, dpv, ov, dmv, sem, osem):
    role = sc[0]
    mb = tt[role]

    @pl.when(mb >= 0)
    def _():
        c, length = sc[1], sc[2 + mb]
        _, ns = counts(length, c)
        for who, hop, rcv in ((0, hop0, rcv0), (2, here2, rcv2), (3, here3, rcv3)):

            @pl.when(role == who)
            def _():
                pltpu.make_async_copy(hop, gv, sem.at[0]).start()
                pltpu.make_async_copy(rcv, rcvv, sem.at[2]).start()

        loads = [
            pltpu.make_async_copy(own, ownv, sem.at[1]),
            pltpu.make_async_copy(st.at[DQ, mb], dqv, sem.at[3]),
            pltpu.make_async_copy(st.at[XS, mb], xv, sem.at[4]),
            pltpu.make_async_copy(st.at[BR, mb], brv, sem.at[5]),
            pltpu.make_async_copy(cos, cv, sem.at[6]),
            pltpu.make_async_copy(sin, sv, sem.at[7]),
        ]
        for copy in loads:
            copy.start()
        in_weight = load_shared(c, role == 3, w, wx_own, wx_oth, pl.ds(0, 3 * D), wv, sem.at[8])
        off, scl = mod[mb, 0:1, :], 1.0 + mod[mb, 1:2, :]
        dmv[...] = jnp.zeros((8, D), f32)
        pltpu.make_async_copy(hop0, gv, sem.at[0]).wait()
        pltpu.make_async_copy(rcv0, rcvv, sem.at[2]).wait()
        for copy in loads:
            copy.wait()

        def first(j, carry):
            rows, nat = block_rows(j), block_rows(c + 2 * j)
            cosine, sine = cv[nat, :], -sv[nat, :]
            for p in range(6):
                ls = slice(p * 128, (p + 1) * 128)
                dpv[rows, ls] = (turn(dqv[rows, ls].astype(f32), cosine, sine) * 0.125).astype(bf16)
                for part in range(2):
                    total = ownv[part, ls, rows].astype(f32) + rcvv[part, ls, rows].astype(f32)
                    grad = total.T
                    if part == 0:
                        grad = turn(grad.astype(bf16).astype(f32), cosine, sine)
                    dpv[rows, (part + 1) * D + p * 128 : (part + 1) * D + (p + 1) * 128] = (
                        grad.astype(bf16)
                    )
            return carry

        lax.fori_loop(0, ns, first, 0)
        sends = Copies(osem)
        sends.add(dpv, y.at[mb, :, pl.ds(0, 3 * D)])
        in_weight.wait()

        def second(j, carry):
            rows = block_rows(j)
            acc = dot_nt(dpv[rows, :], wv[...])
            n, rstd = norm_parts(xv[rows, :].astype(f32))
            nv[rows, :] = (n * scl + off).astype(bf16)
            g = gv[rows, :].astype(f32)
            live = live_column(BLK, c, length, j * BLK)
            gl = jnp.where(live, g, 0.0)
            dmv[0:1, :] += jnp.sum(acc, axis=0, keepdims=True)
            dmv[1:2, :] += jnp.sum(acc * n, axis=0, keepdims=True)
            dmv[2:3, :] += jnp.sum(gl * brv[rows, :].astype(f32), axis=0, keepdims=True)
            ov[rows, :] = (g + norm_back(acc, n, rstd, scl)).astype(bf16)
            return carry

        lax.fori_loop(0, ns, second, 0)
        sends.add(ov, out)
        sends.add(nv, st.at[NM, mb])
        sends.add(dmv, dm.at[mb])
        sends.wait()


def weight_grad_kernel(kind, sc, tt, st, y, out, xv, xt, yv, acc, ov, xsem, ysem, osem):
    chosen, c = tt[sc[0]], sc[1]

    def tile(j):
        return y.at[:, :, pl.ds(pl.multiple_of(j * D, D), D)]

    def into(j):
        at = pl.ds(pl.multiple_of(j * D, D), D)
        return out.at[at] if kind == "down" else out.at[:, at]

    def load_x(which):
        return pltpu.make_async_copy(st.at[which], xv, xsem.at[0])

    def load_y(j):
        slot = lax.rem(j, 2)
        return pltpu.make_async_copy(tile(j), yv.at[slot], ysem.at[slot])

    def store(j):
        slot = lax.rem(j, 2)
        return pltpu.make_async_copy(ov.at[slot], into(j), osem.at[slot])

    def live(mb):
        _, ns = counts(sc[2 + mb], c)
        picked = lax.rem(lax.shift_right_logical(chosen, mb), 2) == 1
        return jnp.where(picked, ns, 0)

    def transpose_rows(x):
        def step(mb, carry):
            def block(j, carry):
                xt[:, block_rows(2 * mb + j)] = x[mb, block_rows(j), :].T
                return carry

            return lax.fori_loop(0, live(mb), block, carry)

        lax.fori_loop(0, MB, step, 0)

    @pl.when(chosen > 0)
    def _():
        first = GB if kind == "down" else NM if kind == "attention" else NF
        load_x(first).start()
        load_y(0).start()
        load_x(first).wait()
        if kind != "down":
            transpose_rows(xv)
        if kind == "attention":
            load_x(AT).start()

        def step(j, carry):
            slot = lax.rem(j, 2)
            pl.when(j < 3)(lambda: load_y(j + 1).start())
            load_y(j).wait()
            if kind == "down":
                transpose_rows(yv.at[slot])
            if kind == "attention":

                @pl.when(j == 3)
                def _():
                    load_x(AT).wait()
                    transpose_rows(xv)

            acc[...] = jnp.zeros((D, D), f32)

            def add(mb, carry):
                for slots in (1, 2):

                    @pl.when(live(mb) == slots)
                    def _():
                        at = pl.ds(pl.multiple_of(mb * HALF, HALF), slots * BLK)
                        if kind == "down":
                            right = xv[mb, 0 : slots * BLK, :]
                        else:
                            right = yv[slot, mb, 0 : slots * BLK, :]
                        acc[...] += dot(xt[:, at], right)

                return carry

            lax.fori_loop(0, MB, add, 0)
            pl.when(j >= 2)(lambda: store(j - 2).wait())
            ov[slot] = acc[...].astype(bf16)
            store(j).start()
            return carry

        lax.fori_loop(0, 4, step, 0)
        store(2).wait()
        store(3).wait()


def reduce_kernel(roles, chips, mine, theirs, *refs):
    count, kept = len(mine[0]) + len(theirs[0]), len(mine[0])
    arrays, outs = refs[:count], refs[count : count + kept]
    near, total = refs[count + kept : 2 * count + kept], refs[2 * count + kept : 3 * count + kept]
    refs = refs[3 * count + kept :]
    paired = len(theirs[0]) > 0
    cross, refs = (refs[:kept], refs[kept:]) if paired else ((), refs)
    gathered, result, refs = refs[:kept], refs[kept : 2 * kept], refs[2 * kept :]
    load_sem, near_send, near_recv, cross_send, cross_recv, far_send, far_recv, out_sem = refs
    seg, dp = lax.axis_index("segment"), lax.axis_index("dp")
    core, place = lax.rem(dp, 2), lax.div(dp, 2)

    def device(segment, chip, at):
        return {"segment": segment, "dp": 2 * chip + at}

    def remote(src, dst, send, recv, target):
        return pltpu.make_async_remote_copy(
            src_ref=src, dst_ref=dst, send_sem=send, recv_sem=recv,
            device_id=target, device_id_type=pl.DeviceIdType.MESH,
        )

    def work(role, other, keep, give):
        barrier = pltpu.get_barrier_semaphore()
        peers = [device(role, place, 1 - core)]
        peers += [device(role, lax.rem(place + k, chips), core) for k in range(1, chips)]
        if paired:
            peers.append(device(other, place, core))
        for peer in peers:
            pl.semaphore_signal(
                barrier, inc=1, device_id=peer, device_id_type=pl.DeviceIdType.MESH
            )
        pl.semaphore_wait(barrier, len(peers))

        order = [lax.rem(place + k, chips) for k in range(1, chips)] + [place]
        nears, loads = [], []
        for z in range(chips):
            for k, at in enumerate(keep + give):
                to = remote(
                    arrays[at].at[2 * z + 1 - core], near[k].at[z],
                    near_send.at[k, z], near_recv.at[k, z], device(role, place, 1 - core),
                )
                to.start()
                nears.append(to)
                load = pltpu.make_async_copy(
                    arrays[at].at[2 * z + core], total[k].at[z], load_sem.at[k, z]
                )
                load.start()
                loads.append(load)
        crossing = []
        for z in range(chips):
            for k in list(range(kept, count)) + list(range(kept)):
                loads[z * count + k].wait()
                nears[z * count + k].wait()
                total[k][z] = total[k][z] + near[k][z]
                if k >= kept:
                    to = remote(
                        total[k].at[z], cross[k - kept].at[z],
                        cross_send.at[k - kept, z], cross_recv.at[k - kept, z],
                        device(other, place, core),
                    )
                    to.start()
                    crossing.append(to)
        far = []
        for z in range(chips):
            for k in range(kept):
                if paired:
                    crossing[z * kept + k].wait()
                    total[k][z] = total[k][z] + cross[k][z]
                far.append(
                    remote(
                        total[k].at[z], gathered[k].at[place],
                        far_send.at[k, z], far_recv.at[k, place], device(role, z, core),
                    )
                )
                pl.when(place != z)(far[-1].start)
        for k in range(kept):
            result[k][...] = total[k][place].astype(f32)
        for z in order[:-1]:
            for k in range(kept):
                remote(
                    total[k].at[z], gathered[k].at[z],
                    far_send.at[k, z], far_recv.at[k, z], device(role, z, core),
                ).wait_recv()
                result[k][...] += gathered[k][z].astype(f32)
        copies = []
        for k in range(kept):
            copies.append(pltpu.make_async_copy(result[k], outs[k], out_sem.at[k]))
            copies[-1].start()
        for z in range(chips):
            for k in range(kept):
                pl.when(place != z)(far[z * kept + k].wait_send)
        for copy in copies:
            copy.wait()

    for index, role in enumerate(roles):
        other = roles[1 - index] if paired else role
        pl.when(seg == role)(functools.partial(work, role, other, mine[index], theirs[index]))


def gather_kernel(size, rows, out, own_sem, send, recv):
    seg, dp = lax.axis_index("segment"), lax.axis_index("dp")

    def peer(k):
        return {"segment": seg, "dp": lax.rem(dp + k, size)}

    barrier = pltpu.get_barrier_semaphore()
    for k in range(1, size):
        pl.semaphore_signal(
            barrier, inc=1, device_id=peer(k), device_id_type=pl.DeviceIdType.MESH
        )
    pl.semaphore_wait(barrier, size - 1)
    own = pltpu.make_async_copy(rows, out.at[dp], own_sem)
    own.start()

    def copy(k, slot):
        return pltpu.make_async_remote_copy(
            src_ref=rows, dst_ref=out.at[slot], send_sem=send.at[k], recv_sem=recv.at[slot],
            device_id=peer(k), device_id_type=pl.DeviceIdType.MESH,
        )

    for k in range(1, size):
        copy(k, dp).start()
    own.wait()
    for k in range(1, size):
        copy(k, dp).wait_send()
        copy(k, lax.rem(dp + k, size)).wait_recv()


def gathered_rows(rows, size, number):
    return pl.pallas_call(
        functools.partial(gather_kernel, size),
        out_shape=jax.ShapeDtypeStruct((size, *rows.shape), rows.dtype),
        in_specs=[VMEM],
        out_specs=VMEM,
        scratch_shapes=[
            pltpu.SemaphoreType.DMA,
            pltpu.SemaphoreType.DMA((size,)),
            pltpu.SemaphoreType.DMA((size,)),
        ],
        compiler_params=pltpu.CompilerParams(
            vmem_limit_bytes=VLIM, collective_id=number, has_side_effects=True
        ),
        name="gather_sums",
    )(rows)


def reduced(arrays, roles, mine, theirs, chips, number, name):
    dims = [a.shape[1:] for a in arrays]
    kept, count = len(mine[0]), len(mine[0]) + len(theirs[0])
    order = mine[0] + theirs[0]
    every = [vm((chips, *dims[k])) for k in order]
    keeps = [vm((chips, *dims[k])) for k in mine[0]]
    pairs = pltpu.SemaphoreType.DMA((count, chips))
    return pl.pallas_call(
        functools.partial(reduce_kernel, roles, chips, mine, theirs),
        out_shape=[jax.ShapeDtypeStruct(dims[k], f32) for k in mine[0]],
        in_specs=[ANY] * len(arrays),
        out_specs=[ANY] * kept,
        scratch_shapes=every + every + (keeps if theirs[0] else []) + keeps
        + [vm(dims[k], f32) for k in mine[0]]
        + [pairs] * 7 + [pltpu.SemaphoreType.DMA((kept,))],
        compiler_params=pltpu.CompilerParams(
            vmem_limit_bytes=VLIM, collective_id=number, has_side_effects=True
        ),
        cost_estimate=cost(60),
        name=name,
    )(*arrays)


ANY = pl.BlockSpec(memory_space=pl.ANY)
VMEM = pl.BlockSpec(memory_space=pltpu.VMEM)


def shape(dims, dtype=bf16):
    return jax.ShapeDtypeStruct(dims, dtype)


ROWS = shape((HALF, D))
ST = shape((10, MB, HALF, D))
KV = shape((2, MB, SEQ_LEN, D))
LSE = shape((MB, HALF, 128), f32)
YS = shape((MB, HALF, FF))
DM = shape((MB, 8, D), f32)
DKV = shape((2, D, HALF))


def vm(dims, dtype=bf16):
    return pltpu.VMEM(dims, dtype)


HV, FV = vm((HALF, D)), vm((SEQ_LEN, D))


def cost(micros):
    return pl.CostEstimate(flops=int(micros * 1e9), bytes_accessed=1 << 20, transcendentals=0)


def call(kernel, scalars, operands, vmem_at, outs, aliases, scratch, sems, name, micros):
    specs = [VMEM if i in vmem_at else ANY for i in range(len(operands))]
    return pl.pallas_call(
        kernel,
        grid_spec=pltpu.PrefetchScalarGridSpec(
            num_scalar_prefetch=2,
            grid=(1,),
            in_specs=specs,
            out_specs=[ANY] * len(outs),
            scratch_shapes=list(scratch)
            + [pltpu.SemaphoreType.DMA((11,)), pltpu.SemaphoreType.DMA((sems,))],
        ),
        out_shape=list(outs),
        input_output_aliases={i + 2: o for i, o in aliases.items()},
        compiler_params=pltpu.CompilerParams(vmem_limit_bytes=VLIM),
        cost_estimate=cost(micros),
        name=name,
    )(*scalars, *operands)


def allocate(outs):
    return pl.pallas_call(
        lambda *refs: None,
        out_shape=list(outs),
        out_specs=[ANY] * len(outs),
        name="allocate",
    )()


def time_cond(steps):
    half_width = D // 2
    frequency = jnp.exp(
        jnp.arange(half_width, dtype=f32) * (-math.log(10000.0) / half_width)
    )
    angles = steps.astype(f32)[:, None] * frequency[None, :]
    return jax.nn.silu(jnp.concatenate([jnp.cos(angles), jnp.sin(angles)], axis=1))


def rope_tables():
    inverse = np.exp(np.arange(32, dtype=np.float32) * np.float32(-math.log(10000.0) / 32))
    angles = np.arange(SEQ_LEN, dtype=np.float32)[:, None] * inverse[None, :]
    cosine, sine = np.cos(angles), np.sin(angles)
    return (
        np.concatenate([cosine] * 4, axis=1).astype(np.float32),
        np.concatenate([-sine, sine, -sine, sine], axis=1).astype(np.float32),
    )


def local(block_input, cotangent, lengths, steps, mod_weight, mod_bias, first_weight, down_rows):
    ndp = lax.axis_size("dp")
    seg, dp = lax.axis_index("segment"), lax.axis_index("dp")
    core, chips, place = dp % 2, ndp // 2, dp // 2
    w, rows2 = first_weight[0], down_rows[0]

    def across(value, moves):
        pairs = [
            (r * ndp + 2 * i + c, q * ndp + 2 * i + e) for (r, c), (q, e) in moves for i in range(chips)
        ]
        return lax.ppermute(value, ("segment", "dp"), pairs)

    def swap(value, roles=(0, 1, 2, 3)):
        return across(value, [((r, c), (r, 1 - c)) for r in roles for c in range(2)])

    def hop(value, pairs):
        return lax.ppermute(value, "segment", pairs)

    def after(value, other):
        return lax.optimization_barrier((value, other))[0]

    quarter = FF // 4
    rows_half = lax.dynamic_slice_in_dim(rows2, core * quarter, quarter, axis=0)
    prt1 = hop(rows_half, [(0, 1)])
    full = (lengths[1] > lengths[0]).astype(i32)
    block_input = after(block_input, rows_half)
    other_info = swap(jnp.stack([lengths, steps]))
    other_full = swap(lax.dynamic_index_in_dim(block_input, full, keepdims=False), (0,))
    info = jnp.stack([lengths, steps])
    info0 = jnp.where(core == 0, info, other_info)
    info1 = jnp.where(core == 0, other_info, info)
    full0 = (info0[0, 1] > info0[0, 0]).astype(i32)
    full1 = (info1[0, 1] > info1[0, 0]).astype(i32)
    places = jnp.stack([full0, full1, 1 - full0, 1 - full1])
    chip = jnp.stack([info0[:, full0], info1[:, full1], info0[:, 1 - full0], info1[:, 1 - full1]])
    sc = jnp.concatenate([jnp.stack([seg, core]), chip[:, 0], places, jnp.zeros((6,), i32)]).astype(i32)
    conditions = time_cond(chip[:, 1]).astype(bf16)
    modulation = jnp.dot(conditions, mod_weight[0], preferred_element_type=f32)
    modulation = modulation + mod_bias[0].astype(f32)
    mod = jnp.pad(modulation.reshape(MB, 3, D), ((0, 0), (0, 5), (0, 0)))
    cos, sin = (jnp.asarray(t) for t in rope_tables())
    st, kv, lse, y, yf, act, dma, dmf, blank = allocate([ST, KV, LSE, YS, YS, YS, DM, DM, ROWS])

    w_half = lax.dynamic_slice_in_dim(after(w, rows_half), core * (D // 2), D // 2, axis=0)
    prt23 = hop(rows_half, [(2, 3), (3, 2)])
    wx_own = hop(w_half, [(2, 3), (3, 2)])
    prt_own = (prt1, prt23)
    wx_oth, prt_oth = wx_own, prt_own
    other_full = after(other_full, prt1)

    other_mod = hop(mod, [(2, 3), (3, 2)])
    mod_att = jnp.where(seg == 3, other_mod, mod)
    mod_ff = jnp.where(seg == 2, other_mod, mod)

    def table(turns):
        return np.array([turns.get(r, -1) for r in range(4)], np.int32)

    def att_f(turns, from2, from3, short, st, kv, lse):
        return call(
            att_f_kernel,
            (sc, table(turns)),
            (*from2, *from3, block_input, other_full, short, w, wx_own, wx_oth, cos, sin, mod_att,
             st, kv, lse),
            (12,),
            (ROWS, ST, KV, LSE),
            {13: 1, 14: 2, 15: 3},
            (FV, FV, vm((D, FF)), FV, FV, HV, HV, HV, HV, vm((HALF, 128), f32),
             vm((SEQ_LEN, 128), f32), vm((SEQ_LEN, 128), f32)),
            9,
            "attention_forward",
            20,
        )

    def ff_f(turns, x, here, st):
        return call(
            ff_f_kernel,
            (sc, table(turns)),
            (x, here, w, wx_own, wx_oth, *prt_own, *prt_oth, rows2, mod_ff, st),
            (10,),
            (ROWS, ST),
            {11: 1},
            (HV, HV, vm((D, FF)), vm((FF, D)), HV, HV, vm((HALF, D), f32)),
            3,
            "feedforward_forward",
            10,
        )

    def ff_b(turns, g, st, yf, act, dm):
        return call(
            ff_b_kernel,
            (sc, table(turns)),
            (g, cotangent, other_c, w, wx_own, wx_oth, *prt_own, *prt_oth, rows2, mod_ff, st, yf, act,
             dm),
            (11,),
            (ROWS, ST, YS, YS, DM),
            {12: 1, 13: 2, 14: 3, 15: 4},
            (HV, HV, HV, HV, HV, vm((D, FF)), vm((FF, D)), vm((HALF, FF)), vm((HALF, FF)), HV,
             vm((8, D), f32), vm((HALF, D), f32)),
            6,
            "feedforward_backward",
            16,
        )

    def att_b(turns, g0, g2, g3, st, y, dm):
        own, snd, st, y = call(
            att_b1_kernel,
            (sc, table(turns)),
            (g0, g2, g3, w, wx_own, wx_oth, mod_att, kv, lse, st, y),
            (6,),
            (DKV, DKV, ST, YS),
            {9: 2, 10: 3},
            (HV, HV, HV, FV, FV, vm((D, D)), vm((HALF, 128), f32), HV, HV, HV,
             vm((D, SEQ_LEN)), vm((D, SEQ_LEN))),
            10,
            "attention_backward",
            22,
        )
        near = swap(snd, (0,)) if 0 in turns else snd
        far = [swap(snd, (r,)) if r in turns else snd for r in (2, 3)]
        return call(
            att_b2_kernel,
            (sc, table(turns)),
            (g0, g2, g3, own, near, *far, w, wx_own, wx_oth, cos, sin, mod_att, st, y, dm),
            (12,),
            (ROWS, ST, YS, DM),
            {13: 1, 14: 2, 15: 3},
            (HV, HV, HV, HV, vm((2, D, HALF)), vm((2, D, HALF)), vm((D, 3 * D)),
             vm((SEQ_LEN, 128), f32), vm((SEQ_LEN, 128), f32), HV, vm((HALF, 3 * D)), HV,
             vm((8, D), f32)),
            4,
            "projection_backward",
            9,
        )

    depth, wide_rows = D // ndp, FF // 2 // ndp

    def weight_grad(kind, chosen, right):
        turns = np.array([chosen.get(r, 0) for r in range(4)], np.int32)
        pairs = pltpu.SemaphoreType.DMA((2,))
        return pl.pallas_call(
            functools.partial(weight_grad_kernel, kind),
            grid_spec=pltpu.PrefetchScalarGridSpec(
                num_scalar_prefetch=2,
                grid=(1,),
                in_specs=[ANY, ANY],
                out_specs=ANY,
                scratch_shapes=[
                    vm((MB, HALF, D)), vm((D, MB * HALF)), vm((2, MB, HALF, D)), vm((D, D), f32),
                    vm((2, D, D)), pairs, pairs, pairs,
                ],
            ),
            out_shape=shape((FF, D) if kind == "down" else (D, FF)),
            compiler_params=pltpu.CompilerParams(vmem_limit_bytes=VLIM),
            cost_estimate=cost(12),
            name=kind + "_gradient",
        )(sc, turns, st, right)

    def ff_grads(chosen):
        up = weight_grad("up", chosen, yf)
        down = weight_grad("down", chosen, act).reshape(2 * ndp, wide_rows, D)
        return up.reshape(ndp, depth, FF), down[:ndp], down[ndp:]

    def owned(ac, bd):
        keep = jnp.where(core == 0, ac, bd)
        give = jnp.where(core == 0, bd, ac)
        return jnp.where(core == seg % 2, keep, swap(give))

    def spread_last(one, two):
        first_one = across(one[:BLK], [((2, c), (c, c)) for c in range(2)])
        first_two = across(two[:BLK], [((3, c), (c, c)) for c in range(2)])
        mid = jnp.where(seg == 2, one[BLK:], two[BLK:])
        crossed = across(mid, [((2, 1), (3, 1)), ((3, 0), (2, 0))])
        return owned(
            jnp.where(seg < 2, first_one, jnp.where(seg == 2, mid, crossed)),
            jnp.where(seg < 2, first_two, jnp.where(seg == 2, crossed, mid)),
        )

    nothing = (blank, blank)
    a, b, cc, d = range(MB)

    out, st, kv, lse = att_f({0: a}, nothing, nothing, other_full, st, kv, lse)
    hop_a = hop(out, [(0, 1)])
    short = swap(lax.dynamic_index_in_dim(after(block_input, out), 1 - full, keepdims=False), (0,))
    other_c = swap(after(cotangent, out), (2, 3))
    prt_oth = (swap(after(prt1, out), (1,)), prt23)

    out, st, kv, lse = att_f({0: b}, nothing, nothing, other_full, st, kv, lse)
    ff_a, st = ff_f({1: a}, hop_a, blank, st)
    to_a = hop(ff_a, [(1, 2)])
    hop_b = hop(after(out, ff_a), [(0, 1)])
    wx_oth = swap(after(wx_own, ff_a), (2, 3))
    prt_oth = (prt_oth[0], swap(after(prt23, ff_a), (2, 3)))
    short = after(short, hop_b)

    att_a, st, kv, lse = att_f({0: cc, 2: a}, (to_a, swap(to_a, (2,))), nothing, short, st, kv, lse)
    ff_b1, st = ff_f({1: b}, hop_b, blank, st)
    to_b = hop(ff_b1, [(1, 3)])
    hop_c = hop(after(att_a, ff_b1), [(0, 1)])

    att_bb, st, kv, lse = att_f({0: d, 3: b}, nothing, (to_b, swap(to_b, (3,))), short, st, kv, lse)
    out_a, st = ff_f({1: cc, 2: a}, hop_c, att_a, st)
    hop_d = hop(after(att_bb, out_a), [(0, 1)])
    grad_a, st, yf, act, dmf = ff_b({2: a}, blank, st, yf, act, dmf)
    out_b, st = ff_f({1: d, 3: b}, hop_d, att_bb, st)
    to_c = hop(after(out_a, out_b), [(1, 2)])
    grad_b, st, yf, act, dmf = ff_b({3: b}, blank, st, yf, act, dmf)
    to_d = hop(after(out_b, grad_b), [(1, 3)])

    early = spread_last(after(out_a, grad_b), out_b)

    masks = {2: 5, 3: 10}
    back, st, y, dma = att_b({2: a, 3: b}, blank, grad_a, grad_b, st, y, dma)
    back_a = hop(back, [(2, 1)])
    to_c = hop(after(out_a, back), [(1, 2)])
    grad_1a, st, yf, act, dmf = ff_b({1: a}, back_a, st, yf, act, dmf)
    end_a = hop(grad_1a, [(1, 0)])
    back_b = hop(after(back, grad_1a), [(3, 1)])
    to_d = hop(after(out_b, grad_1a), [(1, 3)])
    att_cd, st, kv, lse = att_f(
        {2: cc, 3: d}, (to_c, swap(to_c, (2,))), (to_d, swap(to_d, (3,))), short, st, kv, lse
    )
    out_cd, st = ff_f({2: cc, 3: d}, blank, att_cd, st)
    grad_cd, st, yf, act, dmf = ff_b({1: b, 2: cc, 3: d}, back_b, st, yf, act, dmf)
    end_b = hop(grad_cd, [(1, 0)])
    back, st, y, dma = att_b({0: a, 2: cc, 3: d}, end_a, grad_cd, grad_cd, st, y, dma)
    in_a = back
    back_c = hop(back, [(2, 1)])
    grad_1c, st, yf, act, dmf = ff_b({1: cc}, after(back_c, end_b), st, yf, act, dmf)
    end_c = hop(grad_1c, [(1, 0)])
    back_d = hop(after(back, grad_1c), [(3, 1)])
    grad_1d, st, yf, act, dmf = ff_b({1: d}, after(back_d, end_c), st, yf, act, dmf)
    end_d = hop(grad_1d, [(1, 0)])
    att_23 = weight_grad("attention", masks, y).reshape(ndp, depth, FF)
    up_x, low_x, high_x = ff_grads({1: 15, **masks})
    in_b, st, y, dma = att_b({0: b}, end_b, blank, blank, st, y, dma)
    in_c, st, y, dma = att_b({0: cc}, end_c, blank, blank, st, y, dma)
    in_d, st, y, dma = att_b({0: d}, end_d, blank, blank, st, y, dma)
    att_23, up_x, low_x, high_x, _ = lax.optimization_barrier((att_23, up_x, low_x, high_x, in_d))
    first_23, rows_23 = reduced(
        (att_23, up_x, low_x, high_x), (2, 3), ([0, 2], [1, 3]), ([1, 3], [0, 2]), chips, 1,
        "second_layer_sums",
    )
    up_1, low_1, high_1 = reduced(
        (up_x, low_x, high_x), (1,), ([0, 1, 2],), ([],), chips, 2, "feedforward_sums"
    )
    st, _ = lax.optimization_barrier((st, (first_23, up_1)))
    att_0 = weight_grad("attention", {0: 15}, y).reshape(ndp, depth, FF)
    (first_0,) = reduced((att_0,), (0,), ([0],), ([],), chips, 3, "attention_sums")
    low_0 = hop(after(low_1, first_0), [(1, 0)])
    even = seg % 2 == 0
    first_sum = jnp.where(seg == 0, first_0, jnp.where(seg == 1, up_1, first_23))
    rows_sum = jnp.where(seg == 0, low_0, jnp.where(seg == 1, high_1, rows_23))

    late = spread_last(after(out_cd, up_1), out_cd)
    outs = jnp.stack([early, late])
    halves = after(jnp.stack([in_a, in_c, in_b, in_d]), up_1)
    to_one = across(halves[:, :BLK], [((0, 1), (1, 1))])
    to_others = across(halves[:, BLK:], [((0, 0), (2, 0)), ((0, 1), (3, 1))])
    got = jnp.where(seg == 0, halves[:, :BLK], jnp.where(seg == 1, to_one, to_others))
    grads = owned(got[:2], got[2:])

    mine = np.array([[True] * 4, [True] * 4, [True, False] * 2, [False, True] * 2])
    mine = jnp.asarray(mine)[seg][:, None, None]
    dma, dmf = (jnp.where(mine, m[:, :3], 0.0) for m in (dma, dmf))
    sums = jnp.where(even, dma, dmf) + hop(jnp.where(even, dmf, dma), [(2, 3), (3, 2)])
    mod_rows = jnp.concatenate([sums.reshape(MB, 3 * D), conditions.astype(f32)], axis=1)
    all_rows = gathered_rows(mod_rows.reshape(-1, 128), ndp, 4).reshape(ndp * MB, 4 * D)
    mine = lax.dynamic_slice_in_dim(all_rows, 3 * D + dp * depth, depth, axis=1)
    all_rows = all_rows[:, : 3 * D]
    mod_w_sum = jnp.dot(mine.T, all_rows, precision=lax.Precision.HIGHEST, preferred_element_type=f32)
    width = 3 * D // ndp
    mod_b_sum = jnp.sum(lax.dynamic_slice_in_dim(all_rows, dp * width, width, axis=1), axis=0)

    def placed(both, part):
        both = jnp.where(full == 0, both, both[::-1])
        live = (seg * BLK + jnp.arange(BLK))[None, :, None] < lengths[:, None, None]
        return jnp.where(live, both, lax.dynamic_slice_in_dim(part, seg * BLK, BLK, axis=1))

    return (
        placed(outs, block_input),
        placed(grads, cotangent).astype(f32),
        mod_w_sum[None],
        mod_b_sum[None],
        first_sum.astype(f32)[None],
        rows_sum.astype(f32)[None],
    )


def solution(mesh):
    in_specs = (
        P("dp", None, None),
        P("dp", None, None),
        P("dp"),
        P("dp"),
        P("segment", None, None),
        P("segment", None),
        P("segment", None, None),
        P("segment", None, None),
    )
    out_specs = (
        P("dp", "segment", None),
        P("dp", "segment", None),
        P("segment", "dp", None),
        P("segment", "dp"),
        P("segment", "dp", None),
        P("segment", "dp", None),
    )
    return jax.shard_map(local, mesh=mesh, in_specs=in_specs, out_specs=out_specs, check_vma=False)
```

```python
import functools
import math

import jax
import jax.numpy as jnp
import numpy as np
from jax import lax
from jax.experimental import pallas as pl
from jax.experimental.pallas import tpu as pltpu
from jax.sharding import PartitionSpec as P

D = 768
HEADS = 12
HEAD_DIM = 64
FF = 3072
SEQ_LEN = 1024
BLK = 256
HALF = SEQ_LEN // 2
MB = 4
XS, QS, AT, BR, NM, DQ, XF, BF, NF, GB = range(10)
VLIM = 56 << 20
bf16, f32, i32 = jnp.bfloat16, jnp.float32, jnp.int32


def dot(a, b):
    return lax.dot_general(a, b, (((1,), (0,)), ((), ())), preferred_element_type=f32)


def dot_nt(a, b):
    return lax.dot_general(a, b, (((1,), (1,)), ((), ())), preferred_element_type=f32)


def dot_tn(a, b):
    return lax.dot_general(a, b, (((0,), (0,)), ((), ())), preferred_element_type=f32)


def block_rows(b):
    return pl.ds(pl.multiple_of(b * BLK, BLK), BLK)


def lanes(p):
    return pl.ds(pl.multiple_of(p * 128, 128), 128)


def norm_parts(x):
    center = x - jnp.mean(x, axis=-1, keepdims=True)
    rstd = lax.rsqrt(jnp.mean(center * center, axis=-1, keepdims=True) + 1e-06)
    return center * rstd, rstd


def norm_back(d_normed, n, rstd, scl):
    dn = d_normed * scl
    return (
        dn - jnp.mean(dn, axis=-1, keepdims=True) - n * jnp.mean(dn * n, axis=-1, keepdims=True)
    ) * rstd


def turn(v, cosine, sine):
    lane = lax.broadcasted_iota(i32, v.shape, 1)
    partner = jnp.where(lane % 64 < 32, pltpu.roll(v, 96, 1), pltpu.roll(v, 32, 1))
    return v * cosine + partner * sine


def live_column(rows, c, length, first=0):
    r = lax.broadcasted_iota(i32, (rows, 1), 0) + first
    position = r + BLK * c + jnp.where(r >= BLK, BLK, 0)
    return position < length


def counts(length, c):
    nk = lax.shift_right_logical(length + (BLK - 1), 8)
    return nk, lax.shift_right_logical(nk - c + 1, 1)


class Copies:
    def __init__(self, sems):
        self.sems, self.started = sems, []

    def add(self, src, dst):
        copy = pltpu.make_async_copy(src, dst, self.sems.at[len(self.started)])
        copy.start()
        self.started.append(copy)

    def wait(self):
        for copy in self.started:
            copy.wait()


def load_shared(c, borrowed, w, wx_own, wx_oth, cols, wv, sem, into=None):
    into = cols if into is None else into
    whole = pltpu.make_async_copy(w.at[:, cols], wv.at[:, into], sem)
    pl.when(jnp.logical_not(borrowed))(lambda: whole.start())
    half = D // 2

    @pl.when(borrowed)
    def _():
        for source, at in ((wx_own, c), (wx_oth, 1 - c)):
            rows = pl.ds(pl.multiple_of(at * half, half), half)
            pltpu.make_async_copy(source.at[:, cols], wv.at[rows, into], sem).start()

    return whole


def gelu_parts(u):
    u2 = u * u
    t = jnp.tanh(0.7978845608028654 * (u * (1.0 + 0.044715 * u2)))
    return t, u2


def weight_grad_kernel(kind, sc, tt, st, y, out, xv, xt, yv, acc, ov, xsem, ysem, osem):
    chosen, c = tt[sc[0]], sc[1]

    def tile(j):
        return y.at[:, :, pl.ds(pl.multiple_of(j * D, D), D)]

    def into(j):
        at = pl.ds(pl.multiple_of(j * D, D), D)
        return out.at[at] if kind == "down" else out.at[:, at]

    def load_x(which):
        return pltpu.make_async_copy(st.at[which], xv, xsem.at[0])

    def load_y(j):
        slot = lax.rem(j, 2)
        return pltpu.make_async_copy(tile(j), yv.at[slot], ysem.at[slot])

    def store(j):
        slot = lax.rem(j, 2)
        return pltpu.make_async_copy(ov.at[slot], into(j), osem.at[slot])

    def live(mb):
        _, ns = counts(sc[2 + mb], c)
        picked = lax.rem(lax.shift_right_logical(chosen, mb), 2) == 1
        return jnp.where(picked, ns, 0)

    def transpose_rows(x):
        def step(mb, carry):
            def block(j, carry):
                xt[:, block_rows(2 * mb + j)] = x[mb, block_rows(j), :].T
                return carry

            return lax.fori_loop(0, live(mb), block, carry)

        lax.fori_loop(0, MB, step, 0)

    @pl.when(chosen > 0)
    def _():
        first = GB if kind == "down" else NM if kind == "attention" else NF
        load_x(first).start()
        load_y(0).start()
        load_x(first).wait()
        if kind != "down":
            transpose_rows(xv)
        if kind == "attention":
            load_x(AT).start()

        def step(j, carry):
            slot = lax.rem(j, 2)
            pl.when(j < 3)(lambda: load_y(j + 1).start())
            load_y(j).wait()
            if kind == "down":
                transpose_rows(yv.at[slot])
            if kind == "attention":

                @pl.when(j == 3)
                def _():
                    load_x(AT).wait()
                    transpose_rows(xv)

            acc[...] = jnp.zeros((D, D), f32)

            def add(mb, carry):
                for slots in (1, 2):

                    @pl.when(live(mb) == slots)
                    def _():
                        at = pl.ds(pl.multiple_of(mb * HALF, HALF), slots * BLK)
                        if kind == "down":
                            right = xv[mb, 0 : slots * BLK, :]
                        else:
                            right = yv[slot, mb, 0 : slots * BLK, :]
                        acc[...] += dot(xt[:, at], right)

                return carry

            lax.fori_loop(0, MB, add, 0)
            pl.when(j >= 2)(lambda: store(j - 2).wait())
            ov[slot] = acc[...].astype(bf16)
            store(j).start()
            return carry

        lax.fori_loop(0, 4, step, 0)
        store(2).wait()
        store(3).wait()


def reduce_kernel(roles, chips, mine, theirs, *refs):
    count, kept = len(mine[0]) + len(theirs[0]), len(mine[0])
    arrays, outs = refs[:count], refs[count : count + kept]
    near, total = refs[count + kept : 2 * count + kept], refs[2 * count + kept : 3 * count + kept]
    refs = refs[3 * count + kept :]
    paired = len(theirs[0]) > 0
    cross, refs = (refs[:kept], refs[kept:]) if paired else ((), refs)
    gathered, result, refs = refs[:kept], refs[kept : 2 * kept], refs[2 * kept :]
    load_sem, near_send, near_recv, cross_send, cross_recv, far_send, far_recv, out_sem = refs
    seg, dp = lax.axis_index("segment"), lax.axis_index("dp")
    core, place = lax.rem(dp, 2), lax.div(dp, 2)

    def device(segment, chip, at):
        return {"segment": segment, "dp": 2 * chip + at}

    def remote(src, dst, send, recv, target):
        return pltpu.make_async_remote_copy(
            src_ref=src, dst_ref=dst, send_sem=send, recv_sem=recv,
            device_id=target, device_id_type=pl.DeviceIdType.MESH,
        )

    def work(role, other, keep, give):
        barrier = pltpu.get_barrier_semaphore()
        peers = [device(role, place, 1 - core)]
        peers += [device(role, lax.rem(place + k, chips), core) for k in range(1, chips)]
        if paired:
            peers.append(device(other, place, core))
        for peer in peers:
            pl.semaphore_signal(
                barrier, inc=1, device_id=peer, device_id_type=pl.DeviceIdType.MESH
            )
        pl.semaphore_wait(barrier, len(peers))

        order = [lax.rem(place + k, chips) for k in range(1, chips)] + [place]
        nears, loads = [], []
        for z in range(chips):
            for k, at in enumerate(keep + give):
                to = remote(
                    arrays[at].at[2 * z + 1 - core], near[k].at[z],
                    near_send.at[k, z], near_recv.at[k, z], device(role, place, 1 - core),
                )
                to.start()
                nears.append(to)
                load = pltpu.make_async_copy(
                    arrays[at].at[2 * z + core], total[k].at[z], load_sem.at[k, z]
                )
                load.start()
                loads.append(load)
        crossing = []
        for z in range(chips):
            for k in list(range(kept, count)) + list(range(kept)):
                loads[z * count + k].wait()
                nears[z * count + k].wait()
                total[k][z] = total[k][z] + near[k][z]
                if k >= kept:
                    to = remote(
                        total[k].at[z], cross[k - kept].at[z],
                        cross_send.at[k - kept, z], cross_recv.at[k - kept, z],
                        device(other, place, core),
                    )
                    to.start()
                    crossing.append(to)
        far = []
        for z in range(chips):
            for k in range(kept):
                if paired:
                    crossing[z * kept + k].wait()
                    total[k][z] = total[k][z] + cross[k][z]
                far.append(
                    remote(
                        total[k].at[z], gathered[k].at[place],
                        far_send.at[k, z], far_recv.at[k, place], device(role, z, core),
                    )
                )
                pl.when(place != z)(far[-1].start)
        for k in range(kept):
            result[k][...] = total[k][place].astype(f32)
        for z in order[:-1]:
            for k in range(kept):
                remote(
                    total[k].at[z], gathered[k].at[z],
                    far_send.at[k, z], far_recv.at[k, z], device(role, z, core),
                ).wait_recv()
                result[k][...] += gathered[k][z].astype(f32)
        copies = []
        for k in range(kept):
            copies.append(pltpu.make_async_copy(result[k], outs[k], out_sem.at[k]))
            copies[-1].start()
        for z in range(chips):
            for k in range(kept):
                pl.when(place != z)(far[z * kept + k].wait_send)
        for copy in copies:
            copy.wait()

    for index, role in enumerate(roles):
        other = roles[1 - index] if paired else role
        pl.when(seg == role)(functools.partial(work, role, other, mine[index], theirs[index]))


def gather_kernel(size, rows, out, own_sem, send, recv):
    seg, dp = lax.axis_index("segment"), lax.axis_index("dp")

    def peer(k):
        return {"segment": seg, "dp": lax.rem(dp + k, size)}

    barrier = pltpu.get_barrier_semaphore()
    for k in range(1, size):
        pl.semaphore_signal(
            barrier, inc=1, device_id=peer(k), device_id_type=pl.DeviceIdType.MESH
        )
    pl.semaphore_wait(barrier, size - 1)
    own = pltpu.make_async_copy(rows, out.at[dp], own_sem)
    own.start()

    def copy(k, slot):
        return pltpu.make_async_remote_copy(
            src_ref=rows, dst_ref=out.at[slot], send_sem=send.at[k], recv_sem=recv.at[slot],
            device_id=peer(k), device_id_type=pl.DeviceIdType.MESH,
        )

    for k in range(1, size):
        copy(k, dp).start()
    own.wait()
    for k in range(1, size):
        copy(k, dp).wait_send()
        copy(k, lax.rem(dp + k, size)).wait_recv()


def gathered_rows(rows, size, number):
    return pl.pallas_call(
        functools.partial(gather_kernel, size),
        out_shape=jax.ShapeDtypeStruct((size, *rows.shape), rows.dtype),
        in_specs=[VMEM],
        out_specs=VMEM,
        scratch_shapes=[
            pltpu.SemaphoreType.DMA,
            pltpu.SemaphoreType.DMA((size,)),
            pltpu.SemaphoreType.DMA((size,)),
        ],
        compiler_params=pltpu.CompilerParams(
            vmem_limit_bytes=VLIM, collective_id=number, has_side_effects=True
        ),
        name="gather_sums",
    )(rows)


def reduced(arrays, roles, mine, theirs, chips, number, name):
    dims = [a.shape[1:] for a in arrays]
    kept, count = len(mine[0]), len(mine[0]) + len(theirs[0])
    order = mine[0] + theirs[0]
    every = [vm((chips, *dims[k])) for k in order]
    keeps = [vm((chips, *dims[k])) for k in mine[0]]
    pairs = pltpu.SemaphoreType.DMA((count, chips))
    return pl.pallas_call(
        functools.partial(reduce_kernel, roles, chips, mine, theirs),
        out_shape=[jax.ShapeDtypeStruct(dims[k], f32) for k in mine[0]],
        in_specs=[ANY] * len(arrays),
        out_specs=[ANY] * kept,
        scratch_shapes=every + every + (keeps if theirs[0] else []) + keeps
        + [vm(dims[k], f32) for k in mine[0]]
        + [pairs] * 7 + [pltpu.SemaphoreType.DMA((kept,))],
        compiler_params=pltpu.CompilerParams(
            vmem_limit_bytes=VLIM, collective_id=number, has_side_effects=True
        ),
        cost_estimate=cost(60),
        name=name,
    )(*arrays)


ANY = pl.BlockSpec(memory_space=pl.ANY)
VMEM = pl.BlockSpec(memory_space=pltpu.VMEM)


def shape(dims, dtype=bf16):
    return jax.ShapeDtypeStruct(dims, dtype)


ROWS = shape((HALF, D))
ST = shape((10, MB, HALF, D))
KV = shape((2, MB, SEQ_LEN, D))
LSE = shape((MB, HALF, 128), f32)
YS = shape((MB, HALF, FF))
DM = shape((MB, 8, D), f32)
DKV = shape((2, D, HALF))


def vm(dims, dtype=bf16):
    return pltpu.VMEM(dims, dtype)


HV, FV = vm((HALF, D)), vm((SEQ_LEN, D))


def cost(micros):
    return pl.CostEstimate(flops=int(micros * 1e9), bytes_accessed=1 << 20, transcendentals=0)


MESH = pl.DeviceIdType.MESH
ATT_F, FF_F, FF_B, ATT_B = range(4)


def chain_kernel(
    lens, xs, cs, w, rows2, cos, sin, mod,
    xa, xf, gf, ga, st, kv, lse, y, yf, act, dma, dmf, fin,
    wa, w1, w2, xv, nv, kvv, vv, h0, h1, h2, h3, h4, h5, h6, h7, h8, ov, lv, cv, sv,
    dkt, dvt, rcvv, dpv, duv, actv, accv, dmv, moda, modf,
    w_send, w_recv, wf_send, wf_recv, x_send, xa_own, xa_oth, fwd_send, c_send, gf_sem, xf_sem,
    ga_sem, push_sem, dkv_send, dkv_recv, ld, osem,
):
    role, dp = lax.axis_index("segment"), lax.axis_index("dp")
    c, place = lax.rem(dp, 2), lax.div(dp, 2)
    quarter, half_d = FF // 4, D // 2

    def device(segment, core):
        return {"segment": segment, "dp": 2 * place + core}

    def remote(src, dst, send, recv, target):
        return pltpu.make_async_remote_copy(
            src_ref=src, dst_ref=dst, send_sem=send, recv_sem=recv, device_id=target,
            device_id_type=MESH,
        )

    def local_copy(src, dst, sem):
        return pltpu.make_async_copy(src, dst, sem)

    partner = device(role, 1 - c)

    def rows_at(start, size):
        return pl.ds(pl.multiple_of(start, size), size)

    barrier = pltpu.get_barrier_semaphore()
    pl.semaphore_signal(barrier, inc=1, device_id=partner, device_id_type=MESH)
    for who, others in ((0, (1,)), (1, (0, 2, 3)), (2, (1, 3)), (3, (1, 2))):

        @pl.when(role == who)
        def _():
            for other in others:
                pl.semaphore_signal(
                    barrier, inc=1, device_id=device(other, c), device_id_type=MESH
                )
            pl.semaphore_wait(barrier, 1 + len(others))

    tables = [local_copy(cos, cv, ld.at[0]), local_copy(sin, sv, ld.at[1])]
    for copy in tables:
        copy.start()

    def give_x(k):
        return remote(xs.at[k], xa.at[2 * k + c], x_send.at[k], xa_oth.at[2 * k + c, 0], partner)

    def keep_x(k):
        return local_copy(xs.at[k], xa.at[2 * k + c], ld.at[4 + k])

    w_half = rows_at(c * half_d, half_d)
    rows_half = rows_at(c * quarter, quarter)
    high_half = rows_at(2 * quarter + c * quarter, quarter)

    def give_rows(dst, target):
        return remote(rows2.at[rows_half], w2.at[dst], w_send.at[1], w_recv.at[1], device(target, c))

    def give_w(dst, target):
        return remote(w.at[w_half], dst.at[w_half], w_send.at[0], w_recv.at[0], device(target, c))

    def give_mod(dst, target):
        return remote(mod, dst, w_send.at[2], w_recv.at[2], device(target, c))

    def give_c(k, j):
        return remote(
            cs.at[k, block_rows(1 - c + 2 * j)], gf.at[2 * k + c, pl.ds(j * BLK, BLK)],
            c_send.at[k, j], gf_sem.at[2 * k + c, j], partner,
        )

    def keep_c(k, j):
        return local_copy(
            cs.at[k, block_rows(c + 2 * j)], gf.at[2 * k + c, pl.ds(j * BLK, BLK)],
            ld.at[4 + 2 * k + j],
        )

    def forward_w(dst):
        return remote(dst.at[w_half], dst.at[w_half], wf_send.at[0], wf_recv.at[0], partner)

    def forward_rows(dst):
        return remote(w2.at[dst], w2.at[dst], wf_send.at[1], wf_recv.at[1], partner)

    def settle(copies):
        for given, passed in copies:
            given.wait_recv()
            passed.start()
        for given, passed in copies:
            passed.wait()

    @pl.when(role == 0)
    def _():
        for k in range(2):
            give_x(k).start()
            keep_x(k).start()
        give_rows(rows_half, 1).start()
        load = local_copy(w, wa, ld.at[2])
        load.start()
        local_copy(mod, moda, ld.at[3]).start()
        for k in range(2):
            keep_x(k).wait()
        local_copy(mod, moda, ld.at[3]).wait()
        load.wait()

    @pl.when(role == 1)
    def _():
        loads = [
            local_copy(w, w1, ld.at[2]), local_copy(mod, modf, ld.at[3]),
            local_copy(rows2, w2.at[pl.ds(2 * quarter, 2 * quarter)], ld.at[4]),
        ]
        for copy in loads:
            copy.start()
        settle([(give_rows(rows_half, 1), forward_rows(rows_half))])
        for copy in loads:
            copy.wait()

    for who in (2, 3):

        @pl.when(role == who)
        def _():
            other = 5 - who
            mine, theirs = (wa, w1) if who == 2 else (w1, wa)
            mod_mine, mod_theirs = (moda, modf) if who == 2 else (modf, moda)
            there, here = (rows_half, high_half) if who == 2 else (high_half, rows_half)
            give_mod(mod_mine, other).start()
            give_w(mine, other).start()
            give_rows(there, other).start()
            loads = [
                local_copy(w, mine, ld.at[2]), local_copy(mod, mod_mine, ld.at[3]),
                local_copy(
                    rows2, w2.at[pl.ds(0 if who == 2 else 2 * quarter, 2 * quarter)], ld.at[8]
                ),
            ]
            for copy in loads:
                copy.start()

            @pl.when(c == who - 2)
            def _():
                for k in range(2):
                    for j in range(2):
                        give_c(k, j).start()
                        keep_c(k, j).start()
                for k in range(2):
                    for j in range(2):
                        keep_c(k, j).wait()

            settle(
                [(give_w(theirs, other), forward_w(theirs)),
                 (give_rows(here, other), forward_rows(here))]
            )
            give_mod(mod_theirs, other).wait_recv()
            for copy in loads:
                copy.wait()

    for copy in tables:
        copy.wait()

    def pushed(step):
        return (
            ((role == 0) & (step < 4)) | (role == 1) | ((role >= 2) & (lax.rem(step, 4) == 3))
        ) & (step >= 0)

    def wait_pushed(step):
        @pl.when(pushed(step))
        def _():
            for j in range(2):
                at = pl.ds(j * BLK, BLK)
                remote(
                    ov.at[at], xf.at[0, at], push_sem.at[j], xf_sem.at[0, j], partner
                ).wait_send()

    def push(j, dst, recv, segment):
        remote(ov.at[block_rows(j)], dst, push_sem.at[j], recv, device(segment, c)).start()

    def att_f(step, mb):
        length = lens[mb]

        @pl.when(role == 0)
        def _():
            @pl.when(lax.rem(mb, 2) != c)
            def _():
                remote(
                    xs.at[0], xa.at[mb], x_send.at[0], xa_oth.at[mb, 0], partner
                ).wait_recv()

            load = local_copy(xa.at[mb], xv, ld.at[0])
            load.start()
            load.wait()

        def forward(j):
            at = block_rows(c + 2 * j)
            return remote(xa.at[mb, at], xa.at[mb, at], fwd_send.at[j], xa_oth.at[mb, j], partner)

        @pl.when(role != 0)
        def _():
            for j in range(2):
                at = block_rows(c + 2 * j)
                remote(
                    ov.at[pl.ds(j * BLK, BLK)], xa.at[mb, at], push_sem.at[j], xa_own.at[mb, j],
                    partner,
                ).wait_recv()
                forward(j).start()
                local_copy(xa.at[mb, at], xv.at[at], ld.at[j]).start()
            for j in range(2):
                at = block_rows(1 - c + 2 * j)
                remote(
                    xa.at[mb, at], xa.at[mb, at], fwd_send.at[j], xa_oth.at[mb, j], partner
                ).wait_recv()
                local_copy(xa.at[mb, at], xv.at[at], ld.at[2 + j]).start()
            for j in range(2):
                at, to = block_rows(c + 2 * j), block_rows(1 - c + 2 * j)
                local_copy(xa.at[mb, at], xv.at[at], ld.at[j]).wait()
                local_copy(xa.at[mb, to], xv.at[to], ld.at[2 + j]).wait()
                forward(j).wait_send()

        off, scl, gat = moda[mb, 0:1, :], 1.0 + moda[mb, 1:2, :], moda[mb, 2:3, :]

        def kv_block(b, carry):
            rows = block_rows(b)
            norm, _ = norm_parts(xv[rows, :].astype(f32))
            n = (norm * scl + off).astype(bf16)
            nv[rows, :] = n
            cosine, sine = cv[rows, :], sv[rows, :]
            kk = dot(n, wa[:, D : 2 * D])
            for p in range(6):
                ls = slice(p * 128, (p + 1) * 128)
                kvv[rows, ls] = turn(kk[:, ls], cosine, sine).astype(bf16)
            vv[rows, :] = dot(n, wa[:, 2 * D : 3 * D]).astype(bf16)
            return carry

        lax.fori_loop(0, 4, kv_block, 0)

        def q_block(j, carry):
            nat = block_rows(c + 2 * j)
            rows = block_rows(j)
            cosine, sine = cv[nat, :] * 0.125, sv[nat, :] * 0.125
            qq = dot(nv[nat, :], wa[:, 0:D])
            for p in range(6):
                ls = slice(p * 128, (p + 1) * 128)
                h0[rows, ls] = turn(qq[:, ls], cosine, sine).astype(bf16)
            return carry

        lax.fori_loop(0, 2, q_block, 0)
        sends = Copies(osem)
        sends.add(h0, st.at[QS, mb])
        sends.add(kvv, kv.at[0, mb])
        sends.add(vv, kv.at[1, mb])
        lane = lax.broadcasted_iota(i32, (BLK, 128), 1)
        position = lax.broadcasted_iota(i32, (1, SEQ_LEN), 1)
        bias = jnp.where(position < length, 0.0, -1e30).astype(f32)
        lv[...] = jnp.zeros((HALF, 128), f32)
        wait_pushed(step - 1)

        def block(j, carry):
            rows = block_rows(j)

            def pair(hp, carry):
                ls = lanes(hp)
                k2, v2, q2 = kvv[:, ls], vv[:, ls], h0[rows, ls]
                outs, stats = [], lv[rows, :]
                for a in range(2):
                    s = dot_nt(jnp.where((lane < 64) == (a == 0), q2, jnp.zeros_like(q2)), k2)
                    s = s + bias
                    m = jnp.max(s, axis=1, keepdims=True)
                    e = jnp.exp(s - m)
                    total = jnp.sum(e, axis=1, keepdims=True)
                    outs.append(dot(e.astype(bf16), v2) / total)
                    stats = jnp.where(lane == 2 * hp + a, m + jnp.log(total), stats)
                h1[rows, ls] = jnp.where(lane < 64, outs[0], outs[1]).astype(bf16)
                lv[rows, :] = stats
                return carry

            lax.fori_loop(0, HEADS // 2, pair, 0)
            branch = dot(h1[rows, :], wa[:, 3 * D : 4 * D])
            live = live_column(BLK, c, length, j * BLK)
            x = xv[block_rows(c + 2 * j), :].astype(f32)
            ov[rows, :] = (x + jnp.where(live, gat * branch, 0.0)).astype(bf16)
            h2[rows, :] = branch.astype(bf16)
            pl.when(role == 0)(lambda: push(j, xf.at[mb, rows], xf_sem.at[mb, j], 1))
            return carry

        lax.fori_loop(0, 2, block, 0)
        sends.add(h1, st.at[AT, mb])
        sends.add(h2, st.at[BR, mb])
        sends.add(lv, lse.at[mb])

        @pl.when(role != 0)
        def _():
            to_ff = local_copy(ov, xf.at[mb], ld.at[0])
            to_ff.start()
            to_ff.wait()

        sends.wait()

    def ff_f(step, mb):
        length = lens[mb]
        off, scl, gat = modf[mb, 0:1, :], 1.0 + modf[mb, 1:2, :], modf[mb, 2:3, :]
        wait_pushed(step - 1)

        def block(j, carry):
            rows = block_rows(j)

            @pl.when(role == 1)
            def _():
                remote(
                    ov.at[rows], xf.at[mb, rows], push_sem.at[j], xf_sem.at[mb, j], partner
                ).wait_recv()

            load = local_copy(xf.at[mb, rows], h0.at[rows], ld.at[0])
            load.start()
            load.wait()
            x = h0[rows, :].astype(f32)
            norm, _ = norm_parts(x)
            h1[rows, :] = (norm * scl + off).astype(bf16)
            accv[rows, :] = jnp.zeros((BLK, D), f32)

            def part(p, carry):
                at = pl.ds(pl.multiple_of(p * D, D), D)
                u = dot(h1[rows, :], w1[:, at])
                t, _ = gelu_parts(u)
                accv[rows, :] += dot((0.5 * u * (1.0 + t)).astype(bf16), w2[at, :])
                return carry

            lax.fori_loop(0, 4, part, 0)
            acc = accv[rows, :]
            live = live_column(BLK, c, length, j * BLK)
            ov[rows, :] = (h0[rows, :].astype(f32) + jnp.where(live, gat * acc, 0.0)).astype(bf16)
            h2[rows, :] = acc.astype(bf16)

            @pl.when(role == 1)
            def _():
                push(j, xa.at[mb, block_rows(c + 2 * j)], xa_own.at[mb, j], 2 + lax.rem(mb, 2))

            return carry

        lax.fori_loop(0, 2, block, 0)
        sends = Copies(osem)
        sends.add(h2, st.at[BF, mb])

        @pl.when(role != 1)
        def _():
            final = local_copy(ov, fin.at[mb], ld.at[0])
            final.start()
            final.wait()

        sends.wait()

    def ff_b(step, mb):
        length = lens[mb]
        off, scl, gat = modf[mb, 0:1, :], 1.0 + modf[mb, 1:2, :], modf[mb, 2:3, :]
        loads = [
            local_copy(xf.at[mb], h0, ld.at[0]),
            local_copy(st.at[BF, mb], h2, ld.at[1]),
        ]
        for copy in loads:
            copy.start()
        dmv[...] = jnp.zeros((8, D), f32)
        for copy in loads:
            copy.wait()
        wait_pushed(step - 1)

        def block(j, carry):
            rows = block_rows(j)

            @pl.when((role == 1) | (lax.rem(mb, 2) != c))
            def _():
                remote(
                    ov.at[rows], gf.at[mb, rows], push_sem.at[j], gf_sem.at[mb, j], partner
                ).wait_recv()

            load = local_copy(gf.at[mb, rows], h1.at[rows], ld.at[2])
            load.start()
            load.wait()
            norm, _ = norm_parts(h0[rows, :].astype(f32))
            h3[rows, :] = (norm * scl + off).astype(bf16)
            live = live_column(BLK, c, length, j * BLK)
            gl = jnp.where(live, h1[rows, :].astype(f32), 0.0)
            h4[rows, :] = (gl * gat).astype(bf16)
            dmv[2:3, :] += jnp.sum(gl * h2[rows, :].astype(f32), axis=0, keepdims=True)
            accv[rows, :] = jnp.zeros((BLK, D), f32)

            def part(p, carry):
                cols = pl.ds(pl.multiple_of(p * D, D), D)
                u = dot(h3[rows, :], w1[:, cols])
                t, u2 = gelu_parts(u)
                half = 0.5 * (1.0 + t)
                actv[rows, cols] = (u * half).astype(bf16)
                slope = half + 0.5 * u * (1.0 - t * t) * (
                    0.7978845608028654 * (1.0 + 3 * 0.044715 * u2)
                )
                du = (dot_nt(h4[rows, :], w2[cols, :]) * slope).astype(bf16)
                duv[rows, cols] = du
                accv[rows, :] += dot_nt(du, w1[:, cols])
                return carry

            lax.fori_loop(0, 4, part, 0)
            acc = accv[rows, :]
            n, rstd = norm_parts(h0[rows, :].astype(f32))
            dmv[0:1, :] += jnp.sum(acc, axis=0, keepdims=True)
            dmv[1:2, :] += jnp.sum(acc * n, axis=0, keepdims=True)
            ov[rows, :] = (h1[rows, :].astype(f32) + norm_back(acc, n, rstd, scl)).astype(bf16)
            pl.when(role == 1)(lambda: push(j, ga.at[mb, rows], ga_sem.at[mb, j], 0))
            return carry

        lax.fori_loop(0, 2, block, 0)
        sends = Copies(osem)
        sends.add(h3, st.at[NF, mb])
        sends.add(h4, st.at[GB, mb])
        sends.add(duv, yf.at[mb])
        sends.add(actv, act.at[mb])
        sends.add(dmv, dmf.at[mb])

        @pl.when(role != 1)
        def _():
            to_att = local_copy(ov, ga.at[mb], ld.at[0])
            to_att.start()
            to_att.wait()

        sends.wait()

    def att_b(step, mb):
        length = lens[mb]
        off, scl, gat = moda[mb, 0:1, :], 1.0 + moda[mb, 1:2, :], moda[mb, 2:3, :]
        gv, atv, qv, gbv, dov, dqv, xo, brv, no = h0, h1, h2, h3, h4, h5, h6, h7, h8
        loads = [
            local_copy(st.at[QS, mb], qv, ld.at[0]),
            local_copy(kv.at[0, mb], kvv, ld.at[1]),
            local_copy(kv.at[1, mb], vv, ld.at[2]),
            local_copy(st.at[AT, mb], atv, ld.at[3]),
            local_copy(lse.at[mb], lv, ld.at[4]),
            local_copy(st.at[BR, mb], brv, ld.at[5]),
        ]
        for j in range(2):
            loads.append(
                local_copy(
                    xa.at[mb, block_rows(c + 2 * j)], xo.at[pl.ds(j * BLK, BLK)], ld.at[6 + j]
                )
            )
        for copy in loads:
            copy.start()
        dmv[...] = jnp.zeros((8, D), f32)

        def grad_block(j, carry):
            rows = block_rows(j)

            @pl.when(role == 0)
            def _():
                remote(
                    ov.at[rows], ga.at[mb, rows], push_sem.at[j], ga_sem.at[mb, j], partner
                ).wait_recv()

            load = local_copy(ga.at[mb, rows], gv.at[rows], ld.at[8])
            load.start()
            load.wait()
            live = live_column(BLK, c, length, j * BLK)
            gb = jnp.where(live, gv[rows, :].astype(f32) * gat, 0.0).astype(bf16)
            gbv[rows, :] = gb
            dov[rows, :] = dot_nt(gb, wa[:, 3 * D : 4 * D]).astype(bf16)
            return carry

        lax.fori_loop(0, 2, grad_block, 0)
        sends = Copies(osem)
        sends.add(gbv, y.at[mb, :, pl.ds(3 * D, D)])
        for copy in loads:
            copy.wait()
        lane = lax.broadcasted_iota(i32, (HALF, 128), 1)
        position = lax.broadcasted_iota(i32, (1, SEQ_LEN), 1)
        bias = jnp.where(position < length, 0.0, -1e30).astype(f32)

        def pair(hp, carry):
            ls = lanes(hp)
            k2, v2 = kvv[:, ls], vv[:, ls]
            q2, do2 = qv[:, ls], dov[:, ls]
            q2t, do2t = q2.T, do2.T
            both = do2.astype(f32) * atv[:, ls].astype(f32)
            stats = lv[...]
            dqs = []
            for a in range(2):
                head = (lane < 64) == (a == 0)
                zero = jnp.zeros_like(q2)
                s = dot_nt(jnp.where(head, q2, zero), k2) + bias
                base = jnp.sum(jnp.where(lane == 2 * hp + a, stats, 0.0), axis=1, keepdims=True)
                p = jnp.exp(s - base)
                dp_ = dot_nt(jnp.where(head, do2, zero), v2)
                delta = jnp.sum(jnp.where(head, both, 0.0), axis=1, keepdims=True)
                ds = (p * (dp_ - delta)).astype(bf16)
                dqs.append(dot(ds, k2))
                at = pl.ds(pl.multiple_of(hp * 128 + a * 64, 64), 64)
                dkt[at, :] = dot(q2t[a * 64 : (a + 1) * 64, :], ds).astype(bf16)
                dvt[at, :] = dot(do2t[a * 64 : (a + 1) * 64, :], p.astype(bf16)).astype(bf16)
            dqv[:, ls] = jnp.where(lane < 64, dqs[0], dqs[1]).astype(bf16)
            return carry

        lax.fori_loop(0, HEADS // 2, pair, 0)
        gives = []
        for part, grad in enumerate((dkt, dvt)):
            for j in range(2):
                give = remote(
                    grad.at[:, block_rows(1 - c + 2 * j)],
                    rcvv.at[mb, part, :, pl.ds(j * BLK, BLK)],
                    dkv_send.at[part, j], dkv_recv.at[mb, part, j], partner,
                )
                give.start()
                gives.append(give)
        wait_pushed(step - 1)
        for give in gives:
            give.wait()

        def last(j, carry):
            rows, nat = block_rows(j), block_rows(c + 2 * j)
            cosine, sine = cv[nat, :], -sv[nat, :]
            for p in range(6):
                ls = slice(p * 128, (p + 1) * 128)
                dpv[rows, ls] = (turn(dqv[rows, ls].astype(f32), cosine, sine) * 0.125).astype(bf16)
                for part, own in enumerate((dkt, dvt)):
                    total = own[ls, nat].astype(f32) + rcvv[mb, part, ls, rows].astype(f32)
                    grad = total.T
                    if part == 0:
                        grad = turn(grad.astype(bf16).astype(f32), cosine, sine)
                    dpv[rows, (part + 1) * D + p * 128 : (part + 1) * D + (p + 1) * 128] = (
                        grad.astype(bf16)
                    )
            acc = dot_nt(dpv[rows, :], wa[:, 0 : 3 * D])
            n, rstd = norm_parts(xo[rows, :].astype(f32))
            no[rows, :] = (n * scl + off).astype(bf16)
            g = gv[rows, :].astype(f32)
            live = live_column(BLK, c, length, j * BLK)
            gl = jnp.where(live, g, 0.0)
            dmv[0:1, :] += jnp.sum(acc, axis=0, keepdims=True)
            dmv[1:2, :] += jnp.sum(acc * n, axis=0, keepdims=True)
            dmv[2:3, :] += jnp.sum(gl * brv[rows, :].astype(f32), axis=0, keepdims=True)
            ov[rows, :] = (g + norm_back(acc, n, rstd, scl)).astype(bf16)
            pl.when(role != 0)(lambda: push(j, gf.at[mb, rows], gf_sem.at[mb, j], 1))
            return carry

        lax.fori_loop(0, 2, last, 0)
        sends.add(dpv, y.at[mb, :, pl.ds(0, 3 * D)])
        sends.add(no, st.at[NM, mb])
        sends.add(dmv, dma.at[mb])

        @pl.when(role == 0)
        def _():
            final = local_copy(ov, fin.at[mb], ld.at[0])
            final.start()
            final.wait()

        sends.wait()

    def run(step, carry):
        first = step < 4
        kind = jnp.where(
            role == 0, jnp.where(first, ATT_F, ATT_B),
            jnp.where(role == 1, jnp.where(first, FF_F, FF_B), lax.rem(step, 4)),
        )
        mb = jnp.where(role < 2, lax.rem(step, 4), lax.div(step, 4) * 2 + role - 2)
        for which, work in ((ATT_F, att_f), (FF_F, ff_f), (FF_B, ff_b), (ATT_B, att_b)):
            pl.when(kind == which)(functools.partial(work, step, mb))
        return carry

    lax.fori_loop(0, 8, run, 0)
    wait_pushed(7)

    @pl.when(role == 0)
    def _():
        for k in range(2):
            give_x(k).wait_send()
        give_rows(rows_half, 1).wait_send()

    for who in (2, 3):

        @pl.when(role == who)
        def _():
            other = 5 - who
            mine, mod_mine = (wa, moda) if who == 2 else (w1, modf)
            there = rows_half if who == 2 else high_half
            give_mod(mod_mine, other).wait_send()
            give_w(mine, other).wait_send()
            give_rows(there, other).wait_send()

            @pl.when(c == who - 2)
            def _():
                for k in range(2):
                    for j in range(2):
                        give_c(k, j).wait_send()


def chain(lens, xs, cs, w, rows2, cos, sin, mod):
    def sems(*dims):
        return pltpu.SemaphoreType.DMA(dims)

    outs = [shape((MB, SEQ_LEN, D)), shape((MB, HALF, D)), shape((MB, HALF, D)), shape((MB, HALF, D)),
            ST, KV, LSE, YS, YS, YS, DM, DM, shape((MB, HALF, D))]
    table = vm((SEQ_LEN, 128), f32)
    return pl.pallas_call(
        chain_kernel,
        out_shape=outs,
        in_specs=[pl.BlockSpec(memory_space=pltpu.SMEM)] + [ANY] * 7,
        out_specs=[ANY] * len(outs),
        scratch_shapes=[
            vm((D, FF)), vm((D, FF)), vm((FF, D)), FV, FV, FV, FV,
            HV, HV, HV, HV, HV, HV, HV, HV, HV, HV, vm((HALF, 128), f32), table, table,
            vm((D, SEQ_LEN)), vm((D, SEQ_LEN)), vm((MB, 2, D, HALF)), vm((HALF, 3 * D)),
            vm((HALF, FF)), vm((HALF, FF)), vm((HALF, D), f32), vm((8, D), f32),
            vm((MB, 8, D), f32), vm((MB, 8, D), f32),
            sems(3), sems(3), sems(2), sems(2), sems(2), sems(MB, 2), sems(MB, 2), sems(2),
            sems(2, 2), sems(MB, 2), sems(MB, 2), sems(MB, 2), sems(2), sems(2, 2),
            sems(MB, 2, 2), sems(12), sems(10),
        ],
        compiler_params=pltpu.CompilerParams(
            vmem_limit_bytes=62 << 20, collective_id=0, has_side_effects=True
        ),
        cost_estimate=cost(300),
        name="layers",
    )(lens, xs, cs, w, rows2, cos, sin, mod)


def time_cond(steps):
    half_width = D // 2
    frequency = jnp.exp(
        jnp.arange(half_width, dtype=f32) * (-math.log(10000.0) / half_width)
    )
    angles = steps.astype(f32)[:, None] * frequency[None, :]
    return jax.nn.silu(jnp.concatenate([jnp.cos(angles), jnp.sin(angles)], axis=1))


def rope_tables():
    inverse = np.exp(np.arange(32, dtype=np.float32) * np.float32(-math.log(10000.0) / 32))
    angles = np.arange(SEQ_LEN, dtype=np.float32)[:, None] * inverse[None, :]
    cosine, sine = np.cos(angles), np.sin(angles)
    return (
        np.concatenate([cosine] * 4, axis=1).astype(np.float32),
        np.concatenate([-sine, sine, -sine, sine], axis=1).astype(np.float32),
    )


def local(block_input, cotangent, lengths, steps, mod_weight, mod_bias, first_weight, down_rows):
    ndp = lax.axis_size("dp")
    seg, dp = lax.axis_index("segment"), lax.axis_index("dp")
    core, chips, place = dp % 2, ndp // 2, dp // 2
    w, rows2 = first_weight[0], down_rows[0]

    def across(value, moves):
        pairs = [
            (r * ndp + 2 * i + c, q * ndp + 2 * i + e) for (r, c), (q, e) in moves for i in range(chips)
        ]
        return lax.ppermute(value, ("segment", "dp"), pairs)

    def swap(value, roles=(0, 1, 2, 3)):
        return across(value, [((r, c), (r, 1 - c)) for r in roles for c in range(2)])

    def hop(value, pairs):
        return lax.ppermute(value, "segment", pairs)

    def after(value, other):
        return lax.optimization_barrier((value, other))[0]

    info = jnp.stack([lengths, steps])
    other_info = swap(info)
    full = (lengths[1] > lengths[0]).astype(i32)
    xs = jnp.where(full == 0, block_input, block_input[::-1])
    cs = jnp.where(full == 0, cotangent, cotangent[::-1])
    info0 = jnp.where(core == 0, info, other_info)
    info1 = jnp.where(core == 0, other_info, info)
    full0 = (info0[0, 1] > info0[0, 0]).astype(i32)
    full1 = (info1[0, 1] > info1[0, 0]).astype(i32)
    chip = jnp.stack([info0[:, full0], info1[:, full1], info0[:, 1 - full0], info1[:, 1 - full1]])
    lens = chip[:, 0]
    sc = jnp.concatenate([jnp.stack([seg, core]), lens]).astype(i32)
    conditions = time_cond(chip[:, 1]).astype(bf16)
    modulation = jnp.dot(conditions, mod_weight[0], preferred_element_type=f32)
    modulation = modulation + mod_bias[0].astype(f32)
    mod = jnp.pad(modulation.reshape(MB, 3, D), ((0, 0), (0, 5), (0, 0)))
    cos, sin = (jnp.asarray(t) for t in rope_tables())
    _, _, _, _, st, _, _, y, yf, act, dma, dmf, fin = chain(lens, xs, cs, w, rows2, cos, sin, mod)

    depth, wide_rows = D // ndp, FF // 2 // ndp

    def weight_grad(kind, chosen, right):
        turns = np.array([chosen.get(r, 0) for r in range(4)], np.int32)
        pairs = pltpu.SemaphoreType.DMA((2,))
        return pl.pallas_call(
            functools.partial(weight_grad_kernel, kind),
            grid_spec=pltpu.PrefetchScalarGridSpec(
                num_scalar_prefetch=2,
                grid=(1,),
                in_specs=[ANY, ANY],
                out_specs=ANY,
                scratch_shapes=[
                    vm((MB, HALF, D)), vm((D, MB * HALF)), vm((2, MB, HALF, D)), vm((D, D), f32),
                    vm((2, D, D)), pairs, pairs, pairs,
                ],
            ),
            out_shape=shape((FF, D) if kind == "down" else (D, FF)),
            compiler_params=pltpu.CompilerParams(vmem_limit_bytes=VLIM),
            cost_estimate=cost(12),
            name=kind + "_gradient",
        )(sc, turns, st, right)

    def ff_grads(chosen):
        up = weight_grad("up", chosen, yf)
        down = weight_grad("down", chosen, act).reshape(2 * ndp, wide_rows, D)
        return up.reshape(ndp, depth, FF), down[:ndp], down[ndp:]

    def owned(ac, bd):
        keep = jnp.where(core == 0, ac, bd)
        give = jnp.where(core == 0, bd, ac)
        return jnp.where(core == seg % 2, keep, swap(give))

    masks = {2: 5, 3: 10}
    att_23 = weight_grad("attention", {0: 15, **masks}, y).reshape(ndp, depth, FF)
    up_x, low_x, high_x = ff_grads({1: 15, **masks})
    first_23, rows_23 = reduced(
        (att_23, up_x, low_x, high_x), (2, 3), ([0, 2], [1, 3]), ([1, 3], [0, 2]), chips, 1,
        "second_layer_sums",
    )
    up_1, low_1, high_1 = reduced(
        (up_x, low_x, high_x), (1,), ([0, 1, 2],), ([],), chips, 2, "feedforward_sums"
    )
    (first_0,) = reduced((att_23,), (0,), ([0],), ([],), chips, 3, "attention_sums")
    low_0 = hop(after(low_1, first_0), [(1, 0)])
    even = seg % 2 == 0
    first_sum = jnp.where(seg == 0, first_0, jnp.where(seg == 1, up_1, first_23))
    rows_sum = jnp.where(seg == 0, low_0, jnp.where(seg == 1, high_1, rows_23))

    pairs = fin.reshape(2, 2, HALF, D)
    one, two = pairs[:, 0], pairs[:, 1]
    first_one = across(one[:, :BLK], [((2, c), (c, c)) for c in range(2)])
    first_two = across(two[:, :BLK], [((3, c), (c, c)) for c in range(2)])
    mid = jnp.where(seg == 2, one[:, BLK:], two[:, BLK:])
    crossed = across(mid, [((2, 1), (3, 1)), ((3, 0), (2, 0))])
    outs = owned(
        jnp.where(seg < 2, first_one, jnp.where(seg == 2, mid, crossed)),
        jnp.where(seg < 2, first_two, jnp.where(seg == 2, crossed, mid)),
    )
    to_one = across(pairs[:, :, :BLK], [((0, 1), (1, 1))])
    to_others = across(pairs[:, :, BLK:], [((0, 0), (2, 0)), ((0, 1), (3, 1))])
    got = jnp.where(seg == 0, pairs[:, :, :BLK], jnp.where(seg == 1, to_one, to_others))
    grads = owned(got[:, 0], got[:, 1])

    mine = np.array([[True] * 4, [True] * 4, [True, False] * 2, [False, True] * 2])
    mine = jnp.asarray(mine)[seg][:, None, None]
    dma, dmf = (jnp.where(mine, m[:, :3], 0.0) for m in (dma, dmf))
    sums = jnp.where(even, dma, dmf) + hop(jnp.where(even, dmf, dma), [(2, 3), (3, 2)])
    mod_rows = jnp.concatenate([sums.reshape(MB, 3 * D), conditions.astype(f32)], axis=1)
    all_rows = gathered_rows(mod_rows.reshape(-1, 128), ndp, 4).reshape(ndp * MB, 4 * D)
    mine = lax.dynamic_slice_in_dim(all_rows, 3 * D + dp * depth, depth, axis=1)
    all_rows = all_rows[:, : 3 * D]
    mod_w_sum = jnp.dot(mine.T, all_rows, precision=lax.Precision.HIGHEST, preferred_element_type=f32)
    width = 3 * D // ndp
    mod_b_sum = jnp.sum(lax.dynamic_slice_in_dim(all_rows, dp * width, width, axis=1), axis=0)

    def placed(both, part):
        both = jnp.where(full == 0, both, both[::-1])
        live = (seg * BLK + jnp.arange(BLK))[None, :, None] < lengths[:, None, None]
        return jnp.where(live, both, lax.dynamic_slice_in_dim(part, seg * BLK, BLK, axis=1))

    return (
        placed(outs, block_input),
        placed(grads, cotangent).astype(f32),
        mod_w_sum[None],
        mod_b_sum[None],
        first_sum.astype(f32)[None],
        rows_sum.astype(f32)[None],
    )


def solution(mesh):
    in_specs = (
        P("dp", None, None),
        P("dp", None, None),
        P("dp"),
        P("dp"),
        P("segment", None, None),
        P("segment", None),
        P("segment", None, None),
        P("segment", None, None),
    )
    out_specs = (
        P("dp", "segment", None),
        P("dp", "segment", None),
        P("segment", "dp", None),
        P("segment", "dp"),
        P("segment", "dp", None),
        P("segment", "dp", None),
    )
    return jax.shard_map(local, mesh=mesh, in_specs=in_specs, out_specs=out_specs, check_vma=False)
```

```python
import functools
import math

import jax
import jax.numpy as jnp
import numpy as np
from jax import lax
from jax.experimental import pallas as pl
from jax.experimental.pallas import tpu as pltpu
from jax.sharding import PartitionSpec as P

D = 768
HEADS = 12
HEAD_DIM = 64
FF = 3072
SEQ_LEN = 1024
BLK = 256
HALF = SEQ_LEN // 2
MB = 4
QS, AT, BR, NM, BF, NF, GB = range(7)
VLIM = 56 << 20
bf16, f32, i32 = jnp.bfloat16, jnp.float32, jnp.int32


def dot(a, b):
    return lax.dot_general(a, b, (((1,), (0,)), ((), ())), preferred_element_type=f32)


def dot_nt(a, b):
    return lax.dot_general(a, b, (((1,), (1,)), ((), ())), preferred_element_type=f32)


def dot_tn(a, b):
    return lax.dot_general(a, b, (((0,), (0,)), ((), ())), preferred_element_type=f32)


def block_rows(b):
    return pl.ds(pl.multiple_of(b * BLK, BLK), BLK)


def lanes(p):
    return pl.ds(pl.multiple_of(p * 128, 128), 128)


def norm_parts(x):
    center = x - jnp.mean(x, axis=-1, keepdims=True)
    rstd = lax.rsqrt(jnp.mean(center * center, axis=-1, keepdims=True) + 1e-06)
    return center * rstd, rstd


def norm_back(d_normed, n, rstd, scl):
    dn = d_normed * scl
    return (
        dn - jnp.mean(dn, axis=-1, keepdims=True) - n * jnp.mean(dn * n, axis=-1, keepdims=True)
    ) * rstd


def turn(v, cosine, sine):
    lane = lax.broadcasted_iota(i32, v.shape, 1)
    partner = jnp.where(lane % 64 < 32, pltpu.roll(v, 96, 1), pltpu.roll(v, 32, 1))
    return v * cosine + partner * sine


def live_column(c, length, j):
    r = lax.broadcasted_iota(i32, (BLK, 1), 0) + BLK * (c + 2 * j)
    return r.astype(f32) < length


def gelu_parts(u):
    u2 = u * u
    t = jnp.tanh(0.7978845608028654 * (u * (1.0 + 0.044715 * u2)))
    return t, u2


def weight_grad_kernel(kind, roles, st, y, out, xv, yv, acc, ov, xsem, ysem, osem):
    role = lax.axis_index("segment")
    parts = jnp.where(role < 2, 2, 1)

    def tile(j):
        return y.at[:, :, pl.ds(pl.multiple_of(j * D, D), D)]

    def into(j):
        at = pl.ds(pl.multiple_of(j * D, D), D)
        return out.at[at] if kind == "down" else out.at[:, at]

    def load_x(which):
        return pltpu.make_async_copy(st.at[which], xv, xsem.at[0])

    def load_y(j):
        slot = lax.rem(j, 2)
        return pltpu.make_async_copy(tile(j), yv.at[slot], ysem.at[slot])

    def store(j):
        slot = lax.rem(j, 2)
        return pltpu.make_async_copy(ov.at[slot], into(j), osem.at[slot])

    chosen = functools.reduce(jnp.logical_or, [role == r for r in roles])

    @pl.when(chosen)
    def _():
        load_x(GB if kind == "down" else NM if kind == "attention" else NF).start()
        load_y(0).start()
        load_x(0).wait()

        def step(j, carry):
            slot = lax.rem(j, 2)
            pl.when(j < 3)(lambda: load_y(j + 1).start())
            load_y(j).wait()
            if kind == "attention":

                @pl.when(j == 3)
                def _():
                    load_x(AT).start()
                    load_x(AT).wait()

            def product(h):
                if kind == "down":
                    return dot_tn(yv[slot, h], xv[h])
                return dot_tn(xv[h], yv[slot, h])

            pl.when(j >= 2)(lambda: store(j - 2).wait())

            @pl.when(parts == 1)
            def _():
                ov[slot] = product(0).astype(bf16)

            @pl.when(parts == 2)
            def _():
                acc[...] = product(0)
                ov[slot] = (acc[...] + product(1)).astype(bf16)

            store(j).start()
            return carry

        lax.fori_loop(0, 4, step, 0)
        store(2).wait()
        store(3).wait()


ANY = pl.BlockSpec(memory_space=pl.ANY)
VMEM = pl.BlockSpec(memory_space=pltpu.VMEM)


def shape(dims, dtype=bf16):
    return jax.ShapeDtypeStruct(dims, dtype)


ST = shape((7, 2, SEQ_LEN, D))
KV = shape((2, MB, SEQ_LEN, D))
LSE = shape((MB, HALF, 128), f32)
YS = shape((2, SEQ_LEN, FF))
DM = shape((MB, 8, D), f32)
OWNED = shape((2, BLK, D))


def vm(dims, dtype=bf16):
    return pltpu.VMEM(dims, dtype)


HV, FV = vm((HALF, D)), vm((SEQ_LEN, D))


def cost(micros):
    return pl.CostEstimate(flops=int(micros * 1e9), bytes_accessed=1 << 20, transcendentals=0)


MESH = pl.DeviceIdType.MESH


def sums_kernel(
    chips, att, up, down, dma, dmf, mod, fin, first_out, rows_out, gathered, out_g,
    near_w, near_r, tot_w, tot_r, cross_w, cross_r, right_w, right_r, left_w, left_r, res_w, res_r,
    dm_own, dm_near, dm_tot, modv,
    load_sem, near_send, near_recv, cross_send, cross_recv, line_send, right_recv, left_recv,
    dm_load, dm_send, dm_recv, g_send, g_recv, fin_send, fin_recv,
):
    seg, dp = lax.axis_index("segment"), lax.axis_index("dp")
    core, place = lax.rem(dp, 2), lax.div(dp, 2)
    size = 2 * chips

    def device(segment, chip, at):
        return {"segment": segment, "dp": 2 * chip + at}

    def remote(src, dst, send, recv, target):
        return pltpu.make_async_remote_copy(
            src_ref=src, dst_ref=dst, send_sem=send, recv_sem=recv,
            device_id=target, device_id_type=MESH,
        )

    def work(role):
        other = 5 - role if role >= 2 else 1 - role
        second = role >= 2
        low, high = 0, size
        parts = {
            0: {0: (att, 0)},
            1: {0: (up, 0), 1: (down, high), 3: (down, low)},
            2: {0: (att, 0), 1: (down, low), 2: (up, 0), 3: (down, high)},
            3: {0: (up, 0), 1: (down, high), 2: (att, 0), 3: (down, low)},
        }[role]
        kept = 2
        give = [k for k in (0, 1) if k + 2 in parts]
        taken = {0: [1], 1: [], 2: [0, 1], 3: [0, 1]}[role]

        def pick(wide, rows, k):
            return (rows if k % 2 else wide).at[k // 2]

        def near(k):
            return pick(near_w, near_r, k)

        def total(k):
            return pick(tot_w, tot_r, k)

        def right(k):
            return pick(right_w, right_r, k)

        def left(k):
            return pick(left_w, left_r, k)

        def cross(k):
            return pick(cross_w, cross_r, k)

        barrier = pltpu.get_barrier_semaphore()

        def greet(target):
            pl.semaphore_signal(barrier, inc=1, device_id=target, device_id_type=MESH)

        for k in range(1, size):
            greet({"segment": role, "dp": lax.rem(dp + k, size)})
        waits = size - 1
        if role < 2:
            greet(device(1 - role, place, core))
            waits += 1
        else:
            for k in range(size):
                greet({"segment": other, "dp": lax.rem(dp + k, size)})
            waits += size
        if role > 0:
            greet(device(0, place, role % 2))
        else:
            waits += 2 + 2 * core
        pl.semaphore_wait(barrier, waits)

        def each_part(act_local, act_remote):
            for j in range(2):
                segment = core + 2 * j
                for mb in range(MB):
                    src, dst = fin.at[mb, pl.ds(j * BLK, BLK)], out_g.at[mb // 2]
                    here = (segment == 0) & (core == mb % 2)
                    local = pltpu.make_async_copy(src, dst, fin_send.at[mb, j])
                    there = remote(
                        src, dst, fin_send.at[mb, j], fin_recv.at[mb // 2],
                        device(segment, place, mb % 2),
                    )
                    pl.when(here)(functools.partial(act_local, local))
                    pl.when(jnp.logical_not(here))(functools.partial(act_remote, there))

        if role == 0:
            each_part(lambda x: x.start(), lambda x: x.start())

        partner = device(role, place, 1 - core)
        mates = [dma, dmf] if role % 2 == 0 else [dmf, dma]
        mates = mates[: 2 if second else 1]
        def nears(k, z):
            array, base = parts[k]
            return remote(
                array.at[base + 2 * z + 1 - core], near(k).at[z], near_send.at[k, z],
                near_recv.at[k, z], partner,
            )

        for k in sorted(parts, reverse=True):
            array, base = parts[k]
            for z in range(chips):
                nears(k, z).start()
                pltpu.make_async_copy(
                    array.at[base + 2 * z + core], total(k).at[z], load_sem.at[k, z]
                ).start()
        small = []
        for n, rows in enumerate(mates):
            for k in range(2):
                move = remote(
                    rows.at[2 * k + 1 - core], dm_near.at[n, k], dm_send.at[n, k],
                    dm_recv.at[n, k], partner,
                )
                move.start()
                small.append(move)
                load = pltpu.make_async_copy(rows.at[2 * k + core], dm_own.at[n, k], dm_load.at[n, k])
                load.start()
                small.append(load)
        load = pltpu.make_async_copy(mod, modv, dm_load.at[2, 0])
        load.start()
        small.append(load)

        def nth(p):
            near_end = jnp.minimum(place, chips - 1 - place)
            lead = chips - 1 - 2 * near_end
            rest = p - lead
            z = jnp.where(
                rest < 0, chips - 1 - p,
                jnp.where(lax.rem(rest, 2) == 0, 2 * near_end - lax.div(rest, 2), lax.div(rest, 2)),
            )
            return jnp.where(place > chips - 1 - place, chips - 1 - z, z)

        def in_turn(body):
            def turn_at(p, carry):
                z = nth(p)
                pl.when(z > place)(lambda: body(p, z, 1))
                pl.when(z < place)(lambda: body(p, z, -1))
                return carry

            lax.fori_loop(0, chips - 1, turn_at, 0)

        at_end = (place == 0) | (place == chips - 1)

        def line_sent(z):
            for k in range(kept):
                remote(
                    total(k).at[z], right(k).at[z], line_send.at[k, z], right_recv.at[k, z], partner
                ).wait_send()

        def near_add(k, z):
            nears(k, z).wait()
            pltpu.make_async_copy(total(k).at[z], total(k).at[z], load_sem.at[k, z]).wait()
            total(k)[z] = total(k)[z] + near(k)[z]

        def crossing(k, z):
            return remote(
                total(kept + k).at[z], cross(k).at[z], cross_send.at[k, z], cross_recv.at[k, z],
                device(other, place, core),
            )

        def cross_start(z):
            for k in give:
                near_add(kept + k, z)
                crossing(k, z).start()

        def cross_sent(z):
            for k in give:
                crossing(k, z).wait_send()

        cross_start(nth(0))
        for k in (0, 1):
            for z in range(chips):
                if k in parts:
                    near_add(k, z)

        for move in small:
            move.wait()
        for n in range(len(mates)):
            for k in range(2):
                dm_tot[n, k] = dm_own[n, k] + dm_near[n, k]
                dm_tot[n, k, 4:5, :] = modv[k, 4:5, :]

        def column_move(n, k, slot):
            return remote(
                dm_tot.at[n], gathered.at[n, slot], g_send.at[n, k], g_recv.at[n, slot],
                {"segment": role if n == 0 else other, "dp": lax.rem(dp + k, size)},
            )

        for n in range(len(mates)):
            for k in range(1 - n, size):
                column_move(n, k, dp).start()
        mine = pltpu.make_async_copy(dm_tot.at[0], gathered.at[0, dp], dm_load.at[2, 1])
        mine.start()

        def settle(k, z):
            if k in taken:
                crossing(k, z).wait_recv()
                total(k)[z] = total(k)[z] + cross(k)[z] if k in parts else cross(k)[z]

        def forward(p, z, by):
            line, recv = (right, right_recv) if by > 0 else (left, left_recv)
            first = place == (0 if by > 0 else chips - 1)
            target = device(role, place + by, core)
            cross_sent(z)
            cross_start(nth(p + 1))
            pl.when(at_end & (p > 0))(lambda: line_sent(nth(p - 1)))
            for k in range(kept):
                settle(k, z)
                here = remote(line(k).at[z], line(k).at[z], line_send.at[k, z], recv.at[k, z], target)
                start = remote(total(k).at[z], line(k).at[z], line_send.at[k, z], recv.at[k, z], target)
                pl.when(first)(start.start)

                @pl.when(jnp.logical_not(first))
                def _():
                    here.wait_recv()
                    line(k)[z] = line(k)[z] + total(k)[z]
                    here.start()

        in_turn(forward)
        cross_sent(place)
        for k in range(kept):
            settle(k, place)

        def result(k):
            return res_r if k else res_w

        for k in range(kept):
            result(k)[...] = total(k)[place].astype(f32)
            for line, recv, edge in ((right, right_recv, 0), (left, left_recv, chips - 1)):

                @pl.when(place != edge)
                def _():
                    remote(
                        line(k).at[place], line(k).at[place], line_send.at[k, 0],
                        recv.at[k, place], partner,
                    ).wait_recv()
                    result(k)[...] += line(k)[place].astype(f32)

        outs = [
            pltpu.make_async_copy(res_w, first_out, load_sem.at[0, 0]),
            pltpu.make_async_copy(res_r, rows_out, load_sem.at[1, 0]),
        ]
        for copy in outs:
            copy.start()
        pl.when(at_end)(lambda: line_sent(nth(chips - 2)))
        pl.when(jnp.logical_not(at_end))(lambda: in_turn(lambda p, z, by: line_sent(z)))
        mine.wait()
        for n in range(len(mates)):
            for k in range(1 - n, size):
                column_move(n, k, dp).wait_send()
                column_move(n, k, lax.rem(dp + k, size)).wait_recv()
        for copy in outs:
            copy.wait()
        if role == 0:
            each_part(lambda x: x.wait(), lambda x: x.wait_send())
        for k in range(2):
            remote(
                fin.at[0, pl.ds(0, BLK)], out_g.at[k], fin_send.at[0, 0], fin_recv.at[k], partner
            ).wait_recv() if role > 0 else pl.when(core != 0)(
                remote(
                    fin.at[0, pl.ds(0, BLK)], out_g.at[k], fin_send.at[0, 0], fin_recv.at[k], partner
                ).wait_recv
            )

    for role in range(4):
        pl.when(seg == role)(functools.partial(work, role))


def sums(att, up, down, dma, dmf, mod, fin, chips):
    wide, rows = att.shape[1:], down.shape[1:]

    def sems(*dims):
        return pltpu.SemaphoreType.DMA(dims)

    each = sems(4, chips)
    return pl.pallas_call(
        functools.partial(sums_kernel, chips),
        out_shape=[
            jax.ShapeDtypeStruct(wide, f32), jax.ShapeDtypeStruct(rows, f32),
            jax.ShapeDtypeStruct((2, 2 * chips, 2, 8, D), f32), OWNED,
        ],
        in_specs=[ANY] * 7,
        out_specs=[ANY] * 4,
        scratch_shapes=[
            vm((2, chips, *wide)), vm((2, chips, *rows)), vm((2, chips, *wide)), vm((2, chips, *rows)),
            vm((1, chips, *wide)), vm((1, chips, *rows)),
            vm((1, chips, *wide)), vm((1, chips, *rows)), vm((1, chips, *wide)), vm((1, chips, *rows)),
            vm(wide, f32), vm(rows, f32),
            vm((2, 2, 8, D), f32), vm((2, 2, 8, D), f32), vm((2, 2, 8, D), f32), vm((2, 8, D), f32),
            each, each, each, each, each, each, each, each, sems(3, 2),
            sems(2, 2), sems(2, 2), sems(2, 2 * chips), sems(2, 2 * chips), sems(MB, 2), sems(2),
        ],
        compiler_params=pltpu.CompilerParams(
            vmem_limit_bytes=VLIM, collective_id=1, has_side_effects=True
        ),
        name="gradient_sums",
    )(att, up, down, dma, dmf, mod, fin)


ATT_F, FF_F, FF_B, ATT_B = range(4)


def chain_kernel(
    xs, cs, w, rows2, cos, sin, mod,
    xa, st, kv, lse, y, yf, act, dma, dmf, out_x, fin,
    wa, w1, w2, xv, nv, kvv, vv, inbox, qv, atv, bra, n1, brf, gbv, dov, dqv, xo, ov, fv, lv, cv, sv,
    dkt, dvt, rcvv, dpv, duv, actv, accv, dmv, zerov, moda, modf,
    w_send, w_recv, wf_send, wf_recv, x_send, x_recv, row_recv, fwd_send, fwd_recv, c_send, c_recv,
    push_sem, dkv_send, dkv_recv, mod_send, mod_recv, far_send, far_recv, fin_send, out_recv, ld, osem,
):
    role, dp = lax.axis_index("segment"), lax.axis_index("dp")
    c, place = lax.rem(dp, 2), lax.div(dp, 2)
    quarter, half_d = FF // 4, D // 2

    def device(segment, core):
        return {"segment": segment, "dp": 2 * place + core}

    def remote(src, dst, send, recv, target):
        return pltpu.make_async_remote_copy(
            src_ref=src, dst_ref=dst, send_sem=send, recv_sem=recv, device_id=target,
            device_id_type=MESH,
        )

    def local_copy(src, dst, sem):
        return pltpu.make_async_copy(src, dst, sem)

    partner = device(role, 1 - c)

    def rows_at(start, size):
        return pl.ds(pl.multiple_of(start, size), size)

    barrier = pltpu.get_barrier_semaphore()
    for k in range(1, 8):
        to = lax.rem(role * 2 + c + k, 8)
        pl.semaphore_signal(
            barrier, inc=1, device_id=device(lax.div(to, 2), lax.rem(to, 2)), device_id_type=MESH
        )
    pl.semaphore_wait(barrier, 7)

    tables = [local_copy(cos, cv, ld.at[0]), local_copy(sin, sv, ld.at[1])]
    for copy in tables:
        copy.start()

    def give_x(k):
        return remote(xs.at[k], xa.at[2 * k + c], x_send.at[k], x_recv.at[k], partner)

    def keep_x(k):
        return local_copy(xs.at[k], xa.at[2 * k + c], ld.at[4 + k])

    w_half = rows_at(c * half_d, half_d)
    rows_half = rows_at(c * quarter, quarter)
    high_half = rows_at(2 * quarter + c * quarter, quarter)

    def give_rows(dst, target):
        return remote(rows2.at[rows_half], w2.at[dst], w_send.at[1], w_recv.at[1], device(target, c))

    def give_w(dst, target):
        return remote(w.at[w_half], dst.at[w_half], w_send.at[0], w_recv.at[0], device(target, c))

    def keep_mod(k, dst):
        return local_copy(mod.at[k], dst.at[2 * k + c], ld.at[9 + k])

    def give_mod(k, dst):
        return remote(mod.at[k], dst.at[2 * k + c], mod_send.at[k], mod_recv.at[k], partner)

    def far_mod(k, dst, segment, core):
        return remote(
            mod.at[k], dst.at[2 * k + c], far_send.at[k, core], far_recv.at[k, c],
            device(segment, core),
        )

    def share_mod(dst):
        for k in range(2):
            keep_mod(k, dst).start()
            give_mod(k, dst).start()

    def shared_mod(dst):
        for k in range(2):
            keep_mod(k, dst).wait()
            give_mod(k, dst).wait()

    def give_c(k, j):
        return remote(
            cs.at[k, block_rows(1 - c + 2 * j)], inbox.at[4 + k, pl.ds(j * BLK, BLK)],
            c_send.at[k, j], c_recv.at[k, j], partner,
        )

    def keep_c(k, j):
        return local_copy(
            cs.at[k, block_rows(c + 2 * j)], inbox.at[4 + k, pl.ds(j * BLK, BLK)],
            ld.at[4 + 2 * k + j],
        )

    def forward_w(dst):
        return remote(dst.at[w_half], dst.at[w_half], wf_send.at[0], wf_recv.at[0], partner)

    def forward_rows(dst):
        return remote(w2.at[dst], w2.at[dst], wf_send.at[1], wf_recv.at[1], partner)

    def settle(given, passed):
        given.wait_recv()
        passed.start()
        passed.wait()

    @pl.when(role == 0)
    def _():
        share_mod(moda)
        for k in range(2):
            give_x(k).start()
            keep_x(k).start()
        give_rows(rows_half, 1).start()
        load = local_copy(w, wa, ld.at[2])
        load.start()
        for k in range(2):
            keep_x(k).wait()
        shared_mod(moda)
        load.wait()

    @pl.when(role == 1)
    def _():
        share_mod(modf)
        loads = [
            local_copy(w, w1, ld.at[2]),
            local_copy(rows2, w2.at[pl.ds(2 * quarter, 2 * quarter)], ld.at[8]),
        ]
        for copy in loads:
            copy.start()
        settle(give_rows(rows_half, 1), forward_rows(rows_half))
        shared_mod(modf)
        for copy in loads:
            copy.wait()

    for who in (2, 3):

        @pl.when(role == who)
        def _():
            other = 5 - who
            mine, mod_mine = (wa, moda) if who == 2 else (w1, modf)
            there = rows_half if who == 2 else high_half
            share_mod(mod_mine)
            for k in range(2):
                for core in range(2):
                    far_mod(k, mod_mine, other, core).start()
            give_w(mine, other).start()
            give_rows(there, other).start()
            loads = [
                local_copy(w, mine, ld.at[2]),
                local_copy(
                    rows2, w2.at[pl.ds(0 if who == 2 else 2 * quarter, 2 * quarter)], ld.at[8]
                ),
            ]
            for copy in loads:
                copy.start()

            @pl.when(c == who - 2)
            def _():
                for k in range(2):
                    for j in range(2):
                        give_c(k, j).start()
                        keep_c(k, j).start()
                for k in range(2):
                    for j in range(2):
                        keep_c(k, j).wait()

            shared_mod(mod_mine)
            for copy in loads:
                copy.wait()

    def prepare(step):
        for who in (2, 3):
            other = 5 - who
            theirs, mod_theirs = (w1, modf) if who == 2 else (wa, moda)
            here = high_half if who == 2 else rows_half

            @pl.when((role == who) & (step == 3 - who))
            def _():
                settle(give_w(theirs, other), forward_w(theirs))
                for k in range(2):
                    for core in range(2):
                        remote(
                            mod.at[k], mod_theirs.at[2 * k + core], far_send.at[k, core],
                            far_recv.at[k, core], partner,
                        ).wait_recv()

            @pl.when((role == who) & (step == 1))
            def _():
                settle(give_rows(here, other), forward_rows(here))

    for copy in tables:
        copy.wait()

    def kind_of(step):
        first = step < 4
        return jnp.where(
            role == 0, jnp.where(first, ATT_F, ATT_B),
            jnp.where(role == 1, jnp.where(first, FF_F, FF_B), lax.rem(step, 4)),
        )

    def place_of(step):
        return jnp.where(role < 2, lax.rem(step, 4), lax.div(step, 4) * 2 + role - 2)

    def slot_rows(mb):
        n = jnp.where(role < 2, mb, lax.div(mb, 2))
        return lax.div(n, 2), pl.ds(pl.multiple_of(lax.rem(n, 2) * HALF, HALF), HALF)

    def x_rows(mb, b):
        slot = 2 * lax.div(mb, 2) + lax.div(b, 2)
        return inbox.at[slot, block_rows(lax.rem(b, 2))]

    def stores(kind, mb):
        half, spot = slot_rows(mb)
        if kind == ATT_F:
            kept = [
                (qv, st.at[QS, half, spot]), (kvv, kv.at[0, mb]), (vv, kv.at[1, mb]),
                (bra, st.at[BR, half, spot]), (lv, lse.at[mb]),
            ]
            return [(atv, st.at[AT, half, spot])], kept, role == 0
        if kind == FF_F:
            return [], [(brf, st.at[BF, half, spot])], role == 1
        if kind == FF_B:
            rows = [
                (n1, st.at[NF, half, spot]), (gbv, st.at[GB, half, spot]),
                (duv, yf.at[half, spot]), (actv, act.at[half, spot]), (dmv, dmf.at[mb]),
            ]
            return rows, [(zerov, dmf.at[mb + 1 - 2 * lax.rem(mb, 2)])], role >= 2
        rows = [
            (gbv, y.at[half, spot, pl.ds(3 * D, D)]), (dpv, y.at[half, spot, pl.ds(0, 3 * D)]),
            (n1, st.at[NM, half, spot]), (dmv, dma.at[mb]),
        ]
        return rows, [(zerov, dma.at[mb + 1 - 2 * lax.rem(mb, 2)])], role >= 2

    def copies(kind, mb):
        always, sometimes, when = stores(kind, mb)
        first = [local_copy(a, b, osem.at[k]) for k, (a, b) in enumerate(always)]
        rest = [local_copy(a, b, osem.at[len(always) + k]) for k, (a, b) in enumerate(sometimes)]
        return first, rest, when

    def store(kind, mb):
        first, rest, when = copies(kind, mb)
        for copy in first:
            copy.start()

        @pl.when(when)
        def _():
            for copy in rest:
                copy.start()

        if kind == ATT_B:
            pl.when(role == 0)(lambda: local_copy(ov, fin.at[mb], osem.at[5]).start())

    def wait_stored(step):
        kind_then, mb = kind_of(step), place_of(step)
        for kind in (ATT_F, FF_F, FF_B, ATT_B):

            @pl.when((step >= 0) & (kind_then == kind))
            def _():
                first, rest, when = copies(kind, mb)
                for copy in first:
                    copy.wait()

                @pl.when(when)
                def _():
                    for copy in rest:
                        copy.wait()

                if kind == ATT_B:
                    pl.when(role == 0)(lambda: local_copy(ov, fin.at[mb], osem.at[5]).wait())

    def wait_pushed(step):
        went = (
            ((role == 0) & (step < 4)) | (role == 1) | ((role >= 2) & (lax.rem(step, 4) == 3))
        ) & (step >= 0)

        @pl.when(went)
        def _():
            for j in range(2):
                at = pl.ds(j * BLK, BLK)
                remote(
                    ov.at[at], inbox.at[0, at], push_sem.at[j], row_recv.at[0, j], partner
                ).wait_send()

    def free(step):
        wait_pushed(step - 1)
        wait_stored(step - 1)

    def push(j, slot, rows, segment):
        remote(
            ov.at[block_rows(j)], inbox.at[slot, rows], push_sem.at[j], row_recv.at[slot, j],
            device(segment, c),
        ).start()

    def arrived(slot, j):
        at = block_rows(j)
        remote(
            ov.at[at], inbox.at[slot, at], push_sem.at[j], row_recv.at[slot, j], partner
        ).wait_recv()

    def spread(j, mb):
        segment, owner = c + 2 * j, lax.rem(mb, 2)
        here = (role == segment) & (c == owner)
        rows, k = block_rows(j), lax.div(mb, 2)

        @pl.when(here)
        def _():
            local_copy(fv.at[rows], out_x.at[k], fin_send.at[j]).start()

        @pl.when(jnp.logical_not(here))
        def _():
            remote(
                fv.at[rows], out_x.at[k], fin_send.at[j], out_recv.at[k], device(segment, owner)
            ).start()

    def wait_spread(mb):
        for j in range(2):
            here = (role == c + 2 * j) & (c == lax.rem(mb, 2))
            rows = pl.ds(j * BLK, BLK)

            @pl.when(here)
            def _():
                local_copy(fv.at[rows], out_x.at[0], fin_send.at[j]).wait()

            @pl.when(jnp.logical_not(here))
            def _():
                remote(
                    fv.at[rows], out_x.at[0], fin_send.at[j], out_recv.at[0], partner
                ).wait_send()

    def att_f(step, mb):
        length = moda[mb, 3:4, 0:1]
        off, scl, gat = moda[mb, 0:1, :], 1.0 + moda[mb, 1:2, :], moda[mb, 2:3, :]

        @pl.when(role == 0)
        def _():
            @pl.when(lax.rem(mb, 2) != c)
            def _():
                k = lax.div(mb, 2)
                remote(xs.at[0], xa.at[mb], x_send.at[0], x_recv.at[k], partner).wait_recv()

            load = local_copy(xa.at[mb], xv, ld.at[0])
            load.start()
            free(step)
            load.wait()

        def forward(j):
            rows = x_rows(mb, c + 2 * j)
            k = 2 * lax.div(mb, 2) + j
            return remote(rows, rows, fwd_send.at[j], fwd_recv.at[k], partner)

        @pl.when(role != 0)
        def _():
            for j in range(2):
                rows = x_rows(mb, c + 2 * j)
                remote(
                    ov.at[pl.ds(j * BLK, BLK)], rows, push_sem.at[j],
                    row_recv.at[2 * lax.div(mb, 2) + j, c], partner,
                ).wait_recv()
                forward(j).start()
            free(step)

        def kv_block(b, carry):
            rows = block_rows(b)

            @pl.when(role != 0)
            def _():
                j, there = lax.div(b, 2), lax.rem(b, 2) != c

                @pl.when(there)
                def _():
                    at = x_rows(mb, b)
                    remote(
                        at, at, fwd_send.at[0], fwd_recv.at[2 * lax.div(mb, 2) + j], partner
                    ).wait_recv()

                slot = 2 * lax.div(mb, 2) + j
                xv[rows, :] = inbox[slot, block_rows(lax.rem(b, 2)), :]

            norm, _ = norm_parts(xv[rows, :].astype(f32))
            n = (norm * scl + off).astype(bf16)
            nv[rows, :] = n
            cosine, sine = cv[rows, :], sv[rows, :]
            kk = dot(n, wa[:, D : 2 * D])
            for p in range(6):
                ls = slice(p * 128, (p + 1) * 128)
                kvv[rows, ls] = turn(kk[:, ls], cosine, sine).astype(bf16)
            vv[rows, :] = dot(n, wa[:, 2 * D : 3 * D]).astype(bf16)
            return carry

        lax.fori_loop(0, 4, kv_block, 0)

        @pl.when(role != 0)
        def _():
            for j in range(2):
                forward(j).wait_send()

        def q_block(j, carry):
            nat = block_rows(c + 2 * j)
            rows = block_rows(j)
            cosine, sine = cv[nat, :] * 0.125, sv[nat, :] * 0.125
            qq = dot(nv[nat, :], wa[:, 0:D])
            for p in range(6):
                ls = slice(p * 128, (p + 1) * 128)
                qv[rows, ls] = turn(qq[:, ls], cosine, sine).astype(bf16)
            return carry

        lax.fori_loop(0, 2, q_block, 0)
        lane = lax.broadcasted_iota(i32, (BLK, 128), 1)
        position = lax.broadcasted_iota(i32, (1, SEQ_LEN), 1).astype(f32)
        bias = jnp.where(position < length, 0.0, -1e30).astype(f32)
        lv[...] = jnp.zeros((HALF, 128), f32)

        def block(j, carry):
            rows = block_rows(j)

            def pair(hp, carry):
                ls = lanes(hp)
                k2, v2, q2 = kvv[:, ls], vv[:, ls], qv[rows, ls]
                outs, stats = [], lv[rows, :]
                for a in range(2):
                    s = dot_nt(jnp.where((lane < 64) == (a == 0), q2, jnp.zeros_like(q2)), k2)
                    s = s + bias
                    m = jnp.max(s, axis=1, keepdims=True)
                    e = jnp.exp(s - m)
                    total = jnp.sum(e, axis=1, keepdims=True)
                    outs.append(dot(e.astype(bf16), v2) / total)
                    stats = jnp.where(lane == 2 * hp + a, m + jnp.log(total), stats)
                atv[rows, ls] = jnp.where(lane < 64, outs[0], outs[1]).astype(bf16)
                lv[rows, :] = stats
                return carry

            lax.fori_loop(0, HEADS // 2, pair, 0)
            branch = dot(atv[rows, :], wa[:, 3 * D : 4 * D])
            live = live_column(c, length, j)
            x = xv[block_rows(c + 2 * j), :].astype(f32)
            out = (x + jnp.where(live, gat * branch, 0.0)).astype(bf16)
            bra[rows, :] = branch.astype(bf16)

            @pl.when(role == 0)
            def _():
                ov[rows, :] = out
                push(j, mb, rows, 1)

            @pl.when(role != 0)
            def _():
                inbox[6, rows, :] = out

            return carry

        lax.fori_loop(0, 2, block, 0)
        store(ATT_F, mb)

    def ff_f(step, mb):
        length = modf[mb, 3:4, 0:1]
        off, scl, gat = modf[mb, 0:1, :], 1.0 + modf[mb, 1:2, :], modf[mb, 2:3, :]
        slot = jnp.where(role == 1, mb, 6)
        pl.when((role >= 2) & (step >= 4))(lambda: wait_spread(mb))
        pl.when(role == 1)(lambda: arrived(mb, 0))
        free(step)

        def block(j, carry):
            rows = block_rows(j)
            pl.when((role == 1) & (j > 0))(lambda: arrived(mb, j))
            norm, _ = norm_parts(inbox[slot, rows, :].astype(f32))
            n1[rows, :] = (norm * scl + off).astype(bf16)
            accv[rows, :] = jnp.zeros((BLK, D), f32)

            def part(p, carry):
                at = pl.ds(pl.multiple_of(p * D, D), D)
                u = dot(n1[rows, :], w1[:, at])
                t, _ = gelu_parts(u)
                accv[rows, :] += dot((0.5 * u * (1.0 + t)).astype(bf16), w2[at, :])
                return carry

            lax.fori_loop(0, 4, part, 0)
            acc = accv[rows, :]
            live = live_column(c, length, j)
            x = inbox[slot, rows, :].astype(f32)
            out = (x + jnp.where(live, gat * acc, 0.0)).astype(bf16)
            brf[rows, :] = acc.astype(bf16)

            @pl.when(role != 1)
            def _():
                fv[rows, :] = out
                spread(j, mb)

            @pl.when(role == 1)
            def _():
                ov[rows, :] = out
                slot_there = 2 * lax.div(mb, 2) + j
                remote(
                    ov.at[rows], inbox.at[slot_there, block_rows(c)], push_sem.at[j],
                    row_recv.at[slot_there, c], device(2 + lax.rem(mb, 2), c),
                ).start()

            return carry

        lax.fori_loop(0, 2, block, 0)
        store(FF_F, mb)

    def ff_b(step, mb):
        length = modf[mb, 3:4, 0:1]
        off, scl, gat = modf[mb, 0:1, :], 1.0 + modf[mb, 1:2, :], modf[mb, 2:3, :]
        slot = jnp.where(role == 1, mb, 6)
        from_slot = jnp.where(role == 1, 4 + mb, 4 + lax.div(mb, 2))

        def wait_rows(j):
            pl.when(role == 1)(lambda: arrived(4 + mb, j))

            @pl.when((role != 1) & (lax.rem(mb, 2) != c))
            def _():
                at = block_rows(j)
                remote(
                    ov.at[at], inbox.at[from_slot, at], push_sem.at[j],
                    c_recv.at[lax.div(mb, 2), j], partner,
                ).wait_recv()

        wait_rows(0)
        free(step)

        @pl.when(role == 1)
        def _():
            half, spot = slot_rows(mb)
            load = local_copy(st.at[BF, half, spot], brf, ld.at[1])
            load.start()
            load.wait()

        dmv[...] = jnp.zeros((8, D), f32)

        def block(j, carry):
            rows = block_rows(j)
            pl.when(j > 0)(lambda: wait_rows(j))
            norm, _ = norm_parts(inbox[slot, rows, :].astype(f32))
            n1[rows, :] = (norm * scl + off).astype(bf16)
            live = live_column(c, length, j)
            gl = jnp.where(live, inbox[from_slot, rows, :].astype(f32), 0.0)
            gbv[rows, :] = (gl * gat).astype(bf16)
            dmv[2:3, :] += jnp.sum(gl * brf[rows, :].astype(f32), axis=0, keepdims=True)
            accv[rows, :] = jnp.zeros((BLK, D), f32)

            def part(p, carry):
                cols = pl.ds(pl.multiple_of(p * D, D), D)
                u = dot(n1[rows, :], w1[:, cols])
                t, u2 = gelu_parts(u)
                half = 0.5 * (1.0 + t)
                actv[rows, cols] = (u * half).astype(bf16)
                slope = half + 0.5 * u * (1.0 - t * t) * (
                    0.7978845608028654 * (1.0 + 3 * 0.044715 * u2)
                )
                du = (dot_nt(gbv[rows, :], w2[cols, :]) * slope).astype(bf16)
                duv[rows, cols] = du
                accv[rows, :] += dot_nt(du, w1[:, cols])
                return carry

            lax.fori_loop(0, 4, part, 0)
            acc = accv[rows, :]
            n, rstd = norm_parts(inbox[slot, rows, :].astype(f32))
            dmv[0:1, :] += jnp.sum(acc, axis=0, keepdims=True)
            dmv[1:2, :] += jnp.sum(acc * n, axis=0, keepdims=True)
            out = (
                inbox[from_slot, rows, :].astype(f32) + norm_back(acc, n, rstd, scl)
            ).astype(bf16)

            @pl.when(role == 1)
            def _():
                ov[rows, :] = out
                push(j, mb, rows, 0)

            @pl.when(role != 1)
            def _():
                inbox[7, rows, :] = out

            return carry

        lax.fori_loop(0, 2, block, 0)
        store(FF_B, mb)

    def att_b(step, mb):
        length = moda[mb, 3:4, 0:1]
        off, scl, gat = moda[mb, 0:1, :], 1.0 + moda[mb, 1:2, :], moda[mb, 2:3, :]
        slot = jnp.where(role == 0, mb, 7)
        half, spot = slot_rows(mb)
        turn_of = jnp.where(role == 0, lax.rem(mb, 2), lax.div(mb, 2))
        loads = [
            local_copy(st.at[QS, half, spot], qv, ld.at[0]),
            local_copy(kv.at[0, mb], kvv, ld.at[1]),
            local_copy(kv.at[1, mb], vv, ld.at[2]),
            local_copy(st.at[AT, half, spot], atv, ld.at[3]),
            local_copy(lse.at[mb], lv, ld.at[4]),
            local_copy(st.at[BR, half, spot], bra, ld.at[5]),
        ]
        for j in range(2):
            loads.append(
                local_copy(
                    xa.at[mb, block_rows(c + 2 * j)], xo.at[pl.ds(j * BLK, BLK)], ld.at[6 + j]
                )
            )
        free(step)

        @pl.when(role == 0)
        def _():
            for copy in loads:
                copy.start()

        dmv[...] = jnp.zeros((8, D), f32)

        def grad_block(j, carry):
            rows = block_rows(j)
            pl.when(role == 0)(lambda: arrived(mb, j))

            @pl.when(role != 0)
            def _():
                xo[rows, :] = inbox[2 * lax.div(mb, 2) + j, block_rows(c), :]

            live = live_column(c, length, j)
            gb = jnp.where(live, inbox[slot, rows, :].astype(f32) * gat, 0.0).astype(bf16)
            gbv[rows, :] = gb
            dov[rows, :] = dot_nt(gb, wa[:, 3 * D : 4 * D]).astype(bf16)
            return carry

        lax.fori_loop(0, 2, grad_block, 0)

        @pl.when(role == 0)
        def _():
            for copy in loads:
                copy.wait()

        lane = lax.broadcasted_iota(i32, (HALF, 128), 1)
        position = lax.broadcasted_iota(i32, (1, SEQ_LEN), 1).astype(f32)
        bias = jnp.where(position < length, 0.0, -1e30).astype(f32)

        def pair(hp, carry):
            ls = lanes(hp)
            k2, v2 = kvv[:, ls], vv[:, ls]
            q2, do2 = qv[:, ls], dov[:, ls]
            q2t, do2t = q2.T, do2.T
            both = do2.astype(f32) * atv[:, ls].astype(f32)
            stats = lv[...]
            dqs = []
            for a in range(2):
                head = (lane < 64) == (a == 0)
                zero = jnp.zeros_like(q2)
                s = dot_nt(jnp.where(head, q2, zero), k2) + bias
                base = jnp.sum(jnp.where(lane == 2 * hp + a, stats, 0.0), axis=1, keepdims=True)
                p = jnp.exp(s - base)
                dp_ = dot_nt(jnp.where(head, do2, zero), v2)
                delta = jnp.sum(jnp.where(head, both, 0.0), axis=1, keepdims=True)
                ds = (p * (dp_ - delta)).astype(bf16)
                dqs.append(dot(ds, k2))
                at = pl.ds(pl.multiple_of(hp * 128 + a * 64, 64), 64)
                dkt[at, :] = dot(q2t[a * 64 : (a + 1) * 64, :], ds).astype(bf16)
                dvt[at, :] = dot(do2t[a * 64 : (a + 1) * 64, :], p.astype(bf16)).astype(bf16)
            dqv[:, ls] = jnp.where(lane < 64, dqs[0], dqs[1]).astype(bf16)
            for part, grad in enumerate((dkt, dvt)):
                for j in range(2):
                    give_pair(hp, part, j).start()
            return carry

        def give_pair(hp, part, j):
            grad = (dkt, dvt)[part]
            return remote(
                grad.at[lanes(hp), block_rows(1 - c + 2 * j)],
                rcvv.at[turn_of, part, lanes(hp), pl.ds(j * BLK, BLK)],
                dkv_send.at[hp, part, j], dkv_recv.at[turn_of, hp, part, j], partner,
            )

        lax.fori_loop(0, HEADS // 2, pair, 0)

        def settled(hp, carry):
            for part in range(2):
                for j in range(2):
                    give_pair(hp, part, j).wait()
            return carry

        def first(j, carry):
            rows, nat = block_rows(j), block_rows(c + 2 * j)
            cosine, sine = cv[nat, :], -sv[nat, :]
            for p in range(6):
                ls = slice(p * 128, (p + 1) * 128)
                dpv[rows, ls] = (turn(dqv[rows, ls].astype(f32), cosine, sine) * 0.125).astype(bf16)
            return carry

        lax.fori_loop(0, 2, first, 0)
        lax.fori_loop(0, HEADS // 2, settled, 0)

        def last(j, carry):
            rows, nat = block_rows(j), block_rows(c + 2 * j)
            cosine, sine = cv[nat, :], -sv[nat, :]
            for p in range(6):
                ls = slice(p * 128, (p + 1) * 128)
                for part, own in enumerate((dkt, dvt)):
                    total = own[ls, nat].astype(f32) + rcvv[turn_of, part, ls, rows].astype(f32)
                    grad = total.T
                    if part == 0:
                        grad = turn(grad.astype(bf16).astype(f32), cosine, sine)
                    dpv[rows, (part + 1) * D + p * 128 : (part + 1) * D + (p + 1) * 128] = (
                        grad.astype(bf16)
                    )
            acc = dot_nt(dpv[rows, :], wa[:, 0 : 3 * D])
            n, rstd = norm_parts(xo[rows, :].astype(f32))
            n1[rows, :] = (n * scl + off).astype(bf16)
            g = inbox[slot, rows, :].astype(f32)
            live = live_column(c, length, j)
            gl = jnp.where(live, g, 0.0)
            dmv[0:1, :] += jnp.sum(acc, axis=0, keepdims=True)
            dmv[1:2, :] += jnp.sum(acc * n, axis=0, keepdims=True)
            dmv[2:3, :] += jnp.sum(gl * bra[rows, :].astype(f32), axis=0, keepdims=True)
            ov[rows, :] = (g + norm_back(acc, n, rstd, scl)).astype(bf16)
            pl.when(role != 0)(lambda: push(j, 4 + mb, rows, 1))
            return carry

        lax.fori_loop(0, 2, last, 0)
        store(ATT_B, mb)

    def run(step, carry):
        kind, mb = kind_of(step), place_of(step)
        prepare(step)
        for which, work in ((ATT_F, att_f), (FF_F, ff_f), (FF_B, ff_b), (ATT_B, att_b)):
            pl.when(kind == which)(functools.partial(work, step, mb))
        return carry

    zerov[...] = jnp.zeros((8, D), f32)
    lax.fori_loop(0, 8, run, 0)
    free(8)
    pl.when(role >= 2)(lambda: wait_spread(role))

    @pl.when(role != c + 2)
    def _():
        for k in range(2):
            remote(
                fv.at[pl.ds(0, BLK)], out_x.at[k], fin_send.at[0], out_recv.at[k], partner
            ).wait_recv()

    @pl.when(role == 0)
    def _():
        for k in range(2):
            give_x(k).wait_send()
        give_rows(rows_half, 1).wait_send()

    for who in (2, 3):

        @pl.when(role == who)
        def _():
            other = 5 - who
            mine, mod_mine = (wa, moda) if who == 2 else (w1, modf)
            there = rows_half if who == 2 else high_half
            for k in range(2):
                for core in range(2):
                    far_mod(k, mod_mine, other, core).wait_send()
            give_w(mine, other).wait_send()
            give_rows(there, other).wait_send()

            @pl.when(c == who - 2)
            def _():
                for k in range(2):
                    for j in range(2):
                        give_c(k, j).wait_send()


def chain(xs, cs, w, rows2, cos, sin, mod):
    def sems(*dims):
        return pltpu.SemaphoreType.DMA(dims)

    table = vm((SEQ_LEN, 128), f32)
    outs = [
        shape((MB, SEQ_LEN, D)), ST, KV, LSE, YS, YS, YS, DM, DM, OWNED, shape((MB, HALF, D)),
    ]
    return pl.pallas_call(
        chain_kernel,
        out_shape=outs,
        in_specs=[ANY] * 7,
        out_specs=[ANY] * len(outs),
        scratch_shapes=[
            vm((D, FF)), vm((D, FF)), vm((FF, D)), FV, FV, FV, FV, vm((8, HALF, D)),
            HV, HV, HV, HV, HV, HV, HV, HV, HV, HV, HV, vm((HALF, 128), f32), table, table,
            vm((D, SEQ_LEN)), vm((D, SEQ_LEN)), vm((2, 2, D, HALF)), vm((HALF, 3 * D)),
            vm((HALF, FF)), vm((HALF, FF)), vm((HALF, D), f32), vm((8, D), f32), vm((8, D), f32),
            vm((MB, 8, D), f32), vm((MB, 8, D), f32),
            sems(3), sems(3), sems(2), sems(2), sems(2), sems(2), sems(8, 2), sems(2), sems(4),
            sems(2, 2), sems(2, 2), sems(2), sems(HEADS // 2, 2, 2), sems(2, HEADS // 2, 2, 2),
            sems(2), sems(2), sems(2, 2), sems(2, 2), sems(2), sems(2), sems(12), sems(6),
        ],
        compiler_params=pltpu.CompilerParams(
            vmem_limit_bytes=62 << 20, collective_id=0, has_side_effects=True
        ),
        cost_estimate=cost(300),
        name="layers",
    )(xs, cs, w, rows2, cos, sin, mod)


def time_cond(steps):
    half_width = D // 2
    frequency = jnp.exp(
        jnp.arange(half_width, dtype=f32) * (-math.log(10000.0) / half_width)
    )
    angles = steps.astype(f32)[:, None] * frequency[None, :]
    return jax.nn.silu(jnp.concatenate([jnp.cos(angles), jnp.sin(angles)], axis=1))


def rope_tables():
    inverse = np.exp(np.arange(32, dtype=np.float32) * np.float32(-math.log(10000.0) / 32))
    angles = np.arange(SEQ_LEN, dtype=np.float32)[:, None] * inverse[None, :]
    cosine, sine = np.cos(angles), np.sin(angles)
    return (
        np.concatenate([cosine] * 4, axis=1).astype(np.float32),
        np.concatenate([-sine, sine, -sine, sine], axis=1).astype(np.float32),
    )


def local(block_input, cotangent, lengths, steps, mod_weight, mod_bias, first_weight, down_rows):
    ndp = lax.axis_size("dp")
    seg, dp = lax.axis_index("segment"), lax.axis_index("dp")
    chips = ndp // 2
    w, rows2 = first_weight[0], down_rows[0]
    conditions = time_cond(steps).astype(bf16)
    modulation = jnp.dot(conditions, mod_weight[0], preferred_element_type=f32)
    modulation = (modulation + mod_bias[0].astype(f32)).reshape(2, 3, D)
    length = jnp.broadcast_to(lengths.astype(f32)[:, None, None], (2, 1, D))
    mod = jnp.concatenate(
        [modulation, length, conditions.astype(f32)[:, None], jnp.zeros((2, 3, D), f32)], axis=1
    )
    cos, sin = (jnp.asarray(t) for t in rope_tables())
    _, st, _, _, y, yf, act, dma, dmf, out_x, fin = chain(
        block_input, cotangent, w, rows2, cos, sin, mod
    )
    depth, wide_rows = D // ndp, FF // 2 // ndp

    def weight_grad(kind, roles, right):
        pairs = pltpu.SemaphoreType.DMA((2,))
        return pl.pallas_call(
            functools.partial(weight_grad_kernel, kind, roles),
            in_specs=[ANY, ANY],
            out_specs=ANY,
            scratch_shapes=[
                vm((2, SEQ_LEN, D)), vm((2, 2, SEQ_LEN, D)), vm((D, D), f32), vm((2, D, D)),
                pairs, pairs, pairs,
            ],
            out_shape=shape((FF, D) if kind == "down" else (D, FF)),
            compiler_params=pltpu.CompilerParams(vmem_limit_bytes=VLIM),
            cost_estimate=cost(12),
            name=kind + "_gradient",
        )(st, right)

    down = weight_grad("down", (1, 2, 3), act).reshape(2 * ndp, wide_rows, D)
    up = weight_grad("up", (1, 2, 3), yf).reshape(ndp, depth, FF)
    att = weight_grad("attention", (0, 2, 3), y).reshape(ndp, depth, FF)
    first_sum, rows_sum, rows, out_g = sums(att, up, down, dma, dmf, mod, fin, chips)

    rows = jnp.where((jnp.arange(2) == 1)[:, None, None, None, None] & (seg < 2), 0.0, rows)
    columns = rows[:, :, :, :3].reshape(4 * ndp, 3 * D)
    kept = rows[:, :, :, 4].reshape(4 * ndp, D)
    mine = lax.dynamic_slice_in_dim(kept, dp * depth, depth, axis=1)
    mod_w_sum = jnp.dot(
        mine.T, columns, precision=lax.Precision.HIGHEST, preferred_element_type=f32
    )
    width = 3 * D // ndp
    mod_b_sum = jnp.sum(lax.dynamic_slice_in_dim(columns, dp * width, width, axis=1), axis=0)

    live = (seg * BLK + jnp.arange(BLK))[None, :, None] < lengths[:, None, None]

    def placed(given, part):
        return jnp.where(live, given, lax.dynamic_slice_in_dim(part, seg * BLK, BLK, axis=1))

    return (
        placed(out_x, block_input),
        placed(out_g, cotangent).astype(f32),
        mod_w_sum[None],
        mod_b_sum[None],
        first_sum[None],
        rows_sum[None],
    )


def solution(mesh):
    in_specs = (
        P("dp", None, None),
        P("dp", None, None),
        P("dp"),
        P("dp"),
        P("segment", None, None),
        P("segment", None),
        P("segment", None, None),
        P("segment", None, None),
    )
    out_specs = (
        P("dp", "segment", None),
        P("dp", "segment", None),
        P("segment", "dp", None),
        P("segment", "dp"),
        P("segment", "dp", None),
        P("segment", "dp", None),
    )
    return jax.shard_map(local, mesh=mesh, in_specs=in_specs, out_specs=out_specs, check_vma=False)
```

```python
import functools
import math

import jax
import jax.numpy as jnp
import numpy as np
from jax import lax
from jax.experimental import pallas as pl
from jax.experimental.pallas import tpu as pltpu
from jax.sharding import PartitionSpec as P

D = 768
HEADS = 12
HEAD_DIM = 64
FF = 3072
SEQ_LEN = 1024
BLK = 256
HALF = SEQ_LEN // 2
MB = 4
QS, AT, BR, NM, BF, NF, GB = range(7)
VLIM = 56 << 20
bf16, f32, i32 = jnp.bfloat16, jnp.float32, jnp.int32


def dot(a, b):
    return lax.dot_general(a, b, (((1,), (0,)), ((), ())), preferred_element_type=f32)


def dot_nt(a, b):
    return lax.dot_general(a, b, (((1,), (1,)), ((), ())), preferred_element_type=f32)


def dot_tn(a, b):
    return lax.dot_general(a, b, (((0,), (0,)), ((), ())), preferred_element_type=f32)


def block_rows(b):
    return pl.ds(pl.multiple_of(b * BLK, BLK), BLK)


def lanes(p):
    return pl.ds(pl.multiple_of(p * 128, 128), 128)


def norm_parts(x):
    center = x - jnp.mean(x, axis=-1, keepdims=True)
    rstd = lax.rsqrt(jnp.mean(center * center, axis=-1, keepdims=True) + 1e-06)
    return center * rstd, rstd


def norm_back(d_normed, n, rstd, scl):
    dn = d_normed * scl
    return (
        dn - jnp.mean(dn, axis=-1, keepdims=True) - n * jnp.mean(dn * n, axis=-1, keepdims=True)
    ) * rstd


def turn(v, cosine, sine):
    lane = lax.broadcasted_iota(i32, v.shape, 1)
    partner = jnp.where(lane % 64 < 32, pltpu.roll(v, 96, 1), pltpu.roll(v, 32, 1))
    return v * cosine + partner * sine


def live_column(c, length, j):
    r = lax.broadcasted_iota(i32, (BLK, 1), 0) + BLK * (c + 2 * j)
    return r.astype(f32) < length


def gelu_parts(u):
    u2 = u * u
    t = jnp.tanh(0.7978845608028654 * (u * (1.0 + 0.044715 * u2)))
    return t, u2


def weight_grad_kernel(kind, roles, st, y, out, xv, yv, acc, ov, xsem, ysem, osem):
    role = lax.axis_index("segment")
    parts = jnp.where(role < 2, 2, 1)

    def tile(j):
        return y.at[:, :, pl.ds(pl.multiple_of(j * D, D), D)]

    def into(j):
        at = pl.ds(pl.multiple_of(j * D, D), D)
        return out.at[at] if kind == "down" else out.at[:, at]

    def load_x(which):
        return pltpu.make_async_copy(st.at[which], xv, xsem.at[0])

    def load_y(j):
        slot = lax.rem(j, 2)
        return pltpu.make_async_copy(tile(j), yv.at[slot], ysem.at[slot])

    def store(j):
        slot = lax.rem(j, 2)
        return pltpu.make_async_copy(ov.at[slot], into(j), osem.at[slot])

    chosen = functools.reduce(jnp.logical_or, [role == r for r in roles])

    @pl.when(chosen)
    def _():
        load_x(GB if kind == "down" else NM if kind == "attention" else NF).start()
        load_y(0).start()
        load_x(0).wait()

        def step(j, carry):
            slot = lax.rem(j, 2)
            pl.when(j < 3)(lambda: load_y(j + 1).start())
            load_y(j).wait()
            if kind == "attention":

                @pl.when(j == 3)
                def _():
                    load_x(AT).start()
                    load_x(AT).wait()

            def product(h):
                if kind == "down":
                    return dot_tn(yv[slot, h], xv[h])
                return dot_tn(xv[h], yv[slot, h])

            pl.when(j >= 2)(lambda: store(j - 2).wait())

            @pl.when(parts == 1)
            def _():
                ov[slot] = product(0).astype(bf16)

            @pl.when(parts == 2)
            def _():
                acc[...] = product(0)
                ov[slot] = (acc[...] + product(1)).astype(bf16)

            store(j).start()
            return carry

        lax.fori_loop(0, 4, step, 0)
        store(2).wait()
        store(3).wait()


ANY = pl.BlockSpec(memory_space=pl.ANY)
VMEM = pl.BlockSpec(memory_space=pltpu.VMEM)


def shape(dims, dtype=bf16):
    return jax.ShapeDtypeStruct(dims, dtype)


ST = shape((7, 2, SEQ_LEN, D))
KV = shape((2, MB, SEQ_LEN, D))
LSE = shape((MB, HALF, 128), f32)
YS = shape((2, SEQ_LEN, FF))
DM = shape((MB, 8, D), f32)
OWNED = shape((2, BLK, D))


def vm(dims, dtype=bf16):
    return pltpu.VMEM(dims, dtype)


HV, FV = vm((HALF, D)), vm((SEQ_LEN, D))


def cost(micros):
    return pl.CostEstimate(flops=int(micros * 1e9), bytes_accessed=1 << 20, transcendentals=0)


MESH = pl.DeviceIdType.MESH


def sums_kernel(
    chips, att, up, down, dma, dmf, mod, fin, first_out, rows_out, gathered, out_g,
    near_w, near_r, tot_w, tot_r, cross_w, cross_r, right_w, right_r, left_w, left_r, res_w, res_r,
    dm_own, dm_near, dm_tot, modv,
    load_sem, near_send, near_recv, cross_send, cross_recv, line_send, right_recv, left_recv,
    dm_load, dm_send, dm_recv, g_send, g_recv, fin_send, fin_recv,
):
    seg, dp = lax.axis_index("segment"), lax.axis_index("dp")
    core, place = lax.rem(dp, 2), lax.div(dp, 2)
    size = 2 * chips

    def device(segment, chip, at):
        return {"segment": segment, "dp": 2 * chip + at}

    def remote(src, dst, send, recv, target):
        return pltpu.make_async_remote_copy(
            src_ref=src, dst_ref=dst, send_sem=send, recv_sem=recv,
            device_id=target, device_id_type=MESH,
        )

    def work(role):
        other = 5 - role if role >= 2 else 1 - role
        second = role >= 2
        low, high = 0, size
        parts = {
            0: {0: (att, 0)},
            1: {0: (up, 0), 1: (down, high), 3: (down, low)},
            2: {0: (att, 0), 1: (down, low), 2: (up, 0), 3: (down, high)},
            3: {0: (up, 0), 1: (down, high), 2: (att, 0), 3: (down, low)},
        }[role]
        kept = 2
        give = [k for k in (0, 1) if k + 2 in parts]
        taken = {0: [1], 1: [], 2: [0, 1], 3: [0, 1]}[role]

        def pick(wide, rows, k):
            return (rows if k % 2 else wide).at[k // 2]

        def near(k):
            return pick(near_w, near_r, k)

        def total(k):
            return pick(tot_w, tot_r, k)

        def right(k):
            return pick(right_w, right_r, k)

        def left(k):
            return pick(left_w, left_r, k)

        def cross(k):
            return pick(cross_w, cross_r, k)

        barrier = pltpu.get_barrier_semaphore()

        def greet(target):
            pl.semaphore_signal(barrier, inc=1, device_id=target, device_id_type=MESH)

        for k in range(1, size):
            greet({"segment": role, "dp": lax.rem(dp + k, size)})
        waits = size - 1
        if role < 2:
            greet(device(1 - role, place, core))
            waits += 1
        else:
            for k in range(size):
                greet({"segment": other, "dp": lax.rem(dp + k, size)})
            waits += size
        if role > 0:
            greet(device(0, place, role % 2))
        else:
            waits += 2 + 2 * core
        pl.semaphore_wait(barrier, waits)

        def each_part(act_local, act_remote):
            for j in range(2):
                segment = core + 2 * j
                for mb in range(MB):
                    src, dst = fin.at[mb, pl.ds(j * BLK, BLK)], out_g.at[mb // 2]
                    here = (segment == 0) & (core == mb % 2)
                    local = pltpu.make_async_copy(src, dst, fin_send.at[mb, j])
                    there = remote(
                        src, dst, fin_send.at[mb, j], fin_recv.at[mb // 2],
                        device(segment, place, mb % 2),
                    )
                    pl.when(here)(functools.partial(act_local, local))
                    pl.when(jnp.logical_not(here))(functools.partial(act_remote, there))

        if role == 0:
            each_part(lambda x: x.start(), lambda x: x.start())

        partner = device(role, place, 1 - core)
        mates = [dma, dmf] if role % 2 == 0 else [dmf, dma]
        mates = mates[: 2 if second else 1]
        def nears(k, z):
            array, base = parts[k]
            return remote(
                array.at[base + 2 * z + 1 - core], near(k).at[z], near_send.at[k, z],
                near_recv.at[k, z], partner,
            )

        for k in sorted(parts, reverse=True):
            array, base = parts[k]
            for z in range(chips):
                nears(k, z).start()
                pltpu.make_async_copy(
                    array.at[base + 2 * z + core], total(k).at[z], load_sem.at[k, z]
                ).start()
        small = []
        for n, rows in enumerate(mates):
            for k in range(2):
                move = remote(
                    rows.at[2 * k + 1 - core], dm_near.at[n, k], dm_send.at[n, k],
                    dm_recv.at[n, k], partner,
                )
                move.start()
                small.append(move)
                load = pltpu.make_async_copy(rows.at[2 * k + core], dm_own.at[n, k], dm_load.at[n, k])
                load.start()
                small.append(load)
        load = pltpu.make_async_copy(mod, modv, dm_load.at[2, 0])
        load.start()
        small.append(load)

        def nth(p):
            near_end = jnp.minimum(place, chips - 1 - place)
            lead = chips - 1 - 2 * near_end
            rest = p - lead
            z = jnp.where(
                rest < 0, chips - 1 - p,
                jnp.where(lax.rem(rest, 2) == 0, 2 * near_end - lax.div(rest, 2), lax.div(rest, 2)),
            )
            return jnp.where(place > chips - 1 - place, chips - 1 - z, z)

        def in_turn(body):
            def turn_at(p, carry):
                z = nth(p)
                pl.when(z > place)(lambda: body(p, z, 1))
                pl.when(z < place)(lambda: body(p, z, -1))
                return carry

            lax.fori_loop(0, chips - 1, turn_at, 0)

        at_end = (place == 0) | (place == chips - 1)

        def line_sent(z):
            for k in range(kept):
                remote(
                    total(k).at[z], right(k).at[z], line_send.at[k, z], right_recv.at[k, z], partner
                ).wait_send()

        def near_add(k, z):
            nears(k, z).wait()
            pltpu.make_async_copy(total(k).at[z], total(k).at[z], load_sem.at[k, z]).wait()
            total(k)[z] = total(k)[z] + near(k)[z]

        def crossing(k, z):
            return remote(
                total(kept + k).at[z], cross(k).at[z], cross_send.at[k, z], cross_recv.at[k, z],
                device(other, place, core),
            )

        def cross_start(z):
            for k in give:
                near_add(kept + k, z)
                crossing(k, z).start()

        def cross_sent(z):
            for k in give:
                crossing(k, z).wait_send()

        cross_start(nth(0))
        for k in (0, 1):
            for z in range(chips):
                if k in parts:
                    near_add(k, z)

        for move in small:
            move.wait()
        for n in range(len(mates)):
            for k in range(2):
                dm_tot[n, k] = dm_own[n, k] + dm_near[n, k]
                dm_tot[n, k, 4:5, :] = modv[k, 4:5, :]

        def column_move(n, k, slot):
            return remote(
                dm_tot.at[n], gathered.at[n, slot], g_send.at[n, k], g_recv.at[n, slot],
                {"segment": role if n == 0 else other, "dp": lax.rem(dp + k, size)},
            )

        for n in range(len(mates)):
            for k in range(1 - n, size):
                column_move(n, k, dp).start()
        mine = pltpu.make_async_copy(dm_tot.at[0], gathered.at[0, dp], dm_load.at[2, 1])
        mine.start()

        def settle(k, z):
            if k in taken:
                crossing(k, z).wait_recv()
                total(k)[z] = total(k)[z] + cross(k)[z] if k in parts else cross(k)[z]

        def forward(p, z, by):
            line, recv = (right, right_recv) if by > 0 else (left, left_recv)
            first = place == (0 if by > 0 else chips - 1)
            target = device(role, place + by, core)
            cross_sent(z)
            cross_start(nth(p + 1))
            pl.when(at_end & (p > 0))(lambda: line_sent(nth(p - 1)))
            for k in range(kept):
                settle(k, z)
                here = remote(line(k).at[z], line(k).at[z], line_send.at[k, z], recv.at[k, z], target)
                start = remote(total(k).at[z], line(k).at[z], line_send.at[k, z], recv.at[k, z], target)
                pl.when(first)(start.start)

                @pl.when(jnp.logical_not(first))
                def _():
                    here.wait_recv()
                    line(k)[z] = line(k)[z] + total(k)[z]
                    here.start()

        in_turn(forward)
        cross_sent(place)
        for k in range(kept):
            settle(k, place)

        def result(k):
            return res_r if k else res_w

        for k in range(kept):
            result(k)[...] = total(k)[place].astype(f32)
            for line, recv, edge in ((right, right_recv, 0), (left, left_recv, chips - 1)):

                @pl.when(place != edge)
                def _():
                    remote(
                        line(k).at[place], line(k).at[place], line_send.at[k, 0],
                        recv.at[k, place], partner,
                    ).wait_recv()
                    result(k)[...] += line(k)[place].astype(f32)

        outs = [
            pltpu.make_async_copy(res_w, first_out, load_sem.at[0, 0]),
            pltpu.make_async_copy(res_r, rows_out, load_sem.at[1, 0]),
        ]
        for copy in outs:
            copy.start()
        pl.when(at_end)(lambda: line_sent(nth(chips - 2)))
        pl.when(jnp.logical_not(at_end))(lambda: in_turn(lambda p, z, by: line_sent(z)))
        mine.wait()
        for n in range(len(mates)):
            for k in range(1 - n, size):
                column_move(n, k, dp).wait_send()
                column_move(n, k, lax.rem(dp + k, size)).wait_recv()
        for copy in outs:
            copy.wait()
        if role == 0:
            each_part(lambda x: x.wait(), lambda x: x.wait_send())
        for k in range(2):
            remote(
                fin.at[0, pl.ds(0, BLK)], out_g.at[k], fin_send.at[0, 0], fin_recv.at[k], partner
            ).wait_recv() if role > 0 else pl.when(core != 0)(
                remote(
                    fin.at[0, pl.ds(0, BLK)], out_g.at[k], fin_send.at[0, 0], fin_recv.at[k], partner
                ).wait_recv
            )

    for role in range(4):
        pl.when(seg == role)(functools.partial(work, role))


def sums(att, up, down, dma, dmf, mod, fin, chips):
    wide, rows = att.shape[1:], down.shape[1:]

    def sems(*dims):
        return pltpu.SemaphoreType.DMA(dims)

    each = sems(4, chips)
    return pl.pallas_call(
        functools.partial(sums_kernel, chips),
        out_shape=[
            jax.ShapeDtypeStruct(wide, f32), jax.ShapeDtypeStruct(rows, f32),
            jax.ShapeDtypeStruct((2, 2 * chips, 2, 8, D), f32), OWNED,
        ],
        in_specs=[ANY] * 7,
        out_specs=[ANY] * 4,
        scratch_shapes=[
            vm((2, chips, *wide)), vm((2, chips, *rows)), vm((2, chips, *wide)), vm((2, chips, *rows)),
            vm((1, chips, *wide)), vm((1, chips, *rows)),
            vm((1, chips, *wide)), vm((1, chips, *rows)), vm((1, chips, *wide)), vm((1, chips, *rows)),
            vm(wide, f32), vm(rows, f32),
            vm((2, 2, 8, D), f32), vm((2, 2, 8, D), f32), vm((2, 2, 8, D), f32), vm((2, 8, D), f32),
            each, each, each, each, each, each, each, each, sems(3, 2),
            sems(2, 2), sems(2, 2), sems(2, 2 * chips), sems(2, 2 * chips), sems(MB, 2), sems(2),
        ],
        compiler_params=pltpu.CompilerParams(
            vmem_limit_bytes=VLIM, collective_id=1, has_side_effects=True
        ),
        name="gradient_sums",
    )(att, up, down, dma, dmf, mod, fin)


ATT_F, FF_F, FF_B, ATT_B = range(4)


def chain_kernel(
    xs, cs, w, rows2, cos, sin, mod,
    st, kv, lse, y, yf, act, dma, dmf, out_x, fin,
    wa, w1, w2, xv, nv, kvv, vv, inbox, qv, atv, bra, n1, brf, gbv, dov, dqv, xo, ov, fv, lv, cv, sv,
    dkt, dvt, rcvv, dpv, duv, actv, accv, dmv, zerov, moda, modf,
    w_send, w_recv, wf_send, wf_recv, x_send, x_recv, row_recv, fwd_send, fwd_recv, c_send, c_recv,
    push_sem, dkv_send, dkv_recv, mod_send, mod_recv, far_send, far_recv, fin_send, out_recv, ld, osem,
):
    role, dp = lax.axis_index("segment"), lax.axis_index("dp")
    c, place = lax.rem(dp, 2), lax.div(dp, 2)
    quarter, half_d = FF // 4, D // 2

    def device(segment, core):
        return {"segment": segment, "dp": 2 * place + core}

    def remote(src, dst, send, recv, target):
        return pltpu.make_async_remote_copy(
            src_ref=src, dst_ref=dst, send_sem=send, recv_sem=recv, device_id=target,
            device_id_type=MESH,
        )

    def local_copy(src, dst, sem):
        return pltpu.make_async_copy(src, dst, sem)

    partner = device(role, 1 - c)

    def rows_at(start, size):
        return pl.ds(pl.multiple_of(start, size), size)

    barrier = pltpu.get_barrier_semaphore()
    for k in range(1, 8):
        to = lax.rem(role * 2 + c + k, 8)
        pl.semaphore_signal(
            barrier, inc=1, device_id=device(lax.div(to, 2), lax.rem(to, 2)), device_id_type=MESH
        )
    pl.semaphore_wait(barrier, 7)

    tables = [local_copy(cos, cv, ld.at[0]), local_copy(sin, sv, ld.at[1])]
    for copy in tables:
        copy.start()

    def give_x(k, h):
        return remote(
            xs.at[k, pl.ds(h * HALF, HALF)], inbox.at[4 + 2 * k + h], x_send.at[k, h], x_recv.at[k, h],
            partner,
        )

    w_half = rows_at(c * half_d, half_d)
    rows_half = rows_at(c * quarter, quarter)
    high_half = rows_at(2 * quarter + c * quarter, quarter)

    def give_rows(dst, target):
        return remote(rows2.at[rows_half], w2.at[dst], w_send.at[1], w_recv.at[1], device(target, c))

    def give_w(dst, target):
        return remote(w.at[w_half], dst.at[w_half], w_send.at[0], w_recv.at[0], device(target, c))

    def keep_mod(k, dst):
        return local_copy(mod.at[k], dst.at[2 * k + c], ld.at[9 + k])

    def give_mod(k, dst):
        return remote(mod.at[k], dst.at[2 * k + c], mod_send.at[k], mod_recv.at[k], partner)

    def far_mod(k, dst, segment, core):
        return remote(
            mod.at[k], dst.at[2 * k + c], far_send.at[k, core], far_recv.at[k, c],
            device(segment, core),
        )

    def share_mod(dst):
        for k in range(2):
            keep_mod(k, dst).start()
            give_mod(k, dst).start()

    def shared_mod(dst):
        for k in range(2):
            keep_mod(k, dst).wait()
            give_mod(k, dst).wait()

    def give_c(k, j):
        return remote(
            cs.at[k, block_rows(1 - c + 2 * j)], inbox.at[4 + k, pl.ds(j * BLK, BLK)],
            c_send.at[k, j], c_recv.at[k, j], partner,
        )

    def keep_c(k, j):
        return local_copy(
            cs.at[k, block_rows(c + 2 * j)], inbox.at[4 + k, pl.ds(j * BLK, BLK)],
            ld.at[4 + 2 * k + j],
        )

    def forward_w(dst):
        return remote(dst.at[w_half], dst.at[w_half], wf_send.at[0], wf_recv.at[0], partner)

    def forward_rows(dst):
        return remote(w2.at[dst], w2.at[dst], wf_send.at[1], wf_recv.at[1], partner)

    def settle(given, passed):
        given.wait_recv()
        passed.start()
        passed.wait()

    @pl.when(role == 0)
    def _():
        share_mod(moda)
        for k in range(2):
            for h in range(2):
                give_x(k, h).start()
        give_rows(rows_half, 1).start()
        load = local_copy(w, wa, ld.at[2])
        load.start()
        shared_mod(moda)
        load.wait()

    @pl.when(role == 1)
    def _():
        share_mod(modf)
        loads = [
            local_copy(w, w1, ld.at[2]),
            local_copy(rows2, w2.at[pl.ds(2 * quarter, 2 * quarter)], ld.at[8]),
        ]
        for copy in loads:
            copy.start()
        settle(give_rows(rows_half, 1), forward_rows(rows_half))
        shared_mod(modf)
        for copy in loads:
            copy.wait()

    for who in (2, 3):

        @pl.when(role == who)
        def _():
            other = 5 - who
            mine, mod_mine = (wa, moda) if who == 2 else (w1, modf)
            there = rows_half if who == 2 else high_half
            share_mod(mod_mine)
            for k in range(2):
                for core in range(2):
                    far_mod(k, mod_mine, other, core).start()
            give_w(mine, other).start()
            give_rows(there, other).start()
            loads = [
                local_copy(w, mine, ld.at[2]),
                local_copy(
                    rows2, w2.at[pl.ds(0 if who == 2 else 2 * quarter, 2 * quarter)], ld.at[8]
                ),
            ]
            for copy in loads:
                copy.start()

            @pl.when(c == who - 2)
            def _():
                for k in range(2):
                    for j in range(2):
                        give_c(k, j).start()
                        keep_c(k, j).start()
                for k in range(2):
                    for j in range(2):
                        keep_c(k, j).wait()

            shared_mod(mod_mine)
            for copy in loads:
                copy.wait()

    def prepare(step):
        for who in (2, 3):
            other = 5 - who
            theirs, mod_theirs = (w1, modf) if who == 2 else (wa, moda)
            here = high_half if who == 2 else rows_half

            @pl.when((role == who) & (step == 3 - who))
            def _():
                settle(give_w(theirs, other), forward_w(theirs))
                for k in range(2):
                    for core in range(2):
                        remote(
                            mod.at[k], mod_theirs.at[2 * k + core], far_send.at[k, core],
                            far_recv.at[k, core], partner,
                        ).wait_recv()

            @pl.when((role == who) & (step == 1))
            def _():
                settle(give_rows(here, other), forward_rows(here))

    for copy in tables:
        copy.wait()

    def kind_of(step):
        first = step < 4
        return jnp.where(
            role == 0, jnp.where(first, ATT_F, ATT_B),
            jnp.where(role == 1, jnp.where(first, FF_F, FF_B), lax.rem(step, 4)),
        )

    def place_of(step):
        return jnp.where(role < 2, lax.rem(step, 4), lax.div(step, 4) * 2 + role - 2)

    def slot_rows(mb):
        n = jnp.where(role < 2, mb, lax.div(mb, 2))
        return lax.div(n, 2), pl.ds(pl.multiple_of(lax.rem(n, 2) * HALF, HALF), HALF)

    def x_slot(mb):
        return 2 * lax.div(mb, 2) + jnp.where(role == 0, 4, 0)

    def x_rows(mb, b):
        return inbox.at[x_slot(mb) + lax.div(b, 2), block_rows(lax.rem(b, 2))]

    def own_x(mb):
        return (role == 0) & (lax.rem(mb, 2) == c)

    def stores(kind, mb):
        half, spot = slot_rows(mb)
        if kind == ATT_F:
            kept = [
                (qv, st.at[QS, half, spot]), (kvv, kv.at[0, mb]), (vv, kv.at[1, mb]),
                (bra, st.at[BR, half, spot]), (lv, lse.at[mb]),
            ]
            return [(atv, st.at[AT, half, spot])], kept, role == 0
        if kind == FF_F:
            return [], [(brf, st.at[BF, half, spot])], role == 1
        if kind == FF_B:
            rows = [
                (n1, st.at[NF, half, spot]), (gbv, st.at[GB, half, spot]),
                (duv, yf.at[half, spot]), (actv, act.at[half, spot]), (dmv, dmf.at[mb]),
            ]
            return rows, [(zerov, dmf.at[mb + 1 - 2 * lax.rem(mb, 2)])], role >= 2
        rows = [
            (gbv, y.at[half, spot, pl.ds(3 * D, D)]), (dpv, y.at[half, spot, pl.ds(0, 3 * D)]),
            (n1, st.at[NM, half, spot]), (dmv, dma.at[mb]),
        ]
        return rows, [(zerov, dma.at[mb + 1 - 2 * lax.rem(mb, 2)])], role >= 2

    def copies(kind, mb):
        always, sometimes, when = stores(kind, mb)
        first = [local_copy(a, b, osem.at[k]) for k, (a, b) in enumerate(always)]
        rest = [local_copy(a, b, osem.at[len(always) + k]) for k, (a, b) in enumerate(sometimes)]
        return first, rest, when

    def store(kind, mb):
        first, rest, when = copies(kind, mb)
        for copy in first:
            copy.start()

        @pl.when(when)
        def _():
            for copy in rest:
                copy.start()

        if kind == ATT_B:
            pl.when(role == 0)(lambda: local_copy(ov, fin.at[mb], osem.at[5]).start())

    def wait_stored(step):
        kind_then, mb = kind_of(step), place_of(step)
        for kind in (ATT_F, FF_F, FF_B, ATT_B):

            @pl.when((step >= 0) & (kind_then == kind))
            def _():
                first, rest, when = copies(kind, mb)
                for copy in first:
                    copy.wait()

                @pl.when(when)
                def _():
                    for copy in rest:
                        copy.wait()

                if kind == ATT_B:
                    pl.when(role == 0)(lambda: local_copy(ov, fin.at[mb], osem.at[5]).wait())

    def wait_pushed(step):
        went = (
            ((role == 0) & (step < 4)) | (role == 1) | ((role >= 2) & (lax.rem(step, 4) == 3))
        ) & (step >= 0)

        @pl.when(went)
        def _():
            for j in range(2):
                at = pl.ds(j * BLK, BLK)
                remote(
                    ov.at[at], inbox.at[0, at], push_sem.at[j], row_recv.at[0, j], partner
                ).wait_send()

    def free(step):
        wait_pushed(step - 1)
        wait_stored(step - 1)

    def push(j, slot, rows, segment):
        remote(
            ov.at[block_rows(j)], inbox.at[slot, rows], push_sem.at[j], row_recv.at[slot, j],
            device(segment, c),
        ).start()

    def arrived(slot, j):
        at = block_rows(j)
        remote(
            ov.at[at], inbox.at[slot, at], push_sem.at[j], row_recv.at[slot, j], partner
        ).wait_recv()

    def spread(j, mb):
        segment, owner = c + 2 * j, lax.rem(mb, 2)
        here = (role == segment) & (c == owner)
        rows, k = block_rows(j), lax.div(mb, 2)

        @pl.when(here)
        def _():
            local_copy(fv.at[rows], out_x.at[k], fin_send.at[j]).start()

        @pl.when(jnp.logical_not(here))
        def _():
            remote(
                fv.at[rows], out_x.at[k], fin_send.at[j], out_recv.at[k], device(segment, owner)
            ).start()

    def wait_spread(mb):
        for j in range(2):
            here = (role == c + 2 * j) & (c == lax.rem(mb, 2))
            rows = pl.ds(j * BLK, BLK)

            @pl.when(here)
            def _():
                local_copy(fv.at[rows], out_x.at[0], fin_send.at[j]).wait()

            @pl.when(jnp.logical_not(here))
            def _():
                remote(
                    fv.at[rows], out_x.at[0], fin_send.at[j], out_recv.at[0], partner
                ).wait_send()

    def att_f(step, mb):
        length = moda[mb, 3:4, 0:1]
        off, scl, gat = moda[mb, 0:1, :], 1.0 + moda[mb, 1:2, :], moda[mb, 2:3, :]

        @pl.when(role == 0)
        def _():
            k = lax.div(mb, 2)
            load = local_copy(xs.at[k], xv, ld.at[0])
            pl.when(own_x(mb))(load.start)
            free(step)
            pl.when(own_x(mb))(load.wait)

            @pl.when(jnp.logical_not(own_x(mb)))
            def _():
                for h in range(2):
                    remote(
                        xs.at[0, pl.ds(0, HALF)], inbox.at[4 + 2 * k + h], x_send.at[0, 0],
                        x_recv.at[k, h], partner,
                    ).wait_recv()

        def forward(j):
            rows = x_rows(mb, c + 2 * j)
            k = 2 * lax.div(mb, 2) + j
            return remote(rows, rows, fwd_send.at[j], fwd_recv.at[k], partner)

        @pl.when(role != 0)
        def _():
            for j in range(2):
                rows = x_rows(mb, c + 2 * j)
                remote(
                    ov.at[pl.ds(j * BLK, BLK)], rows, push_sem.at[j],
                    row_recv.at[2 * lax.div(mb, 2) + j, c], partner,
                ).wait_recv()
                forward(j).start()
            free(step)

        def kv_block(b, carry):
            rows = block_rows(b)

            @pl.when(jnp.logical_not(own_x(mb)))
            def _():
                j, there = lax.div(b, 2), lax.rem(b, 2) != c

                @pl.when(there & (role != 0))
                def _():
                    at = x_rows(mb, b)
                    remote(
                        at, at, fwd_send.at[0], fwd_recv.at[2 * lax.div(mb, 2) + j], partner
                    ).wait_recv()

                xv[rows, :] = inbox[x_slot(mb) + j, block_rows(lax.rem(b, 2)), :]

            norm, _ = norm_parts(xv[rows, :].astype(f32))
            n = (norm * scl + off).astype(bf16)
            nv[rows, :] = n
            cosine, sine = cv[rows, :], sv[rows, :]
            kk = dot(n, wa[:, D : 2 * D])
            for p in range(6):
                ls = slice(p * 128, (p + 1) * 128)
                kvv[rows, ls] = turn(kk[:, ls], cosine, sine).astype(bf16)
            vv[rows, :] = dot(n, wa[:, 2 * D : 3 * D]).astype(bf16)
            return carry

        lax.fori_loop(0, 4, kv_block, 0)

        @pl.when(role != 0)
        def _():
            for j in range(2):
                forward(j).wait_send()

        def q_block(j, carry):
            nat = block_rows(c + 2 * j)
            rows = block_rows(j)
            cosine, sine = cv[nat, :] * 0.125, sv[nat, :] * 0.125
            qq = dot(nv[nat, :], wa[:, 0:D])
            for p in range(6):
                ls = slice(p * 128, (p + 1) * 128)
                qv[rows, ls] = turn(qq[:, ls], cosine, sine).astype(bf16)
            return carry

        lax.fori_loop(0, 2, q_block, 0)
        lane = lax.broadcasted_iota(i32, (BLK, 128), 1)
        position = lax.broadcasted_iota(i32, (1, SEQ_LEN), 1).astype(f32)
        bias = jnp.where(position < length, 0.0, -1e30).astype(f32)
        lv[...] = jnp.zeros((HALF, 128), f32)

        def block(j, carry):
            rows = block_rows(j)

            def pair(hp, carry):
                ls = lanes(hp)
                k2, v2, q2 = kvv[:, ls], vv[:, ls], qv[rows, ls]
                outs, stats = [], lv[rows, :]
                for a in range(2):
                    s = dot_nt(jnp.where((lane < 64) == (a == 0), q2, jnp.zeros_like(q2)), k2)
                    s = s + bias
                    m = jnp.max(s, axis=1, keepdims=True)
                    e = jnp.exp(s - m)
                    total = jnp.sum(e, axis=1, keepdims=True)
                    outs.append(dot(e.astype(bf16), v2) / total)
                    stats = jnp.where(lane == 2 * hp + a, m + jnp.log(total), stats)
                atv[rows, ls] = jnp.where(lane < 64, outs[0], outs[1]).astype(bf16)
                lv[rows, :] = stats
                return carry

            lax.fori_loop(0, HEADS // 2, pair, 0)
            branch = dot(atv[rows, :], wa[:, 3 * D : 4 * D])
            live = live_column(c, length, j)
            x = xv[block_rows(c + 2 * j), :].astype(f32)
            out = (x + jnp.where(live, gat * branch, 0.0)).astype(bf16)
            bra[rows, :] = branch.astype(bf16)

            @pl.when(role == 0)
            def _():
                ov[rows, :] = out
                push(j, mb, rows, 1)

            @pl.when(role != 0)
            def _():
                inbox[6, rows, :] = out

            return carry

        lax.fori_loop(0, 2, block, 0)
        store(ATT_F, mb)

    def ff_f(step, mb):
        length = modf[mb, 3:4, 0:1]
        off, scl, gat = modf[mb, 0:1, :], 1.0 + modf[mb, 1:2, :], modf[mb, 2:3, :]
        slot = jnp.where(role == 1, mb, 6)
        pl.when((role >= 2) & (step >= 4))(lambda: wait_spread(mb))
        pl.when(role == 1)(lambda: arrived(mb, 0))
        free(step)

        def block(j, carry):
            rows = block_rows(j)
            pl.when((role == 1) & (j > 0))(lambda: arrived(mb, j))
            norm, _ = norm_parts(inbox[slot, rows, :].astype(f32))
            n1[rows, :] = (norm * scl + off).astype(bf16)
            accv[rows, :] = jnp.zeros((BLK, D), f32)

            def part(p, carry):
                at = pl.ds(pl.multiple_of(p * D, D), D)
                u = dot(n1[rows, :], w1[:, at])
                t, _ = gelu_parts(u)
                accv[rows, :] += dot((0.5 * u * (1.0 + t)).astype(bf16), w2[at, :])
                return carry

            lax.fori_loop(0, 4, part, 0)
            acc = accv[rows, :]
            live = live_column(c, length, j)
            x = inbox[slot, rows, :].astype(f32)
            out = (x + jnp.where(live, gat * acc, 0.0)).astype(bf16)
            brf[rows, :] = acc.astype(bf16)

            @pl.when(role != 1)
            def _():
                fv[rows, :] = out
                spread(j, mb)

            @pl.when(role == 1)
            def _():
                ov[rows, :] = out
                slot_there = 2 * lax.div(mb, 2) + j
                remote(
                    ov.at[rows], inbox.at[slot_there, block_rows(c)], push_sem.at[j],
                    row_recv.at[slot_there, c], device(2 + lax.rem(mb, 2), c),
                ).start()

            return carry

        lax.fori_loop(0, 2, block, 0)
        store(FF_F, mb)

    def ff_b(step, mb):
        length = modf[mb, 3:4, 0:1]
        off, scl, gat = modf[mb, 0:1, :], 1.0 + modf[mb, 1:2, :], modf[mb, 2:3, :]
        slot = jnp.where(role == 1, mb, 6)
        from_slot = jnp.where(role == 1, 4 + mb, 4 + lax.div(mb, 2))

        def wait_rows(j):
            pl.when(role == 1)(lambda: arrived(4 + mb, j))

            @pl.when((role != 1) & (lax.rem(mb, 2) != c))
            def _():
                at = block_rows(j)
                remote(
                    ov.at[at], inbox.at[from_slot, at], push_sem.at[j],
                    c_recv.at[lax.div(mb, 2), j], partner,
                ).wait_recv()

        wait_rows(0)
        free(step)

        @pl.when(role == 1)
        def _():
            half, spot = slot_rows(mb)
            load = local_copy(st.at[BF, half, spot], brf, ld.at[1])
            load.start()
            load.wait()

        dmv[...] = jnp.zeros((8, D), f32)

        def block(j, carry):
            rows = block_rows(j)
            pl.when(j > 0)(lambda: wait_rows(j))
            norm, _ = norm_parts(inbox[slot, rows, :].astype(f32))
            n1[rows, :] = (norm * scl + off).astype(bf16)
            live = live_column(c, length, j)
            gl = jnp.where(live, inbox[from_slot, rows, :].astype(f32), 0.0)
            gbv[rows, :] = (gl * gat).astype(bf16)
            dmv[2:3, :] += jnp.sum(gl * brf[rows, :].astype(f32), axis=0, keepdims=True)
            accv[rows, :] = jnp.zeros((BLK, D), f32)

            def part(p, carry):
                cols = pl.ds(pl.multiple_of(p * D, D), D)
                u = dot(n1[rows, :], w1[:, cols])
                t, u2 = gelu_parts(u)
                half = 0.5 * (1.0 + t)
                actv[rows, cols] = (u * half).astype(bf16)
                slope = half + 0.5 * u * (1.0 - t * t) * (
                    0.7978845608028654 * (1.0 + 3 * 0.044715 * u2)
                )
                du = (dot_nt(gbv[rows, :], w2[cols, :]) * slope).astype(bf16)
                duv[rows, cols] = du
                accv[rows, :] += dot_nt(du, w1[:, cols])
                return carry

            lax.fori_loop(0, 4, part, 0)
            acc = accv[rows, :]
            n, rstd = norm_parts(inbox[slot, rows, :].astype(f32))
            dmv[0:1, :] += jnp.sum(acc, axis=0, keepdims=True)
            dmv[1:2, :] += jnp.sum(acc * n, axis=0, keepdims=True)
            out = (
                inbox[from_slot, rows, :].astype(f32) + norm_back(acc, n, rstd, scl)
            ).astype(bf16)

            @pl.when(role == 1)
            def _():
                ov[rows, :] = out
                push(j, mb, rows, 0)

            @pl.when(role != 1)
            def _():
                inbox[7, rows, :] = out

            return carry

        lax.fori_loop(0, 2, block, 0)
        store(FF_B, mb)

    def att_b(step, mb):
        length = moda[mb, 3:4, 0:1]
        off, scl, gat = moda[mb, 0:1, :], 1.0 + moda[mb, 1:2, :], moda[mb, 2:3, :]
        slot = jnp.where(role == 0, mb, 7)
        half, spot = slot_rows(mb)
        turn_of = jnp.where(role == 0, lax.rem(mb, 2), lax.div(mb, 2))
        loads = [
            local_copy(st.at[QS, half, spot], qv, ld.at[0]),
            local_copy(kv.at[0, mb], kvv, ld.at[1]),
            local_copy(kv.at[1, mb], vv, ld.at[2]),
            local_copy(st.at[AT, half, spot], atv, ld.at[3]),
            local_copy(lse.at[mb], lv, ld.at[4]),
            local_copy(st.at[BR, half, spot], bra, ld.at[5]),
        ]
        own_loads = [
            local_copy(
                xs.at[lax.div(mb, 2), block_rows(c + 2 * j)], xo.at[pl.ds(j * BLK, BLK)], ld.at[6 + j]
            )
            for j in range(2)
        ]
        free(step)

        @pl.when(role == 0)
        def _():
            for copy in loads:
                copy.start()

        @pl.when(own_x(mb))
        def _():
            for copy in own_loads:
                copy.start()

        dmv[...] = jnp.zeros((8, D), f32)

        def grad_block(j, carry):
            rows = block_rows(j)
            pl.when(role == 0)(lambda: arrived(mb, j))

            @pl.when(jnp.logical_not(own_x(mb)))
            def _():
                xo[rows, :] = inbox[x_slot(mb) + j, block_rows(c), :]

            live = live_column(c, length, j)
            gb = jnp.where(live, inbox[slot, rows, :].astype(f32) * gat, 0.0).astype(bf16)
            gbv[rows, :] = gb
            dov[rows, :] = dot_nt(gb, wa[:, 3 * D : 4 * D]).astype(bf16)
            return carry

        lax.fori_loop(0, 2, grad_block, 0)

        @pl.when(role == 0)
        def _():
            for copy in loads:
                copy.wait()

        @pl.when(own_x(mb))
        def _():
            for copy in own_loads:
                copy.wait()

        lane = lax.broadcasted_iota(i32, (HALF, 128), 1)
        position = lax.broadcasted_iota(i32, (1, SEQ_LEN), 1).astype(f32)
        bias = jnp.where(position < length, 0.0, -1e30).astype(f32)

        def pair(hp, carry):
            ls = lanes(hp)
            k2, v2 = kvv[:, ls], vv[:, ls]
            q2, do2 = qv[:, ls], dov[:, ls]
            q2t, do2t = q2.T, do2.T
            both = do2.astype(f32) * atv[:, ls].astype(f32)
            stats = lv[...]
            dqs = []
            for a in range(2):
                head = (lane < 64) == (a == 0)
                zero = jnp.zeros_like(q2)
                s = dot_nt(jnp.where(head, q2, zero), k2) + bias
                base = jnp.sum(jnp.where(lane == 2 * hp + a, stats, 0.0), axis=1, keepdims=True)
                p = jnp.exp(s - base)
                dp_ = dot_nt(jnp.where(head, do2, zero), v2)
                delta = jnp.sum(jnp.where(head, both, 0.0), axis=1, keepdims=True)
                ds = (p * (dp_ - delta)).astype(bf16)
                dqs.append(dot(ds, k2))
                at = pl.ds(pl.multiple_of(hp * 128 + a * 64, 64), 64)
                dkt[at, :] = dot(q2t[a * 64 : (a + 1) * 64, :], ds).astype(bf16)
                dvt[at, :] = dot(do2t[a * 64 : (a + 1) * 64, :], p.astype(bf16)).astype(bf16)
            dqv[:, ls] = jnp.where(lane < 64, dqs[0], dqs[1]).astype(bf16)
            for part, grad in enumerate((dkt, dvt)):
                for j in range(2):
                    give_pair(hp, part, j).start()
            return carry

        def give_pair(hp, part, j):
            grad = (dkt, dvt)[part]
            return remote(
                grad.at[lanes(hp), block_rows(1 - c + 2 * j)],
                rcvv.at[turn_of, part, lanes(hp), pl.ds(j * BLK, BLK)],
                dkv_send.at[hp, part, j], dkv_recv.at[turn_of, hp, part, j], partner,
            )

        lax.fori_loop(0, HEADS // 2, pair, 0)

        def settled(hp, carry):
            for part in range(2):
                for j in range(2):
                    give_pair(hp, part, j).wait()
            return carry

        def first(j, carry):
            rows, nat = block_rows(j), block_rows(c + 2 * j)
            cosine, sine = cv[nat, :], -sv[nat, :]
            for p in range(6):
                ls = slice(p * 128, (p + 1) * 128)
                dpv[rows, ls] = (turn(dqv[rows, ls].astype(f32), cosine, sine) * 0.125).astype(bf16)
            return carry

        lax.fori_loop(0, 2, first, 0)
        lax.fori_loop(0, HEADS // 2, settled, 0)

        def last(j, carry):
            rows, nat = block_rows(j), block_rows(c + 2 * j)
            cosine, sine = cv[nat, :], -sv[nat, :]
            for p in range(6):
                ls = slice(p * 128, (p + 1) * 128)
                for part, own in enumerate((dkt, dvt)):
                    total = own[ls, nat].astype(f32) + rcvv[turn_of, part, ls, rows].astype(f32)
                    grad = total.T
                    if part == 0:
                        grad = turn(grad.astype(bf16).astype(f32), cosine, sine)
                    dpv[rows, (part + 1) * D + p * 128 : (part + 1) * D + (p + 1) * 128] = (
                        grad.astype(bf16)
                    )
            acc = dot_nt(dpv[rows, :], wa[:, 0 : 3 * D])
            n, rstd = norm_parts(xo[rows, :].astype(f32))
            n1[rows, :] = (n * scl + off).astype(bf16)
            g = inbox[slot, rows, :].astype(f32)
            live = live_column(c, length, j)
            gl = jnp.where(live, g, 0.0)
            dmv[0:1, :] += jnp.sum(acc, axis=0, keepdims=True)
            dmv[1:2, :] += jnp.sum(acc * n, axis=0, keepdims=True)
            dmv[2:3, :] += jnp.sum(gl * bra[rows, :].astype(f32), axis=0, keepdims=True)
            ov[rows, :] = (g + norm_back(acc, n, rstd, scl)).astype(bf16)
            pl.when(role != 0)(lambda: push(j, 4 + mb, rows, 1))
            return carry

        lax.fori_loop(0, 2, last, 0)
        store(ATT_B, mb)

    def run(step, carry):
        kind, mb = kind_of(step), place_of(step)
        prepare(step)
        for which, work in ((ATT_F, att_f), (FF_F, ff_f), (FF_B, ff_b), (ATT_B, att_b)):
            pl.when(kind == which)(functools.partial(work, step, mb))
        return carry

    zerov[...] = jnp.zeros((8, D), f32)
    lax.fori_loop(0, 8, run, 0)
    free(8)
    pl.when(role >= 2)(lambda: wait_spread(role))

    @pl.when(role != c + 2)
    def _():
        for k in range(2):
            remote(
                fv.at[pl.ds(0, BLK)], out_x.at[k], fin_send.at[0], out_recv.at[k], partner
            ).wait_recv()

    @pl.when(role == 0)
    def _():
        for k in range(2):
            for h in range(2):
                give_x(k, h).wait_send()
        give_rows(rows_half, 1).wait_send()

    for who in (2, 3):

        @pl.when(role == who)
        def _():
            other = 5 - who
            mine, mod_mine = (wa, moda) if who == 2 else (w1, modf)
            there = rows_half if who == 2 else high_half
            for k in range(2):
                for core in range(2):
                    far_mod(k, mod_mine, other, core).wait_send()
            give_w(mine, other).wait_send()
            give_rows(there, other).wait_send()

            @pl.when(c == who - 2)
            def _():
                for k in range(2):
                    for j in range(2):
                        give_c(k, j).wait_send()


def chain(xs, cs, w, rows2, cos, sin, mod):
    def sems(*dims):
        return pltpu.SemaphoreType.DMA(dims)

    table = vm((SEQ_LEN, 128), f32)
    outs = [
        ST, KV, LSE, YS, YS, YS, DM, DM, OWNED, shape((MB, HALF, D)),
    ]
    return pl.pallas_call(
        chain_kernel,
        out_shape=outs,
        in_specs=[ANY] * 7,
        out_specs=[ANY] * len(outs),
        scratch_shapes=[
            vm((D, FF)), vm((D, FF)), vm((FF, D)), FV, FV, FV, FV, vm((8, HALF, D)),
            HV, HV, HV, HV, HV, HV, HV, HV, HV, HV, HV, vm((HALF, 128), f32), table, table,
            vm((D, SEQ_LEN)), vm((D, SEQ_LEN)), vm((2, 2, D, HALF)), vm((HALF, 3 * D)),
            vm((HALF, FF)), vm((HALF, FF)), vm((HALF, D), f32), vm((8, D), f32), vm((8, D), f32),
            vm((MB, 8, D), f32), vm((MB, 8, D), f32),
            sems(3), sems(3), sems(2), sems(2), sems(2, 2), sems(2, 2), sems(8, 2), sems(2), sems(4),
            sems(2, 2), sems(2, 2), sems(2), sems(HEADS // 2, 2, 2), sems(2, HEADS // 2, 2, 2),
            sems(2), sems(2), sems(2, 2), sems(2, 2), sems(2), sems(2), sems(12), sems(6),
        ],
        compiler_params=pltpu.CompilerParams(
            vmem_limit_bytes=62 << 20, collective_id=0, has_side_effects=True
        ),
        cost_estimate=cost(300),
        name="layers",
    )(xs, cs, w, rows2, cos, sin, mod)


def time_cond(steps):
    half_width = D // 2
    frequency = jnp.exp(
        jnp.arange(half_width, dtype=f32) * (-math.log(10000.0) / half_width)
    )
    angles = steps.astype(f32)[:, None] * frequency[None, :]
    return jax.nn.silu(jnp.concatenate([jnp.cos(angles), jnp.sin(angles)], axis=1))


def rope_tables():
    inverse = np.exp(np.arange(32, dtype=np.float32) * np.float32(-math.log(10000.0) / 32))
    angles = np.arange(SEQ_LEN, dtype=np.float32)[:, None] * inverse[None, :]
    cosine, sine = np.cos(angles), np.sin(angles)
    return (
        np.concatenate([cosine] * 4, axis=1).astype(np.float32),
        np.concatenate([-sine, sine, -sine, sine], axis=1).astype(np.float32),
    )


def local(block_input, cotangent, lengths, steps, mod_weight, mod_bias, first_weight, down_rows):
    ndp = lax.axis_size("dp")
    seg, dp = lax.axis_index("segment"), lax.axis_index("dp")
    chips = ndp // 2
    w, rows2 = first_weight[0], down_rows[0]
    conditions = time_cond(steps).astype(bf16)
    modulation = jnp.dot(conditions, mod_weight[0], preferred_element_type=f32)
    modulation = (modulation + mod_bias[0].astype(f32)).reshape(2, 3, D)
    length = jnp.broadcast_to(lengths.astype(f32)[:, None, None], (2, 1, D))
    mod = jnp.concatenate(
        [modulation, length, conditions.astype(f32)[:, None], jnp.zeros((2, 3, D), f32)], axis=1
    )
    cos, sin = (jnp.asarray(t) for t in rope_tables())
    st, _, _, y, yf, act, dma, dmf, out_x, fin = chain(
        block_input, cotangent, w, rows2, cos, sin, mod
    )
    depth, wide_rows = D // ndp, FF // 2 // ndp

    def weight_grad(kind, roles, right):
        pairs = pltpu.SemaphoreType.DMA((2,))
        return pl.pallas_call(
            functools.partial(weight_grad_kernel, kind, roles),
            in_specs=[ANY, ANY],
            out_specs=ANY,
            scratch_shapes=[
                vm((2, SEQ_LEN, D)), vm((2, 2, SEQ_LEN, D)), vm((D, D), f32), vm((2, D, D)),
                pairs, pairs, pairs,
            ],
            out_shape=shape((FF, D) if kind == "down" else (D, FF)),
            compiler_params=pltpu.CompilerParams(vmem_limit_bytes=VLIM),
            cost_estimate=cost(12),
            name=kind + "_gradient",
        )(st, right)

    down = weight_grad("down", (1, 2, 3), act).reshape(2 * ndp, wide_rows, D)
    up = weight_grad("up", (1, 2, 3), yf).reshape(ndp, depth, FF)
    att = weight_grad("attention", (0, 2, 3), y).reshape(ndp, depth, FF)
    first_sum, rows_sum, rows, out_g = sums(att, up, down, dma, dmf, mod, fin, chips)

    rows = jnp.where((jnp.arange(2) == 1)[:, None, None, None, None] & (seg < 2), 0.0, rows)
    columns = rows[:, :, :, :3].reshape(4 * ndp, 3 * D)
    kept = rows[:, :, :, 4].reshape(4 * ndp, D)
    mine = lax.dynamic_slice_in_dim(kept, dp * depth, depth, axis=1)
    mod_w_sum = jnp.dot(
        mine.T, columns, precision=lax.Precision.HIGHEST, preferred_element_type=f32
    )
    width = 3 * D // ndp
    mod_b_sum = jnp.sum(lax.dynamic_slice_in_dim(columns, dp * width, width, axis=1), axis=0)

    live = (seg * BLK + jnp.arange(BLK))[None, :, None] < lengths[:, None, None]

    def placed(given, part):
        return jnp.where(live, given, lax.dynamic_slice_in_dim(part, seg * BLK, BLK, axis=1))

    return (
        placed(out_x, block_input),
        placed(out_g, cotangent).astype(f32),
        mod_w_sum[None],
        mod_b_sum[None],
        first_sum[None],
        rows_sum[None],
    )


def solution(mesh):
    in_specs = (
        P("dp", None, None),
        P("dp", None, None),
        P("dp"),
        P("dp"),
        P("segment", None, None),
        P("segment", None),
        P("segment", None, None),
        P("segment", None, None),
    )
    out_specs = (
        P("dp", "segment", None),
        P("dp", "segment", None),
        P("segment", "dp", None),
        P("segment", "dp"),
        P("segment", "dp", None),
        P("segment", "dp", None),
    )
    return jax.shard_map(local, mesh=mesh, in_specs=in_specs, out_specs=out_specs, check_vma=False)
```

```python
import functools
import math

import jax
import jax.numpy as jnp
import numpy as np
from jax import lax
from jax.experimental import pallas as pl
from jax.experimental.pallas import tpu as pltpu
from jax.sharding import PartitionSpec as P

D = 768
HEADS = 12
HEAD_DIM = 64
FF = 3072
SEQ_LEN = 1024
BLK = 256
HALF = SEQ_LEN // 2
MB = 4
QS, AT, BR, NM, BF, NF, GB = range(7)
VLIM = 56 << 20
bf16, f32, i32 = jnp.bfloat16, jnp.float32, jnp.int32


def dot(a, b):
    return lax.dot_general(a, b, (((1,), (0,)), ((), ())), preferred_element_type=f32)


def dot_nt(a, b):
    return lax.dot_general(a, b, (((1,), (1,)), ((), ())), preferred_element_type=f32)


def dot_tn(a, b):
    return lax.dot_general(a, b, (((0,), (0,)), ((), ())), preferred_element_type=f32)


def block_rows(b):
    return pl.ds(pl.multiple_of(b * BLK, BLK), BLK)


def lanes(p):
    return pl.ds(pl.multiple_of(p * 128, 128), 128)


def norm_parts(x):
    center = x - jnp.mean(x, axis=-1, keepdims=True)
    rstd = lax.rsqrt(jnp.mean(center * center, axis=-1, keepdims=True) + 1e-06)
    return center * rstd, rstd


def norm_back(d_normed, n, rstd, scl):
    dn = d_normed * scl
    return (
        dn - jnp.mean(dn, axis=-1, keepdims=True) - n * jnp.mean(dn * n, axis=-1, keepdims=True)
    ) * rstd


def turn(v, cosine, sine):
    lane = lax.broadcasted_iota(i32, v.shape, 1)
    partner = jnp.where(lane % 64 < 32, pltpu.roll(v, 96, 1), pltpu.roll(v, 32, 1))
    return v * cosine + partner * sine


def live_column(c, length, j):
    r = lax.broadcasted_iota(i32, (BLK, 1), 0) + BLK * (c + 2 * j)
    return r.astype(f32) < length


def gelu_parts(u):
    u2 = u * u
    t = jnp.tanh(0.7978845608028654 * (u * (1.0 + 0.044715 * u2)))
    return t, u2


def gelu_slope(u, t, u2, half):
    return half + 0.5 * u * (1.0 - t * t) * (
        0.7978845608028654 * (1.0 + 3 * 0.044715 * u2)
    )


def weight_grad_kernel(kind, roles, st, y, out, xv, yv, acc, ov, xsem, ysem, osem):
    role = lax.axis_index("segment")
    parts = jnp.where(role < 2, 2, 1)

    def tile(j, h):
        return y.at[h, :, pl.ds(pl.multiple_of(j * D, D), D)]

    def into(j):
        at = pl.ds(pl.multiple_of(j * D, D), D)
        return out.at[at] if kind == "down" else out.at[:, at]

    def load_x(which, h, into):
        return pltpu.make_async_copy(st.at[which, h], xv.at[into, h], xsem.at[into, h])

    def load_y(j, h):
        slot = lax.rem(j, 2)
        return pltpu.make_async_copy(tile(j, h), yv.at[slot, h], ysem.at[slot, h])

    def store(j):
        slot = lax.rem(j, 2)
        return pltpu.make_async_copy(ov.at[slot], into(j), osem.at[slot])

    chosen = functools.reduce(jnp.logical_or, [role == r for r in roles])

    @pl.when(chosen)
    def _():
        which = GB if kind == "down" else NM if kind == "attention" else NF

        def halves(act):
            act(0)
            pl.when(parts == 2)(lambda: act(1))

        halves(lambda h: load_x(which, h, 0).start())
        halves(lambda h: load_y(0, h).start())
        if kind == "attention":
            halves(lambda h: load_x(AT, h, 1).start())
        halves(lambda h: load_x(which, h, 0).wait())

        def step(j, carry):
            slot = lax.rem(j, 2)
            pl.when(j < 3)(lambda: halves(lambda h: load_y(j + 1, h).start()))
            halves(lambda h: load_y(j, h).wait())
            source = 0
            if kind == "attention":
                pl.when(j == 3)(lambda: halves(lambda h: load_x(AT, h, 1).wait()))
                source = lax.div(j, 3)

            def product(h):
                if kind == "down":
                    return dot_tn(yv[slot, h], xv[source, h])
                return dot_tn(xv[source, h], yv[slot, h])

            pl.when(j >= 2)(lambda: store(j - 2).wait())

            @pl.when(parts == 1)
            def _():
                ov[slot] = product(0).astype(bf16)

            @pl.when(parts == 2)
            def _():
                acc[...] = product(0)
                ov[slot] = (acc[...] + product(1)).astype(bf16)

            store(j).start()
            return carry

        lax.fori_loop(0, 4, step, 0)
        store(2).wait()
        store(3).wait()


ANY = pl.BlockSpec(memory_space=pl.ANY)
VMEM = pl.BlockSpec(memory_space=pltpu.VMEM)


def shape(dims, dtype=bf16):
    return jax.ShapeDtypeStruct(dims, dtype)


ST = shape((7, 2, SEQ_LEN, D))
KV = shape((2, MB, SEQ_LEN, D))
LSE = shape((MB, HALF, 128), f32)
YS = shape((2, SEQ_LEN, FF))
DM = shape((MB, 8, D), f32)
OWNED = shape((2, BLK, D))


def vm(dims, dtype=bf16):
    return pltpu.VMEM(dims, dtype)


HV, FV = vm((HALF, D)), vm((SEQ_LEN, D))


def cost(micros):
    return pl.CostEstimate(flops=int(micros * 1e9), bytes_accessed=1 << 20, transcendentals=0)


MESH = pl.DeviceIdType.MESH


def sums_kernel(
    chips, att, up, down, dma, dmf, mod, fin, first_out, rows_out, gathered, out_g,
    near_w, near_r, tot_w, tot_r, cross_w, cross_r, right_w, right_r, left_w, left_r, res_w, res_r,
    dm_own, dm_near, dm_tot, modv,
    load_sem, near_send, near_recv, cross_send, cross_recv, line_send, right_recv, left_recv,
    dm_load, dm_send, dm_recv, g_send, g_recv, fin_send, fin_recv,
):
    seg, dp = lax.axis_index("segment"), lax.axis_index("dp")
    core, place = lax.rem(dp, 2), lax.div(dp, 2)
    size = 2 * chips

    def device(segment, chip, at):
        return {"segment": segment, "dp": 2 * chip + at}

    def remote(src, dst, send, recv, target):
        return pltpu.make_async_remote_copy(
            src_ref=src, dst_ref=dst, send_sem=send, recv_sem=recv,
            device_id=target, device_id_type=MESH,
        )

    def work(role):
        other = 5 - role if role >= 2 else 1 - role
        second = role >= 2
        low, high = 0, size
        parts = {
            0: {0: (att, 0)},
            1: {0: (up, 0), 1: (down, high), 3: (down, low)},
            2: {0: (att, 0), 1: (down, low), 2: (up, 0), 3: (down, high)},
            3: {0: (up, 0), 1: (down, high), 2: (att, 0), 3: (down, low)},
        }[role]
        kept = 2
        give = [k for k in (0, 1) if k + 2 in parts]
        taken = {0: [1], 1: [], 2: [0, 1], 3: [0, 1]}[role]

        def pick(wide, rows, k):
            return (rows if k % 2 else wide).at[k // 2]

        def near(k):
            return pick(near_w, near_r, k)

        def total(k):
            return pick(tot_w, tot_r, k)

        def right(k):
            return pick(right_w, right_r, k)

        def left(k):
            return pick(left_w, left_r, k)

        def cross(k):
            return pick(cross_w, cross_r, k)

        barrier = pltpu.get_barrier_semaphore()

        def greet(target):
            pl.semaphore_signal(barrier, inc=1, device_id=target, device_id_type=MESH)

        for k in range(1, size):
            greet({"segment": role, "dp": lax.rem(dp + k, size)})
        waits = size - 1
        if role < 2:
            greet(device(1 - role, place, core))
            waits += 1
        else:
            for k in range(size):
                greet({"segment": other, "dp": lax.rem(dp + k, size)})
            waits += size
        if role > 0:
            greet(device(0, place, role % 2))
        else:
            waits += 2 + 2 * core
        pl.semaphore_wait(barrier, waits)

        def each_part(act_local, act_remote):
            for j in range(2):
                segment = core + 2 * j
                for mb in range(MB):
                    src, dst = fin.at[mb, pl.ds(j * BLK, BLK)], out_g.at[mb // 2]
                    here = (segment == 0) & (core == mb % 2)
                    local = pltpu.make_async_copy(src, dst, fin_send.at[mb, j])
                    there = remote(
                        src, dst, fin_send.at[mb, j], fin_recv.at[mb // 2],
                        device(segment, place, mb % 2),
                    )
                    pl.when(here)(functools.partial(act_local, local))
                    pl.when(jnp.logical_not(here))(functools.partial(act_remote, there))

        if role == 0:
            each_part(lambda x: x.start(), lambda x: x.start())

        partner = device(role, place, 1 - core)
        mates = [dma, dmf] if role % 2 == 0 else [dmf, dma]
        mates = mates[: 2 if second else 1]
        def nears(k, z):
            array, base = parts[k]
            return remote(
                array.at[base + 2 * z + 1 - core], near(k).at[z], near_send.at[k, z],
                near_recv.at[k, z], partner,
            )

        for k in sorted(parts, reverse=True):
            array, base = parts[k]
            for z in range(chips):
                nears(k, z).start()
                pltpu.make_async_copy(
                    array.at[base + 2 * z + core], total(k).at[z], load_sem.at[k, z]
                ).start()
        small = []
        for n, rows in enumerate(mates):
            for k in range(2):
                move = remote(
                    rows.at[2 * k + 1 - core], dm_near.at[n, k], dm_send.at[n, k],
                    dm_recv.at[n, k], partner,
                )
                move.start()
                small.append(move)
                load = pltpu.make_async_copy(rows.at[2 * k + core], dm_own.at[n, k], dm_load.at[n, k])
                load.start()
                small.append(load)
        load = pltpu.make_async_copy(mod, modv, dm_load.at[2, 0])
        load.start()
        small.append(load)

        def nth(p):
            near_end = jnp.minimum(place, chips - 1 - place)
            lead = chips - 1 - 2 * near_end
            rest = p - lead
            z = jnp.where(
                rest < 0, chips - 1 - p,
                jnp.where(lax.rem(rest, 2) == 0, 2 * near_end - lax.div(rest, 2), lax.div(rest, 2)),
            )
            return jnp.where(place > chips - 1 - place, chips - 1 - z, z)

        def in_turn(body):
            def turn_at(p, carry):
                z = nth(p)
                pl.when(z > place)(lambda: body(p, z, 1))
                pl.when(z < place)(lambda: body(p, z, -1))
                return carry

            lax.fori_loop(0, chips - 1, turn_at, 0)

        at_end = (place == 0) | (place == chips - 1)

        def line_sent(z):
            for k in range(kept):
                remote(
                    total(k).at[z], right(k).at[z], line_send.at[k, z], right_recv.at[k, z], partner
                ).wait_send()

        def near_add(k, z):
            nears(k, z).wait()
            pltpu.make_async_copy(total(k).at[z], total(k).at[z], load_sem.at[k, z]).wait()
            total(k)[z] = total(k)[z] + near(k)[z]

        def crossing(k, z):
            return remote(
                total(kept + k).at[z], cross(k).at[z], cross_send.at[k, z], cross_recv.at[k, z],
                device(other, place, core),
            )

        def cross_start(z):
            for k in give:
                near_add(kept + k, z)
                crossing(k, z).start()

        def cross_sent(z):
            for k in give:
                crossing(k, z).wait_send()

        cross_start(nth(0))
        for k in (0, 1):
            for z in range(chips):
                if k in parts:
                    near_add(k, z)

        for move in small:
            move.wait()
        for n in range(len(mates)):
            for k in range(2):
                dm_tot[n, k] = dm_own[n, k] + dm_near[n, k]
                dm_tot[n, k, 4:5, :] = modv[k, 4:5, :]

        def column_move(n, k, slot):
            return remote(
                dm_tot.at[n], gathered.at[n, slot], g_send.at[n, k], g_recv.at[n, slot],
                {"segment": role if n == 0 else other, "dp": lax.rem(dp + k, size)},
            )

        for n in range(len(mates)):
            for k in range(1 - n, size):
                column_move(n, k, dp).start()
        mine = pltpu.make_async_copy(dm_tot.at[0], gathered.at[0, dp], dm_load.at[2, 1])
        mine.start()

        def settle(k, z):
            if k in taken:
                crossing(k, z).wait_recv()
                total(k)[z] = total(k)[z] + cross(k)[z] if k in parts else cross(k)[z]

        def forward(p, z, by):
            line, recv = (right, right_recv) if by > 0 else (left, left_recv)
            first = place == (0 if by > 0 else chips - 1)
            target = device(role, place + by, core)
            cross_sent(z)
            cross_start(nth(p + 1))
            pl.when(at_end & (p > 0))(lambda: line_sent(nth(p - 1)))
            for k in range(kept):
                settle(k, z)
                here = remote(line(k).at[z], line(k).at[z], line_send.at[k, z], recv.at[k, z], target)
                start = remote(total(k).at[z], line(k).at[z], line_send.at[k, z], recv.at[k, z], target)
                pl.when(first)(start.start)

                @pl.when(jnp.logical_not(first))
                def _():
                    here.wait_recv()
                    line(k)[z] = line(k)[z] + total(k)[z]
                    here.start()

        in_turn(forward)
        cross_sent(place)
        for k in range(kept):
            settle(k, place)

        def result(k):
            return res_r if k else res_w

        for k in range(kept):
            result(k)[...] = total(k)[place].astype(f32)
            for line, recv, edge in ((right, right_recv, 0), (left, left_recv, chips - 1)):

                @pl.when(place != edge)
                def _():
                    remote(
                        line(k).at[place], line(k).at[place], line_send.at[k, 0],
                        recv.at[k, place], partner,
                    ).wait_recv()
                    result(k)[...] += line(k)[place].astype(f32)

        outs = [
            pltpu.make_async_copy(res_w, first_out, load_sem.at[0, 0]),
            pltpu.make_async_copy(res_r, rows_out, load_sem.at[1, 0]),
        ]
        for copy in outs:
            copy.start()
        pl.when(at_end)(lambda: line_sent(nth(chips - 2)))
        pl.when(jnp.logical_not(at_end))(lambda: in_turn(lambda p, z, by: line_sent(z)))
        mine.wait()
        for n in range(len(mates)):
            for k in range(1 - n, size):
                column_move(n, k, dp).wait_send()
                column_move(n, k, lax.rem(dp + k, size)).wait_recv()
        for copy in outs:
            copy.wait()
        if role == 0:
            each_part(lambda x: x.wait(), lambda x: x.wait_send())
        for k in range(2):
            remote(
                fin.at[0, pl.ds(0, BLK)], out_g.at[k], fin_send.at[0, 0], fin_recv.at[k], partner
            ).wait_recv() if role > 0 else pl.when(core != 0)(
                remote(
                    fin.at[0, pl.ds(0, BLK)], out_g.at[k], fin_send.at[0, 0], fin_recv.at[k], partner
                ).wait_recv
            )

    for role in range(4):
        pl.when(seg == role)(functools.partial(work, role))


def sums(att, up, down, dma, dmf, mod, fin, chips):
    wide, rows = att.shape[1:], down.shape[1:]

    def sems(*dims):
        return pltpu.SemaphoreType.DMA(dims)

    each = sems(4, chips)
    return pl.pallas_call(
        functools.partial(sums_kernel, chips),
        out_shape=[
            jax.ShapeDtypeStruct(wide, f32), jax.ShapeDtypeStruct(rows, f32),
            jax.ShapeDtypeStruct((2, 2 * chips, 2, 8, D), f32), OWNED,
        ],
        in_specs=[ANY] * 7,
        out_specs=[ANY] * 4,
        scratch_shapes=[
            vm((2, chips, *wide)), vm((2, chips, *rows)), vm((2, chips, *wide)), vm((2, chips, *rows)),
            vm((1, chips, *wide)), vm((1, chips, *rows)),
            vm((1, chips, *wide)), vm((1, chips, *rows)), vm((1, chips, *wide)), vm((1, chips, *rows)),
            vm(wide, f32), vm(rows, f32),
            vm((2, 2, 8, D), f32), vm((2, 2, 8, D), f32), vm((2, 2, 8, D), f32), vm((2, 8, D), f32),
            each, each, each, each, each, each, each, each, sems(3, 2),
            sems(2, 2), sems(2, 2), sems(2, 2 * chips), sems(2, 2 * chips), sems(MB, 2), sems(2),
        ],
        compiler_params=pltpu.CompilerParams(
            vmem_limit_bytes=VLIM, collective_id=1, has_side_effects=True
        ),
        name="gradient_sums",
    )(att, up, down, dma, dmf, mod, fin)


ATT_F, FF_F, FF_B, ATT_B = range(4)


def chain_kernel(
    xs, cs, w, rows2, cos, sin, mod,
    st, kv, lse, y, yf, act, dma, dmf, out_x, fin,
    wa, w1, w2, xv, nv, kvv, vv, inbox, qv, atv, bra, n1, brf, gbv, dov, dqv, xo, ov, fv, n2, gb2, lv, cv, sv,
    dkt, dvt, rcvv, dpv, duv, actv, accv, dmv, zerov, moda, modf,
    w_send, w_recv, wf_send, wf_recv, x_send, x_recv, row_recv, fwd_send, fwd_recv, c_send, c_recv,
    push_sem, dkv_send, dkv_recv, mod_send, mod_recv, far_send, far_recv, fin_send, out_recv, ld, osem,
):
    role, dp = lax.axis_index("segment"), lax.axis_index("dp")
    c, place = lax.rem(dp, 2), lax.div(dp, 2)
    quarter, half_d = FF // 4, D // 2

    def device(segment, core):
        return {"segment": segment, "dp": 2 * place + core}

    def remote(src, dst, send, recv, target):
        return pltpu.make_async_remote_copy(
            src_ref=src, dst_ref=dst, send_sem=send, recv_sem=recv, device_id=target,
            device_id_type=MESH,
        )

    def local_copy(src, dst, sem):
        return pltpu.make_async_copy(src, dst, sem)

    partner = device(role, 1 - c)

    def rows_at(start, size):
        return pl.ds(pl.multiple_of(start, size), size)

    barrier = pltpu.get_barrier_semaphore()
    for k in range(1, 8):
        to = lax.rem(role * 2 + c + k, 8)
        pl.semaphore_signal(
            barrier, inc=1, device_id=device(lax.div(to, 2), lax.rem(to, 2)), device_id_type=MESH
        )
    pl.semaphore_wait(barrier, 7)

    tables = [local_copy(cos, cv, ld.at[0]), local_copy(sin, sv, ld.at[1])]
    for copy in tables:
        copy.start()

    def give_x(k, h):
        return remote(
            xs.at[k, pl.ds(h * HALF, HALF)], inbox.at[4 + 2 * k + h], x_send.at[k, h], x_recv.at[k, h],
            partner,
        )

    w_half = rows_at(c * half_d, half_d)
    rows_half = rows_at(c * quarter, quarter)
    high_half = rows_at(2 * quarter + c * quarter, quarter)

    def give_rows(dst, target):
        return remote(rows2.at[rows_half], w2.at[dst], w_send.at[1], w_recv.at[1], device(target, c))

    def give_w(dst, target):
        return remote(w.at[w_half], dst.at[w_half], w_send.at[0], w_recv.at[0], device(target, c))

    def keep_mod(k, dst):
        return local_copy(mod.at[k], dst.at[2 * k + c], ld.at[9 + k])

    def give_mod(k, dst):
        return remote(mod.at[k], dst.at[2 * k + c], mod_send.at[k], mod_recv.at[k], partner)

    def far_mod(k, dst, segment, core):
        return remote(
            mod.at[k], dst.at[2 * k + c], far_send.at[k, core], far_recv.at[k, c],
            device(segment, core),
        )

    def share_mod(dst):
        for k in range(2):
            keep_mod(k, dst).start()
            give_mod(k, dst).start()

    def shared_mod(dst):
        for k in range(2):
            keep_mod(k, dst).wait()
            give_mod(k, dst).wait()

    def give_c(k, j):
        return remote(
            cs.at[k, block_rows(1 - c + 2 * j)], inbox.at[4 + k, pl.ds(j * BLK, BLK)],
            c_send.at[k, j], c_recv.at[k, j], partner,
        )

    def keep_c(k, j):
        return local_copy(
            cs.at[k, block_rows(c + 2 * j)], inbox.at[4 + k, pl.ds(j * BLK, BLK)],
            ld.at[4 + 2 * k + j],
        )

    def forward_w(dst):
        return remote(dst.at[w_half], dst.at[w_half], wf_send.at[0], wf_recv.at[0], partner)

    def forward_rows(dst):
        return remote(w2.at[dst], w2.at[dst], wf_send.at[1], wf_recv.at[1], partner)

    def settle(given, passed):
        given.wait_recv()
        passed.start()
        passed.wait()

    @pl.when(role == 0)
    def _():
        share_mod(moda)
        for k in range(2):
            for h in range(2):
                give_x(k, h).start()
        give_rows(rows_half, 1).start()
        load = local_copy(w, wa, ld.at[2])
        load.start()
        shared_mod(moda)
        load.wait()

    @pl.when(role == 1)
    def _():
        share_mod(modf)
        loads = [
            local_copy(w, w1, ld.at[2]),
            local_copy(rows2, w2.at[pl.ds(2 * quarter, 2 * quarter)], ld.at[8]),
        ]
        for copy in loads:
            copy.start()
        settle(give_rows(rows_half, 1), forward_rows(rows_half))
        shared_mod(modf)
        for copy in loads:
            copy.wait()

    for who in (2, 3):

        @pl.when(role == who)
        def _():
            other = 5 - who
            mine, mod_mine = (wa, moda) if who == 2 else (w1, modf)
            there = rows_half if who == 2 else high_half
            share_mod(mod_mine)
            for k in range(2):
                for core in range(2):
                    far_mod(k, mod_mine, other, core).start()
            give_w(mine, other).start()
            give_rows(there, other).start()
            loads = [
                local_copy(w, mine, ld.at[2]),
                local_copy(
                    rows2, w2.at[pl.ds(0 if who == 2 else 2 * quarter, 2 * quarter)], ld.at[8]
                ),
            ]
            for copy in loads:
                copy.start()

            @pl.when(c == who - 2)
            def _():
                for k in range(2):
                    for j in range(2):
                        give_c(k, j).start()
                        keep_c(k, j).start()
                for k in range(2):
                    for j in range(2):
                        keep_c(k, j).wait()

            shared_mod(mod_mine)
            for copy in loads:
                copy.wait()

    def prepare(step):
        for who in (2, 3):
            other = 5 - who
            theirs, mod_theirs = (w1, modf) if who == 2 else (wa, moda)
            here = high_half if who == 2 else rows_half

            @pl.when((role == who) & (step == 3 - who))
            def _():
                settle(give_w(theirs, other), forward_w(theirs))
                for k in range(2):
                    for core in range(2):
                        remote(
                            mod.at[k], mod_theirs.at[2 * k + core], far_send.at[k, core],
                            far_recv.at[k, core], partner,
                        ).wait_recv()

            @pl.when((role == who) & (step == 1))
            def _():
                settle(give_rows(here, other), forward_rows(here))

    for copy in tables:
        copy.wait()

    def kind_of(step):
        first = step < 4
        return jnp.where(
            role == 0, jnp.where(first, ATT_F, ATT_B),
            jnp.where(role == 1, jnp.where(first, FF_F, FF_B), lax.rem(step, 4)),
        )

    def place_of(step):
        return jnp.where(role < 2, lax.rem(step, 4), lax.div(step, 4) * 2 + role - 2)

    def slot_rows(mb):
        n = jnp.where(role < 2, mb, lax.div(mb, 2))
        return lax.div(n, 2), pl.ds(pl.multiple_of(lax.rem(n, 2) * HALF, HALF), HALF)

    def x_slot(mb):
        return 2 * lax.div(mb, 2) + jnp.where(role == 0, 4, 0)

    def x_rows(mb, b):
        return inbox.at[x_slot(mb) + lax.div(b, 2), block_rows(lax.rem(b, 2))]

    def own_x(mb):
        return (role == 0) & (lax.rem(mb, 2) == c)

    def stores(kind, mb):
        half, spot = slot_rows(mb)
        if kind == ATT_F:
            kept = [
                (qv, st.at[QS, half, spot]), (kvv, kv.at[0, mb]), (vv, kv.at[1, mb]),
                (bra, st.at[BR, half, spot]), (lv, lse.at[mb]),
            ]
            return [(atv, st.at[AT, half, spot])], kept, role == 0
        if kind == FF_F:
            return [], [(brf, st.at[BF, half, spot])], role == 1
        if kind == FF_B:
            rows = [
                (n1, st.at[NF, half, spot]), (gbv, st.at[GB, half, spot]),
                (duv, yf.at[half, spot]), (actv, act.at[half, spot]), (dmv, dmf.at[mb]),
            ]
            return rows, [(zerov, dmf.at[mb + 1 - 2 * lax.rem(mb, 2)])], role >= 2
        rows = [
            (gb2, y.at[half, spot, pl.ds(3 * D, D)]), (dpv, y.at[half, spot, pl.ds(0, 3 * D)]),
            (n2, st.at[NM, half, spot]), (dmv, dma.at[mb]),
        ]
        return rows, [(zerov, dma.at[mb + 1 - 2 * lax.rem(mb, 2)])], role >= 2

    def copies(kind, mb):
        always, sometimes, when = stores(kind, mb)
        first = [local_copy(a, b, osem.at[k]) for k, (a, b) in enumerate(always)]
        rest = [local_copy(a, b, osem.at[len(always) + k]) for k, (a, b) in enumerate(sometimes)]
        return first, rest, when

    def store(kind, mb):
        first, rest, when = copies(kind, mb)
        for copy in first:
            copy.start()

        @pl.when(when)
        def _():
            for copy in rest:
                copy.start()

        if kind == ATT_B:
            pl.when(role == 0)(lambda: local_copy(ov, fin.at[mb], osem.at[5]).start())

    def wait_stored(step):
        kind_then, mb = kind_of(step), place_of(step)
        for kind in (ATT_F, FF_F, FF_B, ATT_B):

            @pl.when((step >= 0) & (kind_then == kind))
            def _():
                first, rest, when = copies(kind, mb)
                for copy in first:
                    copy.wait()

                @pl.when(when)
                def _():
                    for copy in rest:
                        copy.wait()

                if kind == ATT_B:
                    pl.when(role == 0)(lambda: local_copy(ov, fin.at[mb], osem.at[5]).wait())

    def wait_pushed(step):
        went = (
            ((role == 0) & (step < 4)) | (role == 1) | ((role >= 2) & (lax.rem(step, 4) == 3))
        ) & (step >= 0)

        @pl.when(went)
        def _():
            for j in range(2):
                at = pl.ds(j * BLK, BLK)
                remote(
                    ov.at[at], inbox.at[0, at], push_sem.at[j], row_recv.at[0, j], partner
                ).wait_send()

    def free(step):
        wait_pushed(step - 1)
        wait_stored(step - 1)

    def push(j, slot, rows, segment):
        remote(
            ov.at[block_rows(j)], inbox.at[slot, rows], push_sem.at[j], row_recv.at[slot, j],
            device(segment, c),
        ).start()

    def arrived(slot, j):
        at = block_rows(j)
        remote(
            ov.at[at], inbox.at[slot, at], push_sem.at[j], row_recv.at[slot, j], partner
        ).wait_recv()

    def spread(j, mb):
        segment, owner = c + 2 * j, lax.rem(mb, 2)
        here = (role == segment) & (c == owner)
        rows, k = block_rows(j), lax.div(mb, 2)

        @pl.when(here)
        def _():
            local_copy(fv.at[rows], out_x.at[k], fin_send.at[j]).start()

        @pl.when(jnp.logical_not(here))
        def _():
            remote(
                fv.at[rows], out_x.at[k], fin_send.at[j], out_recv.at[k], device(segment, owner)
            ).start()

    def wait_spread(mb):
        for j in range(2):
            here = (role == c + 2 * j) & (c == lax.rem(mb, 2))
            rows = pl.ds(j * BLK, BLK)

            @pl.when(here)
            def _():
                local_copy(fv.at[rows], out_x.at[0], fin_send.at[j]).wait()

            @pl.when(jnp.logical_not(here))
            def _():
                remote(
                    fv.at[rows], out_x.at[0], fin_send.at[j], out_recv.at[0], partner
                ).wait_send()

    def att_f(step, mb):
        length = moda[mb, 3:4, 0:1]
        off, scl, gat = moda[mb, 0:1, :], 1.0 + moda[mb, 1:2, :], moda[mb, 2:3, :]

        @pl.when(role == 0)
        def _():
            k = lax.div(mb, 2)
            load = local_copy(xs.at[k], xv, ld.at[0])
            pl.when(own_x(mb))(load.start)
            free(step)
            pl.when(own_x(mb))(load.wait)

            @pl.when(jnp.logical_not(own_x(mb)))
            def _():
                for h in range(2):
                    remote(
                        xs.at[0, pl.ds(0, HALF)], inbox.at[4 + 2 * k + h], x_send.at[0, 0],
                        x_recv.at[k, h], partner,
                    ).wait_recv()

        def forward(j):
            rows = x_rows(mb, c + 2 * j)
            k = 2 * lax.div(mb, 2) + j
            return remote(rows, rows, fwd_send.at[j], fwd_recv.at[k], partner)

        @pl.when(role != 0)
        def _():
            for j in range(2):
                rows = x_rows(mb, c + 2 * j)
                remote(
                    ov.at[pl.ds(j * BLK, BLK)], rows, push_sem.at[j],
                    row_recv.at[2 * lax.div(mb, 2) + j, c], partner,
                ).wait_recv()
                forward(j).start()
            free(step)

        def kv_block(b, carry):
            rows = block_rows(b)

            @pl.when(jnp.logical_not(own_x(mb)))
            def _():
                j, there = lax.div(b, 2), lax.rem(b, 2) != c

                @pl.when(there & (role != 0))
                def _():
                    at = x_rows(mb, b)
                    remote(
                        at, at, fwd_send.at[0], fwd_recv.at[2 * lax.div(mb, 2) + j], partner
                    ).wait_recv()

                xv[rows, :] = inbox[x_slot(mb) + j, block_rows(lax.rem(b, 2)), :]

            norm, _ = norm_parts(xv[rows, :].astype(f32))
            n = (norm * scl + off).astype(bf16)
            nv[rows, :] = n
            cosine, sine = cv[rows, :], sv[rows, :]
            kk = dot(n, wa[:, D : 2 * D])
            for p in range(6):
                ls = slice(p * 128, (p + 1) * 128)
                kvv[rows, ls] = turn(kk[:, ls], cosine, sine).astype(bf16)
            vv[rows, :] = dot(n, wa[:, 2 * D : 3 * D]).astype(bf16)
            return carry

        lax.fori_loop(0, 4, kv_block, 0)

        @pl.when(role != 0)
        def _():
            for j in range(2):
                forward(j).wait_send()

        def q_block(j, carry):
            nat = block_rows(c + 2 * j)
            rows = block_rows(j)
            cosine, sine = cv[nat, :] * 0.125, sv[nat, :] * 0.125
            qq = dot(nv[nat, :], wa[:, 0:D])
            for p in range(6):
                ls = slice(p * 128, (p + 1) * 128)
                qv[rows, ls] = turn(qq[:, ls], cosine, sine).astype(bf16)
            return carry

        lax.fori_loop(0, 2, q_block, 0)
        lane = lax.broadcasted_iota(i32, (BLK, 128), 1)
        position = lax.broadcasted_iota(i32, (1, SEQ_LEN), 1).astype(f32)
        bias = jnp.where(position < length, 0.0, -1e30).astype(f32)
        lv[...] = jnp.zeros((HALF, 128), f32)

        def block(j, carry):
            rows = block_rows(j)

            def pair(hp, carry):
                ls = lanes(hp)
                k2, v2, q2 = kvv[:, ls], vv[:, ls], qv[rows, ls]
                outs, stats = [], lv[rows, :]
                for a in range(2):
                    s = dot_nt(jnp.where((lane < 64) == (a == 0), q2, jnp.zeros_like(q2)), k2)
                    s = s + bias
                    m = jnp.max(s, axis=1, keepdims=True)
                    e = jnp.exp(s - m)
                    total = jnp.sum(e, axis=1, keepdims=True)
                    outs.append(dot(e.astype(bf16), v2) / total)
                    stats = jnp.where(lane == 2 * hp + a, m + jnp.log(total), stats)
                atv[rows, ls] = jnp.where(lane < 64, outs[0], outs[1]).astype(bf16)
                lv[rows, :] = stats
                return carry

            lax.fori_loop(0, HEADS // 2, pair, 0)
            branch = dot(atv[rows, :], wa[:, 3 * D : 4 * D])
            live = live_column(c, length, j)
            x = xv[block_rows(c + 2 * j), :].astype(f32)
            out = (x + jnp.where(live, gat * branch, 0.0)).astype(bf16)
            bra[rows, :] = branch.astype(bf16)

            @pl.when(role == 0)
            def _():
                ov[rows, :] = out
                push(j, mb, rows, 1)

            @pl.when(role != 0)
            def _():
                inbox[6, rows, :] = out

            return carry

        lax.fori_loop(0, 2, block, 0)
        store(ATT_F, mb)

    def ff_f(step, mb):
        length = modf[mb, 3:4, 0:1]
        off, scl, gat = modf[mb, 0:1, :], 1.0 + modf[mb, 1:2, :], modf[mb, 2:3, :]
        slot = jnp.where(role == 1, mb, 6)
        pl.when((role >= 2) & (step >= 4))(lambda: wait_spread(mb))
        pl.when(role == 1)(lambda: arrived(mb, 0))
        free(step)

        def block(j, carry):
            rows = block_rows(j)
            pl.when((role == 1) & (j > 0))(lambda: arrived(mb, j))
            norm, _ = norm_parts(inbox[slot, rows, :].astype(f32))
            n1[rows, :] = (norm * scl + off).astype(bf16)
            accv[rows, :] = jnp.zeros((BLK, D), f32)

            def part(p, carry):
                at = pl.ds(pl.multiple_of(p * D, D), D)
                u = dot(n1[rows, :], w1[:, at])
                t, u2 = gelu_parts(u)
                half = 0.5 * (1.0 + t)
                actv[rows, at] = (u * half).astype(bf16)

                @pl.when(role != 1)
                def _():
                    duv[rows, at] = gelu_slope(u, t, u2, half).astype(bf16)

                accv[rows, :] += dot(actv[rows, at], w2[at, :])
                return carry

            lax.fori_loop(0, 4, part, 0)
            acc = accv[rows, :]
            live = live_column(c, length, j)
            x = inbox[slot, rows, :].astype(f32)
            out = (x + jnp.where(live, gat * acc, 0.0)).astype(bf16)
            brf[rows, :] = acc.astype(bf16)

            @pl.when(role != 1)
            def _():
                fv[rows, :] = out
                spread(j, mb)

            @pl.when(role == 1)
            def _():
                ov[rows, :] = out
                slot_there = 2 * lax.div(mb, 2) + j
                remote(
                    ov.at[rows], inbox.at[slot_there, block_rows(c)], push_sem.at[j],
                    row_recv.at[slot_there, c], device(2 + lax.rem(mb, 2), c),
                ).start()

            return carry

        lax.fori_loop(0, 2, block, 0)
        store(FF_F, mb)

    def ff_b(step, mb):
        length = modf[mb, 3:4, 0:1]
        off, scl, gat = modf[mb, 0:1, :], 1.0 + modf[mb, 1:2, :], modf[mb, 2:3, :]
        slot = jnp.where(role == 1, mb, 6)
        from_slot = jnp.where(role == 1, 4 + mb, 4 + lax.div(mb, 2))

        def wait_rows(j):
            pl.when(role == 1)(lambda: arrived(4 + mb, j))

            @pl.when((role != 1) & (lax.rem(mb, 2) != c))
            def _():
                at = block_rows(j)
                remote(
                    ov.at[at], inbox.at[from_slot, at], push_sem.at[j],
                    c_recv.at[lax.div(mb, 2), j], partner,
                ).wait_recv()

        wait_rows(0)
        free(step)

        @pl.when(role == 1)
        def _():
            half, spot = slot_rows(mb)
            load = local_copy(st.at[BF, half, spot], brf, ld.at[1])
            load.start()
            load.wait()

        dmv[...] = jnp.zeros((8, D), f32)

        def block(j, carry):
            rows = block_rows(j)
            pl.when(j > 0)(lambda: wait_rows(j))
            norm, _ = norm_parts(inbox[slot, rows, :].astype(f32))
            n1[rows, :] = (norm * scl + off).astype(bf16)
            live = live_column(c, length, j)
            gl = jnp.where(live, inbox[from_slot, rows, :].astype(f32), 0.0)
            gbv[rows, :] = (gl * gat).astype(bf16)
            dmv[2:3, :] += jnp.sum(gl * brf[rows, :].astype(f32), axis=0, keepdims=True)
            accv[rows, :] = jnp.zeros((BLK, D), f32)

            def part(p, carry):
                cols = pl.ds(pl.multiple_of(p * D, D), D)
                @pl.when(role == 1)
                def _():
                    u = dot(n1[rows, :], w1[:, cols])
                    t, u2 = gelu_parts(u)
                    half = 0.5 * (1.0 + t)
                    actv[rows, cols] = (u * half).astype(bf16)
                    duv[rows, cols] = gelu_slope(u, t, u2, half).astype(bf16)

                slope = duv[rows, cols].astype(f32)
                du = (dot_nt(gbv[rows, :], w2[cols, :]) * slope).astype(bf16)
                duv[rows, cols] = du
                accv[rows, :] += dot_nt(du, w1[:, cols])
                return carry

            lax.fori_loop(0, 4, part, 0)
            acc = accv[rows, :]
            n, rstd = norm_parts(inbox[slot, rows, :].astype(f32))
            dmv[0:1, :] += jnp.sum(acc, axis=0, keepdims=True)
            dmv[1:2, :] += jnp.sum(acc * n, axis=0, keepdims=True)
            out = (
                inbox[from_slot, rows, :].astype(f32) + norm_back(acc, n, rstd, scl)
            ).astype(bf16)

            @pl.when(role == 1)
            def _():
                ov[rows, :] = out
                push(j, mb, rows, 0)

            @pl.when(role != 1)
            def _():
                inbox[7, rows, :] = out

            return carry

        lax.fori_loop(0, 2, block, 0)
        store(FF_B, mb)

    def att_b(step, mb):
        length = moda[mb, 3:4, 0:1]
        off, scl, gat = moda[mb, 0:1, :], 1.0 + moda[mb, 1:2, :], moda[mb, 2:3, :]
        slot = jnp.where(role == 0, mb, 7)
        half, spot = slot_rows(mb)
        turn_of = jnp.where(role == 0, lax.rem(mb, 2), lax.div(mb, 2))
        loads = [
            local_copy(st.at[QS, half, spot], qv, ld.at[0]),
            local_copy(kv.at[0, mb], kvv, ld.at[1]),
            local_copy(kv.at[1, mb], vv, ld.at[2]),
            local_copy(st.at[AT, half, spot], atv, ld.at[3]),
            local_copy(lse.at[mb], lv, ld.at[4]),
            local_copy(st.at[BR, half, spot], bra, ld.at[5]),
        ]
        own_loads = [
            local_copy(
                xs.at[lax.div(mb, 2), block_rows(c + 2 * j)], xo.at[pl.ds(j * BLK, BLK)], ld.at[6 + j]
            )
            for j in range(2)
        ]
        pl.when(role == 0)(lambda: free(step))

        @pl.when(role == 0)
        def _():
            for copy in loads:
                copy.start()

        @pl.when(own_x(mb))
        def _():
            for copy in own_loads:
                copy.start()


        def grad_block(j, carry):
            rows = block_rows(j)
            pl.when(role == 0)(lambda: arrived(mb, j))

            @pl.when(jnp.logical_not(own_x(mb)))
            def _():
                xo[rows, :] = inbox[x_slot(mb) + j, block_rows(c), :]

            live = live_column(c, length, j)
            gb = jnp.where(live, inbox[slot, rows, :].astype(f32) * gat, 0.0).astype(bf16)
            gb2[rows, :] = gb
            dov[rows, :] = dot_nt(gb, wa[:, 3 * D : 4 * D]).astype(bf16)
            return carry

        lax.fori_loop(0, 2, grad_block, 0)

        @pl.when(role == 0)
        def _():
            for copy in loads:
                copy.wait()

        @pl.when(own_x(mb))
        def _():
            for copy in own_loads:
                copy.wait()

        lane = lax.broadcasted_iota(i32, (HALF, 128), 1)
        position = lax.broadcasted_iota(i32, (1, SEQ_LEN), 1).astype(f32)
        bias = jnp.where(position < length, 0.0, -1e30).astype(f32)

        def pair(hp, carry):
            ls = lanes(hp)
            k2, v2 = kvv[:, ls], vv[:, ls]
            q2, do2 = qv[:, ls], dov[:, ls]
            q2t, do2t = q2.T, do2.T
            both = do2.astype(f32) * atv[:, ls].astype(f32)
            stats = lv[...]
            dqs = []
            for a in range(2):
                head = (lane < 64) == (a == 0)
                zero = jnp.zeros_like(q2)
                s = dot_nt(jnp.where(head, q2, zero), k2) + bias
                base = jnp.sum(jnp.where(lane == 2 * hp + a, stats, 0.0), axis=1, keepdims=True)
                p = jnp.exp(s - base)
                dp_ = dot_nt(jnp.where(head, do2, zero), v2)
                delta = jnp.sum(jnp.where(head, both, 0.0), axis=1, keepdims=True)
                ds = (p * (dp_ - delta)).astype(bf16)
                dqs.append(dot(ds, k2))
                at = pl.ds(pl.multiple_of(hp * 128 + a * 64, 64), 64)
                dkt[at, :] = dot(q2t[a * 64 : (a + 1) * 64, :], ds).astype(bf16)
                dvt[at, :] = dot(do2t[a * 64 : (a + 1) * 64, :], p.astype(bf16)).astype(bf16)
            dqv[:, ls] = jnp.where(lane < 64, dqs[0], dqs[1]).astype(bf16)
            for part, grad in enumerate((dkt, dvt)):
                for j in range(2):
                    give_pair(hp, part, j).start()
            return carry

        def give_pair(hp, part, j):
            grad = (dkt, dvt)[part]
            return remote(
                grad.at[lanes(hp), block_rows(1 - c + 2 * j)],
                rcvv.at[turn_of, part, lanes(hp), pl.ds(j * BLK, BLK)],
                dkv_send.at[hp, part, j], dkv_recv.at[turn_of, hp, part, j], partner,
            )

        lax.fori_loop(0, HEADS // 2, pair, 0)
        pl.when(role != 0)(lambda: free(step))
        dmv[...] = jnp.zeros((8, D), f32)

        def settled(hp, carry):
            for part in range(2):
                for j in range(2):
                    give_pair(hp, part, j).wait()
            return carry

        def first(j, carry):
            rows, nat = block_rows(j), block_rows(c + 2 * j)
            cosine, sine = cv[nat, :], -sv[nat, :]
            for p in range(6):
                ls = slice(p * 128, (p + 1) * 128)
                dpv[rows, ls] = (turn(dqv[rows, ls].astype(f32), cosine, sine) * 0.125).astype(bf16)
            return carry

        lax.fori_loop(0, 2, first, 0)
        lax.fori_loop(0, HEADS // 2, settled, 0)

        def last(j, carry):
            rows, nat = block_rows(j), block_rows(c + 2 * j)
            cosine, sine = cv[nat, :], -sv[nat, :]
            for p in range(6):
                ls = slice(p * 128, (p + 1) * 128)
                for part, own in enumerate((dkt, dvt)):
                    total = own[ls, nat].astype(f32) + rcvv[turn_of, part, ls, rows].astype(f32)
                    grad = total.T
                    if part == 0:
                        grad = turn(grad.astype(bf16).astype(f32), cosine, sine)
                    dpv[rows, (part + 1) * D + p * 128 : (part + 1) * D + (p + 1) * 128] = (
                        grad.astype(bf16)
                    )
            acc = dot_nt(dpv[rows, :], wa[:, 0 : 3 * D])
            n, rstd = norm_parts(xo[rows, :].astype(f32))
            n2[rows, :] = (n * scl + off).astype(bf16)
            g = inbox[slot, rows, :].astype(f32)
            live = live_column(c, length, j)
            gl = jnp.where(live, g, 0.0)
            dmv[0:1, :] += jnp.sum(acc, axis=0, keepdims=True)
            dmv[1:2, :] += jnp.sum(acc * n, axis=0, keepdims=True)
            dmv[2:3, :] += jnp.sum(gl * bra[rows, :].astype(f32), axis=0, keepdims=True)
            ov[rows, :] = (g + norm_back(acc, n, rstd, scl)).astype(bf16)
            pl.when(role != 0)(lambda: push(j, 4 + mb, rows, 1))
            return carry

        lax.fori_loop(0, 2, last, 0)
        store(ATT_B, mb)

    def run(step, carry):
        kind, mb = kind_of(step), place_of(step)
        prepare(step)
        for which, work in ((ATT_F, att_f), (FF_F, ff_f), (FF_B, ff_b), (ATT_B, att_b)):
            pl.when(kind == which)(functools.partial(work, step, mb))
        return carry

    zerov[...] = jnp.zeros((8, D), f32)
    lax.fori_loop(0, 8, run, 0)
    free(8)
    pl.when(role >= 2)(lambda: wait_spread(role))

    @pl.when(role != c + 2)
    def _():
        for k in range(2):
            remote(
                fv.at[pl.ds(0, BLK)], out_x.at[k], fin_send.at[0], out_recv.at[k], partner
            ).wait_recv()

    @pl.when(role == 0)
    def _():
        for k in range(2):
            for h in range(2):
                give_x(k, h).wait_send()
        give_rows(rows_half, 1).wait_send()

    for who in (2, 3):

        @pl.when(role == who)
        def _():
            other = 5 - who
            mine, mod_mine = (wa, moda) if who == 2 else (w1, modf)
            there = rows_half if who == 2 else high_half
            for k in range(2):
                for core in range(2):
                    far_mod(k, mod_mine, other, core).wait_send()
            give_w(mine, other).wait_send()
            give_rows(there, other).wait_send()

            @pl.when(c == who - 2)
            def _():
                for k in range(2):
                    for j in range(2):
                        give_c(k, j).wait_send()


def chain(xs, cs, w, rows2, cos, sin, mod):
    def sems(*dims):
        return pltpu.SemaphoreType.DMA(dims)

    table = vm((SEQ_LEN, 128), f32)
    outs = [
        ST, KV, LSE, YS, YS, YS, DM, DM, OWNED, shape((MB, HALF, D)),
    ]
    return pl.pallas_call(
        chain_kernel,
        out_shape=outs,
        in_specs=[ANY] * 7,
        out_specs=[ANY] * len(outs),
        scratch_shapes=[
            vm((D, FF)), vm((D, FF)), vm((FF, D)), FV, FV, FV, FV, vm((8, HALF, D)),
            HV, HV, HV, HV, HV, HV, HV, HV, HV, HV, HV, HV, HV, vm((HALF, 128), f32), table, table,
            vm((D, SEQ_LEN)), vm((D, SEQ_LEN)), vm((2, 2, D, HALF)), vm((HALF, 3 * D)),
            vm((HALF, FF)), vm((HALF, FF)), vm((HALF, D), f32), vm((8, D), f32), vm((8, D), f32),
            vm((MB, 8, D), f32), vm((MB, 8, D), f32),
            sems(3), sems(3), sems(2), sems(2), sems(2, 2), sems(2, 2), sems(8, 2), sems(2), sems(4),
            sems(2, 2), sems(2, 2), sems(2), sems(HEADS // 2, 2, 2), sems(2, HEADS // 2, 2, 2),
            sems(2), sems(2), sems(2, 2), sems(2, 2), sems(2), sems(2), sems(12), sems(6),
        ],
        compiler_params=pltpu.CompilerParams(
            vmem_limit_bytes=62 << 20, collective_id=0, has_side_effects=True
        ),
        cost_estimate=cost(300),
        name="layers",
    )(xs, cs, w, rows2, cos, sin, mod)


def time_cond(steps):
    half_width = D // 2
    frequency = jnp.exp(
        jnp.arange(half_width, dtype=f32) * (-math.log(10000.0) / half_width)
    )
    angles = steps.astype(f32)[:, None] * frequency[None, :]
    return jax.nn.silu(jnp.concatenate([jnp.cos(angles), jnp.sin(angles)], axis=1))


def rope_tables():
    inverse = np.exp(np.arange(32, dtype=np.float32) * np.float32(-math.log(10000.0) / 32))
    angles = np.arange(SEQ_LEN, dtype=np.float32)[:, None] * inverse[None, :]
    cosine, sine = np.cos(angles), np.sin(angles)
    return (
        np.concatenate([cosine] * 4, axis=1).astype(np.float32),
        np.concatenate([-sine, sine, -sine, sine], axis=1).astype(np.float32),
    )


def local(block_input, cotangent, lengths, steps, mod_weight, mod_bias, first_weight, down_rows):
    ndp = lax.axis_size("dp")
    seg, dp = lax.axis_index("segment"), lax.axis_index("dp")
    chips = ndp // 2
    w, rows2 = first_weight[0], down_rows[0]
    conditions = time_cond(steps).astype(bf16)
    modulation = jnp.dot(conditions, mod_weight[0], preferred_element_type=f32)
    modulation = (modulation + mod_bias[0].astype(f32)).reshape(2, 3, D)
    length = jnp.broadcast_to(lengths.astype(f32)[:, None, None], (2, 1, D))
    mod = jnp.concatenate(
        [modulation, length, conditions.astype(f32)[:, None], jnp.zeros((2, 3, D), f32)], axis=1
    )
    cos, sin = (jnp.asarray(t) for t in rope_tables())
    st, _, _, y, yf, act, dma, dmf, out_x, fin = chain(
        block_input, cotangent, w, rows2, cos, sin, mod
    )
    depth, wide_rows = D // ndp, FF // 2 // ndp

    def weight_grad(kind, roles, right):
        pairs = pltpu.SemaphoreType.DMA((2,))
        return pl.pallas_call(
            functools.partial(weight_grad_kernel, kind, roles),
            in_specs=[ANY, ANY],
            out_specs=ANY,
            scratch_shapes=[
                vm((2, 2, SEQ_LEN, D)), vm((2, 2, SEQ_LEN, D)), vm((D, D), f32), vm((2, D, D)),
                pltpu.SemaphoreType.DMA((2, 2)), pltpu.SemaphoreType.DMA((2, 2)), pairs,
            ],
            out_shape=shape((FF, D) if kind == "down" else (D, FF)),
            compiler_params=pltpu.CompilerParams(vmem_limit_bytes=VLIM),
            cost_estimate=cost(12),
            name=kind + "_gradient",
        )(st, right)

    down = weight_grad("down", (1, 2, 3), act).reshape(2 * ndp, wide_rows, D)
    up = weight_grad("up", (1, 2, 3), yf).reshape(ndp, depth, FF)
    att = weight_grad("attention", (0, 2, 3), y).reshape(ndp, depth, FF)
    first_sum, rows_sum, rows, out_g = sums(att, up, down, dma, dmf, mod, fin, chips)

    rows = jnp.where((jnp.arange(2) == 1)[:, None, None, None, None] & (seg < 2), 0.0, rows)
    columns = rows[:, :, :, :3].reshape(4 * ndp, 3 * D)
    kept = rows[:, :, :, 4].reshape(4 * ndp, D)
    mine = lax.dynamic_slice_in_dim(kept, dp * depth, depth, axis=1)
    mod_w_sum = jnp.dot(
        mine.T, columns, precision=lax.Precision.HIGHEST, preferred_element_type=f32
    )
    width = 3 * D // ndp
    mod_b_sum = jnp.sum(lax.dynamic_slice_in_dim(columns, dp * width, width, axis=1), axis=0)

    live = (seg * BLK + jnp.arange(BLK))[None, :, None] < lengths[:, None, None]

    def placed(given, part):
        return jnp.where(live, given, lax.dynamic_slice_in_dim(part, seg * BLK, BLK, axis=1))

    return (
        placed(out_x, block_input),
        placed(out_g, cotangent).astype(f32),
        mod_w_sum[None],
        mod_b_sum[None],
        first_sum[None],
        rows_sum[None],
    )


def solution(mesh):
    in_specs = (
        P("dp", None, None),
        P("dp", None, None),
        P("dp"),
        P("dp"),
        P("segment", None, None),
        P("segment", None),
        P("segment", None, None),
        P("segment", None, None),
    )
    out_specs = (
        P("dp", "segment", None),
        P("dp", "segment", None),
        P("segment", "dp", None),
        P("segment", "dp"),
        P("segment", "dp", None),
        P("segment", "dp", None),
    )
    return jax.shard_map(local, mesh=mesh, in_specs=in_specs, out_specs=out_specs, check_vma=False)
```
